32 devices in a mesh: grp: 8 (over y, x, core), seq: 4 (over z).
Axes of the slice: x: 2, y: 2, z: 4, core: 2. Of those that a mesh axis runs over, the one named last changes fastest.
Arguments:
- lengths: int32 [16], replicated, may hold values from 42 to 1024, as said below
- group_of: int32 [16], replicated, may hold values from 0 to 7, as said below
- query_pre: bfloat16 [8192, 8192], P(('grp', 'seq')), may hold values from -170 to 170
- key_pre: bfloat16 [8192, 1024], P(('grp', 'seq')), may hold values from -7 to 7
- value_pre: bfloat16 [8192, 1024], P(('grp', 'seq')), may hold values from -4 to 4
- query_new: bfloat16 [16, 8192], P(None, 'seq'), may hold values from -170 to 170
- key_new: bfloat16 [16, 1024], P(None, 'seq'), may hold values from -4 to 4
- value_new: bfloat16 [16, 1024], P(None, 'seq'), may hold values from -4 to 4
- hidden_new: bfloat16 [16, 8192], P(None, 'grp'), may hold values from -3 to 3
- out_weight: bfloat16 [8192, 8192], P('seq', 'grp'), may hold values from -0.0625 to 0.0625
- norm_gain: bfloat16 [8192], P('grp'), may hold values from 0.099609375 to 1.8984375
- gate_weight: bfloat16 [8192, 16384], P('grp', 'seq'), may hold values from -0.0625 to 0.0625
- up_weight: bfloat16 [8192, 16384], P('grp', 'seq'), may hold values from -0.0625 to 0.0625
- down_weight: bfloat16 [16384, 8192], P('seq', 'grp'), may hold values from -0.046875 to 0.046875
Outputs:
- prefill_attention: bfloat16 [8192, 8192], P(('grp', 'seq'))
- decode_hidden: bfloat16 [16, 8192], P(None, ('grp', 'seq'))
The draws below stay inside these ranges and needn't reach their ends.
Inputs may be any that keep to these rules, and one draw needn't show every extreme that they name: Two requests have length exactly 1024 and are alone in their groups; the others have lengths from 42 to 341; the lengths in one group sum to at most 1024. `group_of`: every group holds at least one request and at most three.
All inputs are finite; a program needn't handle non-finite values.
Results may differ from the reference program's by a relative error of at most 0.0095.
Values may be sent and summed in bfloat16 or wider, within the bound.
No kernel may reach another device: no remote copies, remote signals or barrier semaphores. Data moves between devices by JAX's collectives and lax.ppermute only.
A program may use at most 320 MiB of HBM per device.

```python
import math
import jax
import jax.numpy as jnp
from jax import lax

D = 8192
H = 64
KVH = 8
HD = 128
FF_WIN = 16384
GROUPS = 8
G_TOK = 1024
TOKENS = 8192
REQS = 16
SHORT_MAX = 341


def request_plan(key):
    key_groups = jax.random.fold_in(key, 101)
    key_order = jax.random.fold_in(key, 102)
    key_length = jax.random.fold_in(key, 103)
    groups = jax.random.permutation(key_groups, GROUPS).astype(jnp.int32)
    order = jax.random.permutation(key_order, REQS).astype(jnp.int32)
    ranks = jnp.zeros((REQS,), jnp.int32).at[order].set(jnp.arange(REQS, dtype=jnp.int32))
    short_rank = jnp.maximum(ranks - 2, 0)
    long_group = groups[jnp.minimum(ranks, 1)]
    short_group = groups[2 + jnp.mod(short_rank, GROUPS - 2)]
    group_of = jnp.where(ranks < 2, long_group, short_group).astype(jnp.int32)
    short_len = jax.random.randint(key_length, (REQS,), SHORT_MAX // 8, SHORT_MAX + 1).astype(jnp.int32)
    lengths = jnp.where(ranks < 2, G_TOK, short_len).astype(jnp.int32)
    return (lengths, group_of)


def draw_lengths(key, part):
    return request_plan(key)[0]


def draw_group_of(key, part):
    return request_plan(key)[1]


def attention_rows(key):
    key_query = jax.random.fold_in(key, 201)
    key_key = jax.random.fold_in(key, 202)
    keys = jax.random.truncated_normal(key_key, -6.0, 6.0, (TOKENS, KVH * HD), jnp.float32)
    queries = jax.random.truncated_normal(key_query, -6.0, 6.0, (TOKENS, H * HD), jnp.float32)
    return (queries, keys)


def draw_query_pre(key, part):
    return attention_rows(key)[0].astype(jnp.bfloat16)


def draw_key_pre(key, part):
    return attention_rows(key)[1].astype(jnp.bfloat16)


def draw_query_new(key, part):
    key_query = jax.random.fold_in(key, 301)
    queries = jax.random.truncated_normal(key_query, -6.0, 6.0, (REQS, H * HD), jnp.float32)
    return queries.astype(jnp.bfloat16)


def levels(key, shape, split, least, high):
    level = 1.0
    for dim, shards_of in split:
        heights = jax.random.uniform(jax.random.fold_in(jax.random.fold_in(key, 6), dim), (shards_of,), jnp.float32, least / len(split), high / len(split))
        level = level * jnp.repeat(jnp.exp(heights), shape[dim] // shards_of).reshape((-1,) + (1,) * (len(shape) - 1 - dim))
    return level


def bell_draw(key, dims, width, most, cuts=(), kind=jnp.bfloat16):
    level = levels(key, dims, cuts, -0.22, 0.18) if cuts else 1.0
    values = jax.random.normal(key, dims, jnp.float32) * width * level
    return jnp.minimum(jnp.maximum(values, -most), most).astype(kind)


def setup_inputs(seed: int = 0) -> dict:
    seeds = jax.random.split(jax.random.key(seed), 15)
    lengths = draw_lengths(jax.random.fold_in(seeds[14], 71), 0)
    group_of = draw_group_of(jax.random.fold_in(seeds[14], 71), 0)
    query_pre = draw_query_pre(jax.random.fold_in(seeds[14], 71), 0)
    key_pre = draw_key_pre(jax.random.fold_in(seeds[14], 71), 0)
    value_pre = bell_draw(seeds[4], (TOKENS, KVH * HD), 1.0, 4.0, ((0, 32),))
    query_new = draw_query_new(jax.random.fold_in(seeds[14], 71), 0)
    key_new = bell_draw(seeds[6], (REQS, KVH * HD), 1.0, 4.0, ((1, 4),))
    value_new = bell_draw(seeds[7], (REQS, KVH * HD), 1.0, 4.0, ((1, 4),))
    hidden_new = bell_draw(seeds[8], (REQS, D), 0.5, 3.0, ((1, 8),))
    out_weight = bell_draw(seeds[9], (H * HD, D), (H * HD) ** -0.5, 0.0625, ((0, 4), (1, 8)))
    norm_gain = jnp.clip(1.0 + 0.18 * jax.random.normal(seeds[10], (D,), jnp.float32), 0.099609375, 1.8984375).astype(jnp.bfloat16)
    gate_weight = bell_draw(seeds[11], (D, FF_WIN), D ** -0.5, 0.0625, ((0, 8), (1, 4)))
    up_weight = bell_draw(seeds[12], (D, FF_WIN), D ** -0.5, 0.0625, ((0, 8), (1, 4)))
    down_weight = bell_draw(seeds[13], (FF_WIN, D), FF_WIN ** -0.5, 0.046875, ((0, 4), (1, 8)))
    return {"lengths": lengths, "group_of": group_of, "query_pre": query_pre, "key_pre": key_pre, "value_pre": value_pre, "query_new": query_new, "key_new": key_new, "value_new": value_new, "hidden_new": hidden_new, "out_weight": out_weight, "norm_gain": norm_gain, "gate_weight": gate_weight, "up_weight": up_weight, "down_weight": down_weight}


NEGATIVE = -1e+30

def request_starts(lengths, group_of):
    index = jnp.arange(lengths.shape[0], dtype=jnp.int32)
    same = group_of[None, :] == group_of[:, None]
    before = index[None, :] < index[:, None]
    return lax.optimization_barrier(jnp.sum(jnp.where(same & before, lengths[None, :], 0), axis=1)).astype(jnp.int32)

def slot_owner(group_idx, starts, lengths, group_of, first, count):
    slots = first + jnp.arange(count, dtype=jnp.int32)
    inside = (group_of[None, :] == group_idx) & (slots[:, None] >= starts[None, :]) & (slots[:, None] < (starts + lengths)[None, :])
    labels = jnp.arange(lengths.shape[0], dtype=jnp.int32) + 1
    return (lax.optimization_barrier(jnp.sum(jnp.where(inside, labels[None, :], 0), axis=1)) - 1).astype(jnp.int32)

def reference(lengths, group_of, query_pre, key_pre, value_pre, query_new, key_new, value_new, hidden_new, out_weight, norm_gain, gate_weight, up_weight, down_weight):
    scale = 1.0 / math.sqrt(HD)
    grouped = H // KVH
    block = min(512, G_TOK)
    starts = request_starts(lengths, group_of)
    query_groups = query_pre.reshape(GROUPS, G_TOK, KVH, grouped, HD)
    key_groups = key_pre.reshape(GROUPS, G_TOK, KVH, HD)
    value_groups = value_pre.reshape(GROUPS, G_TOK, KVH, HD)

    def one_group(packed):
        group_idx, queries, keys, values = packed
        owners = slot_owner(group_idx, starts, lengths, group_of, 0, G_TOK)
        keys_wide = keys.astype(jnp.float32)
        values_wide = values.astype(jnp.float32)
        columns = jnp.arange(G_TOK, dtype=jnp.int32)

        def one_block(block_idx):
            first = (block_idx * block).astype(jnp.int32)
            rows_q = lax.dynamic_slice_in_dim(queries, first, block, 0).astype(jnp.float32)
            owner_rows = lax.dynamic_slice_in_dim(owners, first, block, 0)
            rows = first + jnp.arange(block, dtype=jnp.int32)
            scores = jnp.einsum('qkgd,tkd->kgqt', rows_q, keys_wide) * scale
            allowed = (owner_rows[:, None] == owners[None, :]) & (owner_rows[:, None] >= 0) & (columns[None, :] <= rows[:, None])
            scores = jnp.where(allowed[None, None], scores, NEGATIVE)
            top = lax.optimization_barrier(jnp.max(scores, axis=-1, keepdims=True))
            weights = jnp.where(allowed[None, None], jnp.exp(scores - top), 0.0)
            total = lax.optimization_barrier(jnp.sum(weights, axis=-1))
            rounded = weights.astype(jnp.bfloat16).astype(jnp.float32)
            mixed = jnp.einsum('kgqt,tkd->qkgd', rounded, values_wide)
            live = owner_rows >= 0
            denom = jnp.where(live[None, None, :], total, 1.0)
            result = mixed / jnp.transpose(denom, (2, 0, 1))[..., None]
            result = jnp.where(live[:, None, None, None], result, 0.0)
            return result.reshape(block, H * HD).astype(jnp.bfloat16)
        outs = lax.map(one_block, jnp.arange(G_TOK // block, dtype=jnp.int32))
        return outs.reshape(G_TOK, H * HD)
    prefill = lax.map(one_group, (jnp.arange(GROUPS, dtype=jnp.int32), query_groups, key_groups, value_groups))
    prefill_attention = prefill.reshape(TOKENS, H * HD)

    def one_request(request):
        group_idx = group_of[request]
        owners = slot_owner(group_idx, starts, lengths, group_of, 0, G_TOK)
        keys = key_groups[group_idx].astype(jnp.float32)
        values = value_groups[group_idx].astype(jnp.float32)
        query = query_new[request].reshape(KVH, grouped, HD).astype(jnp.float32)
        own_key = key_new[request].reshape(KVH, HD).astype(jnp.float32)
        own_value = value_new[request].reshape(KVH, HD).astype(jnp.float32)
        scores = jnp.einsum('kgd,tkd->kgt', query, keys) * scale
        own = jnp.einsum('kgd,kd->kg', query, own_key) * scale
        match = owners == request
        scores = jnp.where(match[None, None, :], scores, NEGATIVE)
        top = jnp.maximum(lax.optimization_barrier(jnp.max(scores, axis=-1)), own)
        weights = jnp.where(match[None, None, :], jnp.exp(scores - top[..., None]), 0.0)
        own_weight = jnp.exp(own - top)
        total = lax.optimization_barrier(jnp.sum(weights, axis=-1)) + own_weight
        mixed = jnp.einsum('kgt,tkd->kgd', weights.astype(jnp.bfloat16).astype(jnp.float32), values)
        mixed = mixed + own_weight.astype(jnp.bfloat16).astype(jnp.float32)[..., None] * own_value[:, None, :]
        return (mixed / total[..., None]).reshape(H * HD).astype(jnp.bfloat16)
    decode_att = lax.map(one_request, jnp.arange(REQS, dtype=jnp.int32))
    resid = hidden_new.astype(jnp.float32) + jnp.dot(decode_att, out_weight, preferred_element_type=jnp.float32)
    squares = lax.optimization_barrier(jnp.sum(resid * resid, axis=-1, keepdims=True))
    normed = (resid * lax.rsqrt(squares / D + 1e-05) * norm_gain.astype(jnp.float32)[None, :]).astype(jnp.bfloat16)
    gate = jnp.dot(normed, gate_weight, preferred_element_type=jnp.float32)
    upper = jnp.dot(normed, up_weight, preferred_element_type=jnp.float32)
    hidden = (jax.nn.silu(gate) * upper).astype(jnp.bfloat16)
    decode_hidden = (resid + jnp.dot(hidden, down_weight, preferred_element_type=jnp.float32)).astype(jnp.bfloat16)
    return (prefill_attention, decode_hidden)
```

```python
import functools
import math

import jax
import jax.numpy as jnp
from jax import lax
from jax.experimental import pallas as pl
from jax.experimental.pallas import tpu as pltpu
from jax.sharding import PartitionSpec as P

HD = 128
Q_PER_KV = 8
MAX_IN_GROUP = 3
SLOTS_R = 4
NEGATIVE = -1e30
LOG2E = 1.4426950408889634
MIB = 1 << 20

F32 = jnp.float32
BF16 = jnp.bfloat16


def dot(a, b):
    return jnp.dot(a, b, preferred_element_type=F32)


def dot_t(a, b):
    return lax.dot_general(a, b, (((1,), (1,)), ((), ())), preferred_element_type=F32)


def plan(lengths, groups, group):
    ids = [jnp.int32(-1)] * MAX_IN_GROUP
    first = [jnp.int32(0)] * MAX_IN_GROUP
    end = [jnp.int32(0)] * MAX_IN_GROUP
    count = jnp.int32(0)
    used = jnp.int32(0)
    for r in range(lengths.shape[0]):
        mine = groups[r] == group
        length = lengths[r]
        for k in range(MAX_IN_GROUP):
            here = mine & (count == k)
            ids[k] = jnp.where(here, r, ids[k])
            first[k] = jnp.where(here, used, first[k])
            end[k] = jnp.where(here, used + length, end[k])
        count = count + jnp.where(mine, 1, 0)
        used = used + jnp.where(mine, length, 0)
    return ids, first, end


def pick_rows(ids, rows, columns):
    row = lax.broadcasted_iota(jnp.int32, (rows, columns), 0)
    column = lax.broadcasted_iota(jnp.int32, (rows, columns), 1)
    target = jnp.full((rows, columns), -1, jnp.int32)
    for k in range(MAX_IN_GROUP):
        target = jnp.where(row == k, ids[k], target)
    return jnp.where(column == target, 1.0, 0.0).astype(BF16)


def split3(x):
    hi = x.astype(BF16)
    rest = x - hi.astype(F32)
    mid = rest.astype(BF16)
    low = (rest - mid.astype(F32)).astype(BF16)
    return hi, mid, low


def select_kernel(lengths, groups, pos, query_ref, out_ref):
    ids, _, _ = plan(lengths, groups, pos[0])
    pick = pick_rows(ids, 8, query_ref.shape[0])
    out_ref[...] = dot(pick, query_ref[...])[:SLOTS_R].astype(BF16)


def partial_kernel(n, lengths, groups, pos, *refs):
    queries, (key_ref, value_ref), outs = refs[:n], refs[n : n + 2], refs[n + 2 :]
    _, first, end = plan(lengths, groups, pos[0])
    tokens = key_ref.shape[0]
    kv_per = queries[0].shape[1] // (HD * Q_PER_KV)
    rows = Q_PER_KV * SLOTS_R
    slot = pos[1] * tokens + lax.broadcasted_iota(jnp.int32, (rows, tokens), 1)
    rank = lax.broadcasted_iota(jnp.int32, (rows, tokens), 0) & (SLOTS_R - 1)
    low = jnp.zeros((rows, tokens), jnp.int32)
    high = jnp.zeros((rows, tokens), jnp.int32)
    for k in range(MAX_IN_GROUP):
        low = jnp.where(rank == k, first[k], low)
        high = jnp.where(rank == k, end[k], high)
    allowed = (slot >= low) & (slot < high)
    lane = lax.broadcasted_iota(jnp.int32, (rows, HD), 1)
    scale = 1.0 / math.sqrt(HD)
    for t in range(n):
        shard = lax.rem(pos[1] - t + n, n)
        query = queries[t][...].astype(F32)
        for i in range(kv_per):
            columns = pl.ds(pl.multiple_of((shard * kv_per + i) * HD, HD), HD)
            keys = key_ref[:, columns]
            values = value_ref[:, columns]
            heads = [query[:, (i * Q_PER_KV + h) * HD :][:, :HD] for h in range(Q_PER_KV)]
            stacked = jnp.concatenate(heads, axis=0).astype(BF16)
            scores = jnp.where(allowed, dot_t(stacked, keys) * scale, NEGATIVE)
            top = jnp.max(scores, axis=1, keepdims=True)
            weights = jnp.where(allowed, jnp.exp(scores - top), 0.0)
            total = jnp.sum(weights, axis=1, keepdims=True)
            some = total > 0.0
            mixed = dot(weights.astype(BF16), values) / jnp.where(some, total, 1.0)
            level = jnp.where(some, top + jnp.log(jnp.where(some, total, 1.0)), NEGATIVE)
            hi, mid, rest = split3(jnp.broadcast_to(level, (rows, HD)))
            stats = jnp.where(
                lane < 32, hi.astype(F32), jnp.where(lane < 64, mid.astype(F32), rest.astype(F32))
            )
            outs[t][i * rows : (i + 1) * rows, :] = jnp.concatenate([mixed, stats], axis=1).astype(
                BF16
            )


def combine_kernel(n, lengths, groups, pos, *refs):
    parts, (query_ref, key_ref, value_ref, out_ref) = refs[:n], refs[n:]
    ids, _, _ = plan(lengths, groups, pos[0])
    heads = query_ref.shape[1] // HD
    pick = pick_rows(ids, 8, key_ref.shape[0])
    keys = dot(pick, key_ref[...])[:SLOTS_R]
    values = dot(pick, value_ref[...])[:SLOTS_R]
    query = query_ref[...].astype(F32)

    def by_head(array, group):
        return jnp.concatenate(
            [array[:, (h // group) * HD :][:, :HD] for h in range(heads)], axis=0
        )

    own_score = jnp.sum(
        by_head(query, 1) * by_head(keys, Q_PER_KV), axis=1, keepdims=True
    ) * (1.0 / math.sqrt(HD))
    own_value = by_head(values, Q_PER_KV)
    mixes = []
    levels = []
    top = own_score
    for t in range(n):
        part = parts[t][...].astype(F32)
        stats = part[:, HD:]
        level = stats[:, 0:1] + stats[:, 32:33] + stats[:, 64:65]
        mixes.append(part[:, :HD])
        levels.append(level)
        top = jnp.maximum(top, level)
    own_weight = jnp.exp(own_score - top)
    total = own_weight
    mixed = own_weight.astype(BF16).astype(F32) * own_value
    for t in range(n):
        weight = jnp.exp(levels[t] - top)
        total = total + weight
        mixed = mixed + weight * mixes[t]
    result = mixed / total
    for h in range(heads):
        out_ref[:, h * HD : (h + 1) * HD] = result[h * SLOTS_R : (h + 1) * SLOTS_R].astype(BF16)


def project_kernel(count, pos, pick_ref, *refs):
    parts, (weight_ref, out_ref, att_ref, sum_ref) = refs[:count], refs[count:]
    step = pl.program_id(0)
    depth = weight_ref.shape[0]

    @pl.when(step == 0)
    def _():
        stacked = jnp.concatenate([part[...].astype(F32) for part in parts], axis=0).astype(BF16)
        att = dot(pick_ref[...], stacked).astype(BF16)
        for j in range(att_ref.shape[0]):
            att_ref[j] = att[:, j * depth : (j + 1) * depth]
        sum_ref[...] = jnp.zeros_like(sum_ref)

    sum_ref[...] += dot(att_ref[step], weight_ref[...])

    @pl.when(step == pl.num_programs(0) - 1)
    def _():
        out_ref[...] = sum_ref[...].astype(out_ref.dtype)


def gate_up_kernel(n, count, pos, *refs):
    parts, (hidden_ref, gain_ref, gate_ref, up_ref), outs = (
        refs[:n],
        refs[n : n + 4],
        refs[n + 4 :],
    )
    resid_ref, sends, scaled_ref = outs[0], outs[1 : 1 + count], outs[1 + count]
    step = pl.program_id(0)
    width = gate_ref.shape[1]

    @pl.when(step == 0)
    def _():
        resid = parts[0][...].astype(F32)
        for part in parts[1:]:
            resid = resid + part[...].astype(F32)
        resid = resid + hidden_ref[...].astype(F32)
        resid_ref[...] = resid
        scaled_ref[...] = (resid * gain_ref[...].astype(F32)).astype(BF16)
        squares = jnp.sum(resid * resid, axis=1, keepdims=True)
        rows = resid.shape[0]
        hi, mid, low = split3(jnp.broadcast_to(squares, (rows, HD)))
        lane = lax.broadcasted_iota(jnp.int32, (rows, HD), 1)
        stats = jnp.where(
            lane < 32, hi.astype(F32), jnp.where(lane < 64, mid.astype(F32), low.astype(F32))
        )
        for t in range(count):
            sends[t][:, 2 * width :] = stats.astype(BF16)

    scaled = scaled_ref[...]
    gate = dot(scaled, gate_ref[...]).astype(BF16)
    upper = dot(scaled, up_ref[...]).astype(BF16)
    for t in range(count):

        @pl.when(step == t)
        def _():
            sends[t][:, :width] = gate
            sends[t][:, width : 2 * width] = upper


def hidden_kernel(count, features, *refs):
    parts, out_ref = refs[:count], refs[count]
    width = out_ref.shape[1]
    total = parts[0][...].astype(F32)
    for part in parts[1:]:
        total = total + part[...].astype(F32)
    stats = total[:, 2 * width :]
    squares = stats[:, 0:1] + stats[:, 32:33] + stats[:, 64:65]
    inverse = lax.rsqrt(squares / features + 1e-05)
    gate = total[:, :width] * inverse
    upper = total[:, width : 2 * width] * inverse
    out_ref[...] = (gate / (1.0 + jnp.exp(-gate)) * upper).astype(BF16)


def down_kernel(count, n, pos, *refs):
    parts, weight_ref, sends, sum_ref = (
        refs[:count],
        refs[count],
        refs[count + 1 : count + 1 + n],
        refs[count + 1 + n],
    )
    step = pl.program_id(0)
    width = sends[0].shape[1]

    @pl.when(step == 0)
    def _():
        sum_ref[...] = jnp.zeros_like(sum_ref)

    for t in range(count):

        @pl.when(step == t)
        def _():
            sum_ref[...] += dot(parts[t][...], weight_ref[...])

    @pl.when(step == count - 1)
    def _():
        for own in range(n):

            @pl.when(pos[1] == own)
            def _():
                for t in range(n):
                    target = (own + t) % n
                    sends[t][...] = sum_ref[:, target * width : (target + 1) * width]


def prefill_kernel(n, lengths, groups, pos, *refs):
    query_ref, keys, values, out_ref, bias_ref, key_ref, value_ref = (
        refs[0],
        refs[1 : 1 + n],
        refs[1 + n : 1 + 2 * n],
        refs[1 + 2 * n],
        refs[2 + 2 * n],
        refs[3 + 2 * n],
        refs[4 + 2 * n],
    )
    tokens = query_ref.shape[0]
    _, first, end = plan(lengths, groups, pos[0])
    row_first = pos[1] * tokens
    lowest = row_first + tokens
    for k in range(MAX_IN_GROUP):
        meets = (end[k] > row_first) & (first[k] < row_first + tokens)
        lowest = jnp.where(meets, jnp.minimum(lowest, first[k]), lowest)
    needed = pos[1] - lowest // tokens + 1

    @pl.when(pl.program_id(0) == 0)
    def _():
        row = row_first + lax.broadcasted_iota(jnp.int32, (tokens, tokens), 0)
        column = lax.broadcasted_iota(jnp.int32, (tokens, tokens), 1)
        low = jnp.full((tokens, tokens), 1 << 30, jnp.int32)
        for k in range(MAX_IN_GROUP):
            low = jnp.where((row >= first[k]) & (row < end[k]), first[k], low)
        for t in range(n):
            slot = (pos[1] - t) * tokens + column
            bias_ref[:, t * tokens : (t + 1) * tokens] = jnp.where(
                (slot >= low) & (slot <= row), 0.0, NEGATIVE
            )
        value_ref[:, HD:] = jnp.ones((n * tokens, HD), BF16)

    for t in range(n):
        key_ref[t * tokens : (t + 1) * tokens, :] = keys[t][...]
        value_ref[t * tokens : (t + 1) * tokens, :HD] = values[t][...]

    @pl.when(needed == 0)
    def _():
        out_ref[...] = jnp.zeros_like(out_ref)

    row = row_first + lax.broadcasted_iota(jnp.int32, (tokens, HD), 0)
    live = row < 0
    for k in range(MAX_IN_GROUP):
        live = live | ((row >= first[k]) & (row < end[k]))
    constant = LOG2E / math.sqrt(HD)
    for count in range(1, n + 1):

        @pl.when(needed == count)
        def _():
            def head(h, carry):
                columns = pl.ds(pl.multiple_of(h * HD, HD), HD)
                scores = dot_t(query_ref[:, columns], key_ref[: count * tokens, :])
                scores = scores * constant + bias_ref[:, : count * tokens]
                top = jnp.max(scores, axis=1, keepdims=True)
                weights = jnp.exp2(scores - top).astype(BF16)
                mixed = dot(weights, value_ref[: count * tokens, :])
                result = mixed[:, :HD] / mixed[:, HD:]
                out_ref[:, columns] = jnp.where(live, result, 0.0).astype(BF16)
                return carry

            lax.fori_loop(0, Q_PER_KV, head, 0, unroll=2)


def call(body, scalars, args, outs, *, grid=None, in_specs=None, out_specs=None, scratch=(), cost, vmem=32):
    whole = pl.BlockSpec(memory_space=pltpu.VMEM)
    if grid is None:
        grid = (1,)
    flops, exps = cost
    moved = sum(a.size * a.dtype.itemsize for a in args) + sum(
        o.size * o.dtype.itemsize for o in outs
    )
    return pl.pallas_call(
        body,
        out_shape=list(outs),
        grid_spec=pltpu.PrefetchScalarGridSpec(
            num_scalar_prefetch=len(scalars),
            grid=grid,
            in_specs=in_specs or [whole] * len(args),
            out_specs=out_specs or [whole] * len(outs),
            scratch_shapes=list(scratch),
        ),
        compiler_params=pltpu.CompilerParams(
            dimension_semantics=("arbitrary",) * len(grid), vmem_limit_bytes=vmem * MIB
        ),
        cost_estimate=pl.CostEstimate(flops=flops, bytes_accessed=moved, transcendentals=exps),
    )(*scalars, *args)


def shift(x, axis, count, t):
    return lax.ppermute(x, axis, [(i, (i + t) % count) for i in range(count)])


def shards(
    lengths,
    group_of,
    query_pre,
    key_pre,
    value_pre,
    query_new,
    key_new,
    value_new,
    hidden_new,
    out_weight,
    norm_gain,
    gate_weight,
    up_weight,
    down_weight,
):
    n = lax.axis_size("seq")
    count = lax.axis_size("grp")
    seq = lax.axis_index("seq").astype(jnp.int32)
    group = lax.axis_index("grp").astype(jnp.int32)
    tokens = query_pre.shape[0]
    reqs = query_new.shape[0]
    kv_heads = key_pre.shape[1] // HD
    shard_width = query_new.shape[1]
    shard_heads = shard_width // HD
    columns = out_weight.shape[1]
    shape = jax.ShapeDtypeStruct
    vmem = pl.BlockSpec(memory_space=pltpu.VMEM)
    pos = jnp.stack([group, seq])
    scalars = (lengths, group_of, pos)

    keys, values = [key_pre], [value_pre]
    for t in range(1, n):
        hops = [(i, i + 1) for i in range(t - 1, n - 1)]
        keys.append(lax.ppermute(keys[-1], "seq", hops))
        values.append(lax.ppermute(values[-1], "seq", hops))

    (query,) = call(
        select_kernel,
        scalars,
        (query_new,),
        (shape((SLOTS_R, shard_width), BF16),),
        cost=(2 * 8 * reqs * shard_width, 0),
    )
    queries = [query] + [shift(query, "seq", n, t) for t in range(1, n)]
    rows = shard_heads * SLOTS_R
    partials = call(
        functools.partial(partial_kernel, n),
        scalars,
        (*queries, key_pre, value_pre),
        [shape((rows, 2 * HD), BF16)] * n,
        cost=(4 * n * rows * tokens * HD, n * rows * tokens),
    )
    partials = [partials[0]] + [shift(partials[t], "seq", n, n - t) for t in range(1, n)]
    (att,) = call(
        functools.partial(combine_kernel, n),
        scalars,
        (*partials, query, key_new, value_new),
        (shape((SLOTS_R, shard_width), BF16),),
        cost=(8 * n * rows * HD, n * rows),
    )
    atts = [att] + [shift(att, "grp", count, t) for t in range(1, count)]

    index = jnp.arange(reqs, dtype=jnp.int32)
    same = group_of[None, :] == group_of[:, None]
    rank = jnp.sum(jnp.where(same & (index[None, :] < index[:, None]), 1, 0), axis=1)
    place = lax.rem(group - group_of + count, count) * SLOTS_R + rank
    pick = (place[:, None] == jnp.arange(count * SLOTS_R, dtype=jnp.int32)[None, :]).astype(BF16)
    steps = 4
    depth = shard_width // steps
    (proj,) = call(
        functools.partial(project_kernel, count),
        (pos,),
        (pick, *atts, out_weight),
        (shape((reqs, columns), BF16),),
        grid=(steps,),
        in_specs=[vmem] * (1 + count) + [pl.BlockSpec((depth, columns), lambda j, p: (j, 0))],
        scratch=(pltpu.VMEM((steps, reqs, depth), BF16), pltpu.VMEM((reqs, columns), F32)),
        cost=(2 * reqs * shard_width * columns, 0),
    )
    projs = [proj] + [shift(proj, "seq", n, t) for t in range(1, n)]

    hidden_shard = gate_weight.shape[1]
    width = hidden_shard // count
    ahead = pl.BlockSpec((columns, width), lambda j, p: (0, lax.rem(p[0] + j, count)))
    resid, *terms = call(
        functools.partial(gate_up_kernel, n, count),
        (pos,),
        (*projs, hidden_new, norm_gain.reshape(1, -1), gate_weight, up_weight),
        [shape((reqs, columns), F32)] + [shape((reqs, 2 * width + HD), BF16)] * count,
        grid=(count,),
        in_specs=[vmem] * (n + 2) + [ahead, ahead],
        scratch=(pltpu.VMEM((reqs, columns), BF16),),
        cost=(4 * reqs * columns * hidden_shard, 0),
    )
    terms = [terms[0]] + [shift(terms[t], "grp", count, t) for t in range(1, count)]
    (hidden,) = call(
        functools.partial(hidden_kernel, count, columns * count),
        (),
        terms,
        (shape((reqs, width), BF16),),
        cost=(8 * count * reqs * width, reqs * width),
    )
    hiddens = [hidden] + [shift(hidden, "grp", count, t) for t in range(1, count)]
    share = columns // n
    downs = call(
        functools.partial(down_kernel, count, n),
        (pos,),
        (*hiddens, down_weight),
        [shape((reqs, share), F32)] * n,
        grid=(count,),
        in_specs=[vmem] * count
        + [pl.BlockSpec((width, columns), lambda j, p: (lax.rem(p[0] - j + count, count), 0))],
        scratch=(pltpu.VMEM((reqs, columns), F32),),
        cost=(2 * reqs * columns * hidden_shard, 0),
    )
    total = lax.dynamic_slice_in_dim(resid, seq * share, share, 1) + downs[0]
    for t in range(1, n):
        total = total + shift(downs[t], "seq", n, t)
    decode_hidden = total.astype(BF16)

    wide = Q_PER_KV * HD
    (prefill,) = call(
        functools.partial(prefill_kernel, n),
        scalars,
        (query_pre, *keys, *values),
        (shape(query_pre.shape, BF16),),
        grid=(kv_heads,),
        in_specs=[pl.BlockSpec((tokens, wide), lambda h, *_: (0, h))]
        + [pl.BlockSpec((tokens, HD), lambda h, *_: (0, h))] * (2 * n),
        out_specs=[pl.BlockSpec((tokens, wide), lambda h, *_: (0, h))],
        scratch=(
            pltpu.VMEM((tokens, n * tokens), F32),
            pltpu.VMEM((n * tokens, HD), BF16),
            pltpu.VMEM((n * tokens, 2 * HD), BF16),
        ),
        cost=(8 * n * tokens * query_pre.size, n * tokens * query_pre.size // HD),
        vmem=40,
    )
    return (prefill, decode_hidden)


def solution(mesh):
    return jax.shard_map(
        shards,
        mesh=mesh,
        in_specs=(
            P(),
            P(),
            P(("grp", "seq"), None),
            P(("grp", "seq"), None),
            P(("grp", "seq"), None),
            P(None, "seq"),
            P(None, "seq"),
            P(None, "seq"),
            P(None, "grp"),
            P("seq", "grp"),
            P("grp"),
            P("grp", "seq"),
            P("grp", "seq"),
            P("seq", "grp"),
        ),
        out_specs=(P(("grp", "seq"), None), P(None, ("grp", "seq"))),
        check_vma=False,
    )
```

```python
import functools
import math

import jax
import jax.numpy as jnp
from jax import lax
from jax.experimental import pallas as pl
from jax.experimental.pallas import tpu as pltpu
from jax.sharding import PartitionSpec as P

HD = 128
Q_PER_KV = 8
MAX_IN_GROUP = 3
SLOTS_R = 4
NEGATIVE = -1e30
LOG2E = 1.4426950408889634
MIB = 1 << 20
STREAM = 57

F32 = jnp.float32
BF16 = jnp.bfloat16


def dot(a, b):
    return jnp.dot(a, b, preferred_element_type=F32)


def dot_t(a, b):
    return lax.dot_general(a, b, (((1,), (1,)), ((), ())), preferred_element_type=F32)


def plan(facts):
    group = facts[0]
    reqs = (facts.shape[0] - 2) // 2
    ids = [jnp.int32(-1)] * MAX_IN_GROUP
    first = [jnp.int32(0)] * MAX_IN_GROUP
    end = [jnp.int32(0)] * MAX_IN_GROUP
    count = jnp.int32(0)
    used = jnp.int32(0)
    for r in range(reqs):
        mine = facts[2 + r] == group
        length = facts[2 + reqs + r]
        for k in range(MAX_IN_GROUP):
            here = mine & (count == k)
            ids[k] = jnp.where(here, r, ids[k])
            first[k] = jnp.where(here, used, first[k])
            end[k] = jnp.where(here, used + length, end[k])
        count = count + jnp.where(mine, 1, 0)
        used = used + jnp.where(mine, length, 0)
    return ids, first, end


def pick_rows(ids, rows, columns):
    row = lax.broadcasted_iota(jnp.int32, (rows, columns), 0)
    column = lax.broadcasted_iota(jnp.int32, (rows, columns), 1)
    target = jnp.full((rows, columns), -1, jnp.int32)
    for k in range(MAX_IN_GROUP):
        target = jnp.where(row == k, ids[k], target)
    return jnp.where(column == target, 1.0, 0.0).astype(BF16)


def split3(x):
    hi = x.astype(BF16)
    rest = x - hi.astype(F32)
    mid = rest.astype(BF16)
    low = (rest - mid.astype(F32)).astype(BF16)
    return hi, mid, low


def select_kernel(facts, query_ref, out_ref):
    ids, _, _ = plan(facts)
    pick = pick_rows(ids, 8, query_ref.shape[0])
    out_ref[...] = dot(pick, query_ref[...])[:SLOTS_R].astype(BF16)


def partial_kernel(n, facts, *refs):
    queries, (key_ref, value_ref), outs = refs[:n], refs[n : n + 2], refs[n + 2 :]
    _, first, end = plan(facts)
    tokens = key_ref.shape[0]
    kv_per = queries[0].shape[1] // (HD * Q_PER_KV)
    rows = Q_PER_KV * SLOTS_R
    slot = facts[1] * tokens + lax.broadcasted_iota(jnp.int32, (rows, tokens), 1)
    rank = lax.broadcasted_iota(jnp.int32, (rows, tokens), 0) & (SLOTS_R - 1)
    low = jnp.zeros((rows, tokens), jnp.int32)
    high = jnp.zeros((rows, tokens), jnp.int32)
    for k in range(MAX_IN_GROUP):
        low = jnp.where(rank == k, first[k], low)
        high = jnp.where(rank == k, end[k], high)
    allowed = (slot >= low) & (slot < high)
    lane = lax.broadcasted_iota(jnp.int32, (rows, HD), 1)
    scale = 1.0 / math.sqrt(HD)
    for t in range(n):
        shard = lax.rem(facts[1] - t + n, n)
        query = queries[t][...].astype(F32)
        for i in range(kv_per):
            columns = pl.ds(pl.multiple_of((shard * kv_per + i) * HD, HD), HD)
            keys = key_ref[:, columns]
            values = value_ref[:, columns]
            heads = [query[:, (i * Q_PER_KV + h) * HD :][:, :HD] for h in range(Q_PER_KV)]
            stacked = jnp.concatenate(heads, axis=0).astype(BF16)
            scores = jnp.where(allowed, dot_t(stacked, keys) * scale, NEGATIVE)
            top = jnp.max(scores, axis=1, keepdims=True)
            weights = jnp.where(allowed, jnp.exp(scores - top), 0.0)
            total = jnp.sum(weights, axis=1, keepdims=True)
            some = total > 0.0
            mixed = dot(weights.astype(BF16), values) / jnp.where(some, total, 1.0)
            level = jnp.where(some, top + jnp.log(jnp.where(some, total, 1.0)), NEGATIVE)
            hi, mid, rest = split3(jnp.broadcast_to(level, (rows, HD)))
            stats = jnp.where(
                lane < 32, hi.astype(F32), jnp.where(lane < 64, mid.astype(F32), rest.astype(F32))
            )
            outs[t][i * rows : (i + 1) * rows, :] = jnp.concatenate([mixed, stats], axis=1).astype(
                BF16
            )


def combine_kernel(n, count, facts, *refs):
    parts, (query_ref, key_ref, value_ref, out_ref) = refs[:n], refs[n:]
    ids, _, _ = plan(facts)
    heads = query_ref.shape[1] // HD
    pick = pick_rows(ids, 8, key_ref.shape[0])
    keys = dot(pick, key_ref[...])[:SLOTS_R]
    values = dot(pick, value_ref[...])[:SLOTS_R]
    query = query_ref[...].astype(F32)

    def by_head(array, group):
        return jnp.concatenate(
            [array[:, (h // group) * HD :][:, :HD] for h in range(heads)], axis=0
        )

    own_score = jnp.sum(
        by_head(query, 1) * by_head(keys, Q_PER_KV), axis=1, keepdims=True
    ) * (1.0 / math.sqrt(HD))
    own_value = by_head(values, Q_PER_KV)
    mixes = []
    levels = []
    top = own_score
    for t in range(n):
        part = parts[t][...].astype(F32)
        stats = part[:, HD:]
        level = stats[:, 0:1] + stats[:, 32:33] + stats[:, 64:65]
        mixes.append(part[:, :HD])
        levels.append(level)
        top = jnp.maximum(top, level)
    own_weight = jnp.exp(own_score - top)
    total = own_weight
    mixed = own_weight.astype(BF16).astype(F32) * own_value
    for t in range(n):
        weight = jnp.exp(levels[t] - top)
        total = total + weight
        mixed = mixed + weight * mixes[t]
    result = mixed / total
    for h in range(heads):
        head = result[h * SLOTS_R : (h + 1) * SLOTS_R].astype(BF16)
        for g in range(count):
            out_ref[g, :, h * HD : (h + 1) * HD] = head


def project_kernel(count, pick_ref, parts_ref, weight_ref, out_ref, att_ref, sum_ref):
    step = pl.program_id(0)
    depth = weight_ref.shape[0]

    @pl.when(step == 0)
    def _():
        stacked = jnp.concatenate([parts_ref[g].astype(F32) for g in range(count)], axis=0)
        att = dot(pick_ref[...], stacked.astype(BF16)).astype(BF16)
        for j in range(att_ref.shape[0]):
            att_ref[j] = att[:, j * depth : (j + 1) * depth]
        sum_ref[...] = jnp.zeros_like(sum_ref)

    sum_ref[...] += dot(att_ref[step], weight_ref[...])

    @pl.when(step == pl.num_programs(0) - 1)
    def _():
        out_ref[...] = sum_ref[...].astype(out_ref.dtype)


def gate_up_kernel(n, count, *refs):
    parts = refs[:n]
    hidden_ref, gain_ref, gate_ref, up_ref, resid_ref, send_ref, scaled_ref, stats_ref = refs[n:]
    step = pl.program_id(0)
    width = gate_ref.shape[1]

    @pl.when(step == 0)
    def _():
        resid = parts[0][...].astype(F32)
        for part in parts[1:]:
            resid = resid + part[...].astype(F32)
        resid = resid + hidden_ref[...].astype(F32)
        resid_ref[...] = resid
        scaled_ref[...] = (resid * gain_ref[...].astype(F32)).astype(BF16)
        squares = jnp.sum(resid * resid, axis=1, keepdims=True)
        rows = resid.shape[0]
        hi, mid, low = split3(jnp.broadcast_to(squares, (rows, HD)))
        lane = lax.broadcasted_iota(jnp.int32, (rows, HD), 1)
        stats_ref[...] = jnp.where(
            lane < 32, hi.astype(F32), jnp.where(lane < 64, mid.astype(F32), low.astype(F32))
        ).astype(BF16)

    scaled = scaled_ref[...]
    send_ref[step, :, :width] = dot(scaled, gate_ref[...]).astype(BF16)
    send_ref[step, :, width : 2 * width] = dot(scaled, up_ref[...]).astype(BF16)
    send_ref[step, :, 2 * width :] = stats_ref[...]


def hidden_kernel(count, features, parts_ref, out_ref):
    width = out_ref.shape[2]
    total = parts_ref[0].astype(F32)
    for g in range(1, count):
        total = total + parts_ref[g].astype(F32)
    stats = total[:, 2 * width :]
    squares = stats[:, 0:1] + stats[:, 32:33] + stats[:, 64:65]
    inverse = lax.rsqrt(squares / features + 1e-05)
    gate = total[:, :width] * inverse
    upper = total[:, width : 2 * width] * inverse
    hidden = (gate / (1.0 + jnp.exp(-gate)) * upper).astype(BF16)
    for g in range(count):
        out_ref[g] = hidden


def down_kernel(count, n, facts, parts_ref, weight_ref, *refs):
    sends, sum_ref = refs[:n], refs[n]
    step = pl.program_id(0)
    width = sends[0].shape[1]

    @pl.when(step == 0)
    def _():
        sum_ref[...] = jnp.zeros_like(sum_ref)

    sum_ref[...] += dot(parts_ref[step], weight_ref[...])

    for own in range(n):

        @pl.when((step == count - 1) & (facts[1] == own))
        def _():
            for t in range(n):
                target = (own + t) % n
                sends[t][...] = sum_ref[:, target * width : (target + 1) * width]


def row_facts(facts, tokens):
    _, first, end = plan(facts)
    row_first = facts[1] * tokens
    lowest = row_first + tokens
    for k in range(MAX_IN_GROUP):
        meets = (end[k] > row_first) & (first[k] < row_first + tokens)
        lowest = jnp.where(meets, jnp.minimum(lowest, first[k]), lowest)
    needed = facts[1] - lowest // tokens + 1
    return row_first, needed, first, end


def live_rows(row_first, first, end, tokens):
    row = row_first + lax.broadcasted_iota(jnp.int32, (tokens, HD), 0)
    live = row < 0
    for k in range(MAX_IN_GROUP):
        live = live | ((row >= first[k]) & (row < end[k]))
    return live


def store_bias(bias_ref, row_first, first, end, pieces):
    tokens = bias_ref.shape[0]
    row = row_first + lax.broadcasted_iota(jnp.int32, (tokens, tokens), 0)
    column = lax.broadcasted_iota(jnp.int32, (tokens, tokens), 1)
    low = jnp.full((tokens, tokens), 1 << 30, jnp.int32)
    for k in range(MAX_IN_GROUP):
        low = jnp.where((row >= first[k]) & (row < end[k]), first[k], low)
    for place, t in enumerate(pieces):
        slot = row_first - t * tokens + column
        bias_ref[:, place * tokens : (place + 1) * tokens] = jnp.where(
            (slot >= low) & (slot <= row), 0.0, NEGATIVE
        )


STACK = 4
EXP2 = LOG2E / math.sqrt(HD)


def inverse_of(x):
    guess = pl.reciprocal(x, approx=True)
    return guess * (2.0 - x * guess)


def stacked_heads(query_ref, at):
    return jnp.concatenate(
        [query_ref[:, h * HD : (h + 1) * HD] for h in range(at, at + STACK)], axis=0
    )


def near_kernel(m, facts, *refs):
    query_ref, keys, values = refs[0], refs[1 : 1 + m], refs[1 + m : 1 + 2 * m]
    out_ref, level_ref, bias_ref, value_ref = refs[1 + 2 * m :]
    tokens = query_ref.shape[0]
    row_first, needed, first, end = row_facts(facts, tokens)

    @pl.when(pl.program_id(0) == 0)
    def _():
        store_bias(bias_ref, row_first, first, end, range(m))
        value_ref[:, HD:] = jnp.ones((m * tokens, HD), BF16)

    @pl.when(needed == 0)
    def _():
        out_ref[...] = jnp.zeros_like(out_ref)

    def attend(count, masked, live):
        for t in range(count):
            value_ref[t * tokens : (t + 1) * tokens, :HD] = values[t][...]
        for at in range(0, Q_PER_KV, STACK):
            query = stacked_heads(query_ref, at)
            scores = []
            for t in range(count):
                score = dot_t(query, keys[t][...])
                if t in masked:
                    bias = bias_ref[:, t * tokens : (t + 1) * tokens]
                    score = (score.reshape(STACK, tokens, tokens) + bias[None]).reshape(
                        STACK * tokens, tokens
                    )
                scores.append(score)
            most = scores[0]
            for score in scores[1:]:
                most = jnp.maximum(most, score)
            top = jnp.max(most, axis=1, keepdims=True) * EXP2
            weights = jnp.concatenate(
                [jnp.exp2(score * EXP2 - top).astype(BF16) for score in scores], axis=1
            )
            mixed = dot(weights, value_ref[: count * tokens, :])
            result = mixed[:, :HD] * inverse_of(mixed[:, HD:])
            if count == m:
                level = top + jnp.log2(mixed[:, HD : HD + 1])
            for h in range(STACK):
                rows = slice(h * tokens, (h + 1) * tokens)
                head = result[rows]
                if live is not None:
                    head = jnp.where(live, head, 0.0)
                out_ref[:, (at + h) * HD : (at + h + 1) * HD] = head.astype(BF16)
                if count == m:
                    level_ref[:, at + h : at + h + 1] = level[rows]

    lone = needed < 0
    for k in range(MAX_IN_GROUP):
        lone = lone | (
            (first[k] <= row_first - (jnp.minimum(needed, m) - 1) * tokens)
            & (end[k] >= row_first + tokens)
        )
    before = 0
    for count in sorted({c for c in (1, 2, 3, m) if c <= m}):
        here = needed > before
        if count < m:
            here = here & (needed <= count)
        exact = here & ((needed >= count) if count == m else (needed == count)) & lone
        before = count

        @pl.when(exact)
        def _():
            attend(count, (0,), None)

        @pl.when(here & jnp.logical_not(exact))
        def _():
            attend(count, range(count), live_rows(row_first, first, end, tokens))


def far_kernel(n, facts, near_ref, level_ref, query_ref, key_ref, value_ref, out_ref, bias_ref, wide_ref):
    tokens = query_ref.shape[0]
    row_first, needed, first, end = row_facts(facts, tokens)

    @pl.when(needed < n)
    def _():
        out_ref[...] = near_ref[...]

    @pl.when(needed == n)
    def _():
        @pl.when(pl.program_id(0) == 0)
        def _():
            store_bias(bias_ref, row_first, first, end, (n - 1,))
            wide_ref[:, HD:] = jnp.ones((tokens, HD), BF16)

        wide_ref[:, :HD] = value_ref[...]
        live = live_rows(row_first, first, end, tokens)
        for at in range(0, Q_PER_KV, STACK):
            score = dot_t(stacked_heads(query_ref, at), key_ref[...])
            score = (score.reshape(STACK, tokens, tokens) + bias_ref[...][None]).reshape(
                STACK * tokens, tokens
            )
            level = jnp.concatenate(
                [level_ref[:, h : h + 1] for h in range(at, at + STACK)], axis=0
            )
            top = jnp.maximum(jnp.max(score, axis=1, keepdims=True) * EXP2, level)
            weights = jnp.exp2(score * EXP2 - top).astype(BF16)
            near_weight = jnp.exp2(level - top)
            mixed = dot(weights, wide_ref[...])
            inverse = inverse_of(mixed[:, HD:] + near_weight)
            for h in range(STACK):
                rows = slice(h * tokens, (h + 1) * tokens)
                columns = slice((at + h) * HD, (at + h + 1) * HD)
                near = near_ref[:, columns].astype(F32) * near_weight[rows]
                result = (mixed[rows, :HD] + near) * inverse[rows]
                out_ref[:, columns] = jnp.where(live, result, 0.0).astype(BF16)


def call(body, scalars, args, outs, *, grid=None, in_specs=None, out_specs=None, scratch=(), cost, vmem=6, aliases=None):
    whole = pl.BlockSpec(memory_space=pltpu.VMEM)
    if grid is None:
        grid = (1,)
    flops, exps = cost
    moved = sum(a.size * a.dtype.itemsize for a in args) + sum(
        o.size * o.dtype.itemsize for o in outs
    )
    return pl.pallas_call(
        body,
        out_shape=list(outs),
        grid_spec=pltpu.PrefetchScalarGridSpec(
            num_scalar_prefetch=len(scalars),
            grid=grid,
            in_specs=in_specs or [whole] * len(args),
            out_specs=out_specs or [whole] * len(outs),
            scratch_shapes=list(scratch),
        ),
        compiler_params=pltpu.CompilerParams(
            dimension_semantics=("arbitrary",) * len(grid), vmem_limit_bytes=vmem * MIB
        ),
        input_output_aliases=aliases or {},
        cost_estimate=pl.CostEstimate(flops=flops, bytes_accessed=moved, transcendentals=exps),
    )(*scalars, *args)


def shift(x, axis, count, t):
    return lax.ppermute(x, axis, [(i, (i + t) % count) for i in range(count)])


def shards(
    lengths,
    group_of,
    query_pre,
    key_pre,
    value_pre,
    query_new,
    key_new,
    value_new,
    hidden_new,
    out_weight,
    norm_gain,
    gate_weight,
    up_weight,
    down_weight,
):
    n = lax.axis_size("seq")
    count = lax.axis_size("grp")
    seq = lax.axis_index("seq").astype(jnp.int32)
    group = lax.axis_index("grp").astype(jnp.int32)
    tokens = query_pre.shape[0]
    reqs = query_new.shape[0]
    kv_heads = key_pre.shape[1] // HD
    shard_width = query_new.shape[1]
    shard_heads = shard_width // HD
    columns = out_weight.shape[1]
    shape = jax.ShapeDtypeStruct
    vmem = pl.BlockSpec(memory_space=pltpu.VMEM)
    facts = jnp.concatenate([jnp.stack([group, seq]), group_of, lengths])
    scalars = (facts,)

    def to_seq(x):
        return [x] + [shift(x, "seq", n, t) for t in range(1, n)]

    def to_grp(x):
        return lax.all_to_all(x, "grp", split_axis=0, concat_axis=0, tiled=True)

    def up(x, step, after):
        x, _ = lax.optimization_barrier((x, after))
        return lax.ppermute(x, "seq", [(i, i + 1) for i in range(step - 1, n - 1)])

    keys, values = [key_pre], [value_pre]

    (query,) = call(
        select_kernel,
        scalars,
        (query_new,),
        (shape((SLOTS_R, shard_width), BF16),),
        cost=(2 * 8 * reqs * shard_width, 0),
    )
    queries = to_seq(query)
    keys.append(up(keys[-1], 1, queries[1:]))
    rows = shard_heads * SLOTS_R
    partials = call(
        functools.partial(partial_kernel, n),
        scalars,
        (*queries, key_pre, value_pre),
        [shape((rows, 2 * HD), BF16)] * n,
        cost=(4 * n * rows * tokens * HD, n * rows * tokens),
    )
    partials = [partials[0]] + [shift(partials[t], "seq", n, n - t) for t in range(1, n)]
    values.append(up(values[-1], 1, partials[1:]))
    (att,) = call(
        functools.partial(combine_kernel, n, count),
        scalars,
        (*partials, query, key_new, value_new),
        (shape((count, SLOTS_R, shard_width), BF16),),
        cost=(8 * n * rows * HD, n * rows),
    )
    atts = to_grp(att)

    index = jnp.arange(reqs, dtype=jnp.int32)
    same = group_of[None, :] == group_of[:, None]
    rank = jnp.sum(jnp.where(same & (index[None, :] < index[:, None]), 1, 0), axis=1)
    place = group_of * SLOTS_R + rank
    pick = (place[:, None] == jnp.arange(count * SLOTS_R, dtype=jnp.int32)[None, :]).astype(BF16)
    steps = 4
    depth = shard_width // steps
    (proj,) = call(
        functools.partial(project_kernel, count),
        (),
        (pick, atts, out_weight),
        (shape((reqs, columns), BF16),),
        grid=(steps,),
        in_specs=[vmem, vmem, pl.BlockSpec((depth, columns), lambda j: (j, 0))],
        scratch=(pltpu.VMEM((steps, reqs, depth), BF16), pltpu.VMEM((reqs, columns), F32)),
        vmem=STREAM + 3,
        cost=(2 * reqs * shard_width * columns, 0),
    )
    projs = to_seq(proj)
    if n > 2:
        keys.append(up(keys[-1], 2, projs[1:]))
        values.append(up(values[-1], 2, projs[1:]))

    hidden_shard = gate_weight.shape[1]
    width = hidden_shard // count
    resid, terms = call(
        functools.partial(gate_up_kernel, n, count),
        (),
        (*projs, hidden_new, norm_gain.reshape(1, -1), gate_weight, up_weight),
        [shape((reqs, columns), F32), shape((count, reqs, 2 * width + HD), BF16)],
        grid=(count,),
        in_specs=[vmem] * (n + 2) + [pl.BlockSpec((columns, width), lambda j: (0, j))] * 2,
        scratch=(pltpu.VMEM((reqs, columns), BF16), pltpu.VMEM((reqs, HD), BF16)),
        vmem=STREAM,
        cost=(4 * reqs * columns * hidden_shard, 0),
    )
    (hidden,) = call(
        functools.partial(hidden_kernel, count, columns * count),
        (),
        (to_grp(terms),),
        (shape((count, reqs, width), BF16),),
        cost=(8 * count * reqs * width, reqs * width),
    )
    share = columns // n
    downs = call(
        functools.partial(down_kernel, count, n),
        scalars,
        (to_grp(hidden), down_weight),
        [shape((reqs, share), F32)] * n,
        grid=(count,),
        in_specs=[vmem, pl.BlockSpec((width, columns), lambda j, *_: (j, 0))],
        scratch=(pltpu.VMEM((reqs, columns), F32),),
        vmem=STREAM,
        cost=(2 * reqs * columns * hidden_shard, 0),
    )
    arrived = [shift(downs[t], "seq", n, t) for t in range(1, n)]
    total = lax.dynamic_slice_in_dim(resid, seq * share, share, 1) + downs[0]
    for part in arrived:
        total = total + part
    decode_hidden = total.astype(BF16)
    for step in range(len(keys), n):
        keys.append(up(keys[-1], step, arrived))
        values.append(up(values[-1], step, arrived))

    m = n - 1
    wide = Q_PER_KV * HD
    wide_block = pl.BlockSpec((tokens, wide), lambda h, *_: (0, h))
    head_block = pl.BlockSpec((tokens, HD), lambda h, *_: (0, h))
    level_block = pl.BlockSpec((None, tokens, Q_PER_KV), lambda h, *_: (h, 0, 0))
    near, levels = call(
        functools.partial(near_kernel, m),
        scalars,
        (query_pre, *keys[:m], *values[:m]),
        (shape(query_pre.shape, BF16), shape((kv_heads, tokens, Q_PER_KV), F32)),
        grid=(kv_heads,),
        in_specs=[wide_block] + [head_block] * (2 * m),
        out_specs=[wide_block, level_block],
        scratch=(
            pltpu.VMEM((tokens, m * tokens), F32),
            pltpu.VMEM((m * tokens, 2 * HD), BF16),
        ),
        cost=(8 * m * tokens * query_pre.size, m * tokens * query_pre.size // HD),
        vmem=STREAM + 3,
    )
    (prefill,) = call(
        functools.partial(far_kernel, n),
        scalars,
        (near, levels, query_pre, keys[m], values[m]),
        (shape(query_pre.shape, BF16),),
        grid=(kv_heads,),
        in_specs=[wide_block, level_block, wide_block, head_block, head_block],
        out_specs=[wide_block],
        scratch=(
            pltpu.VMEM((tokens, tokens), F32),
            pltpu.VMEM((tokens, 2 * HD), BF16),
        ),
        cost=(8 * tokens * query_pre.size, tokens * query_pre.size // HD),
        vmem=STREAM + 3,
        aliases={1: 0},
    )
    return (prefill, decode_hidden)


def solution(mesh):
    return jax.shard_map(
        shards,
        mesh=mesh,
        in_specs=(
            P(),
            P(),
            P(("grp", "seq"), None),
            P(("grp", "seq"), None),
            P(("grp", "seq"), None),
            P(None, "seq"),
            P(None, "seq"),
            P(None, "seq"),
            P(None, "grp"),
            P("seq", "grp"),
            P("grp"),
            P("grp", "seq"),
            P("grp", "seq"),
            P("seq", "grp"),
        ),
        out_specs=(P(("grp", "seq"), None), P(None, ("grp", "seq"))),
        check_vma=False,
    )
```

```python
import functools
import math

import jax
import jax.numpy as jnp
from jax import lax
from jax.experimental import pallas as pl
from jax.experimental.pallas import tpu as pltpu
from jax.sharding import PartitionSpec as P

HD = 128
Q_PER_KV = 8
MAX_IN_GROUP = 3
SLOTS_R = 4
NEGATIVE = -1e30
LOG2E = 1.4426950408889634
MIB = 1 << 20
STREAM = 57

F32 = jnp.float32
BF16 = jnp.bfloat16


def dot(a, b):
    return jnp.dot(a, b, preferred_element_type=F32)


def dot_t(a, b):
    return lax.dot_general(a, b, (((1,), (1,)), ((), ())), preferred_element_type=F32)


def plan(facts):
    group = facts[0]
    reqs = (facts.shape[0] - 2) // 2
    ids = [jnp.int32(-1)] * MAX_IN_GROUP
    first = [jnp.int32(0)] * MAX_IN_GROUP
    end = [jnp.int32(0)] * MAX_IN_GROUP
    count = jnp.int32(0)
    used = jnp.int32(0)
    for r in range(reqs):
        mine = facts[2 + r] == group
        length = facts[2 + reqs + r]
        for k in range(MAX_IN_GROUP):
            here = mine & (count == k)
            ids[k] = jnp.where(here, r, ids[k])
            first[k] = jnp.where(here, used, first[k])
            end[k] = jnp.where(here, used + length, end[k])
        count = count + jnp.where(mine, 1, 0)
        used = used + jnp.where(mine, length, 0)
    return ids, first, end


def pick_rows(ids, rows, columns):
    row = lax.broadcasted_iota(jnp.int32, (rows, columns), 0)
    column = lax.broadcasted_iota(jnp.int32, (rows, columns), 1)
    target = jnp.full((rows, columns), -1, jnp.int32)
    for k in range(MAX_IN_GROUP):
        target = jnp.where(row == k, ids[k], target)
    return jnp.where(column == target, 1.0, 0.0).astype(BF16)


def split3(x):
    hi = x.astype(BF16)
    rest = x - hi.astype(F32)
    mid = rest.astype(BF16)
    low = (rest - mid.astype(F32)).astype(BF16)
    return hi, mid, low


def select_kernel(facts, query_ref, out_ref):
    ids, _, _ = plan(facts)
    pick = pick_rows(ids, 8, query_ref.shape[0])
    out_ref[...] = dot(pick, query_ref[...])[:SLOTS_R].astype(BF16)


def by_head(array, group):
    heads = array.shape[1] // HD * group
    return jnp.concatenate([array[:, (h // group) * HD :][:, :HD] for h in range(heads)], axis=0)


def partial_kernel(n, facts, *refs):
    queries, sources, outs = refs[:n], refs[n : n + 4], refs[n + 4 : 2 * n + 4]
    own_ref, buffers, sems = refs[2 * n + 4], refs[2 * n + 5 : 2 * n + 9], refs[2 * n + 9]
    copies = [
        pltpu.make_async_copy(source, buffer, sems.at[i])
        for i, (source, buffer) in enumerate(zip(sources, buffers))
    ]
    for copy in copies:
        copy.start()
    ids, first, end = plan(facts)
    key_ref, value_ref, new_key_ref, new_value_ref = buffers
    tokens = key_ref.shape[0]
    kv_per = queries[0].shape[1] // (HD * Q_PER_KV)
    rows = Q_PER_KV * SLOTS_R
    slot = facts[1] * tokens + lax.broadcasted_iota(jnp.int32, (rows, tokens), 1)
    rank = lax.broadcasted_iota(jnp.int32, (rows, tokens), 0) & (SLOTS_R - 1)
    low = jnp.zeros((rows, tokens), jnp.int32)
    high = jnp.zeros((rows, tokens), jnp.int32)
    for k in range(MAX_IN_GROUP):
        low = jnp.where(rank == k, first[k], low)
        high = jnp.where(rank == k, end[k], high)
    allowed = (slot >= low) & (slot < high)
    lane = lax.broadcasted_iota(jnp.int32, (rows, HD), 1)
    scale = 1.0 / math.sqrt(HD)
    for copy in copies:
        copy.wait()
    for t in range(n):
        shard = lax.rem(facts[1] - t + n, n)
        query = queries[t][...].astype(F32)
        for i in range(kv_per):
            columns = pl.ds(pl.multiple_of((shard * kv_per + i) * HD, HD), HD)
            keys = key_ref[:, columns]
            values = value_ref[:, columns]
            stacked = by_head(query[:, i * Q_PER_KV * HD : (i + 1) * Q_PER_KV * HD], 1).astype(BF16)
            scores = jnp.where(allowed, dot_t(stacked, keys) * scale, NEGATIVE)
            top = jnp.max(scores, axis=1, keepdims=True)
            weights = jnp.where(allowed, jnp.exp(scores - top), 0.0)
            total = jnp.sum(weights, axis=1, keepdims=True)
            some = total > 0.0
            mixed = dot(weights.astype(BF16), values) / jnp.where(some, total, 1.0)
            level = jnp.where(some, top + jnp.log(jnp.where(some, total, 1.0)), NEGATIVE)
            hi, mid, rest = split3(jnp.broadcast_to(level, (rows, HD)))
            stats = jnp.where(
                lane < 32, hi.astype(F32), jnp.where(lane < 64, mid.astype(F32), rest.astype(F32))
            )
            outs[t][i * rows : (i + 1) * rows, :] = jnp.concatenate([mixed, stats], axis=1).astype(
                BF16
            )
    pick = pick_rows(ids, 8, new_key_ref.shape[0])
    keys = by_head(dot(pick, new_key_ref[...])[:SLOTS_R], Q_PER_KV)
    values = by_head(dot(pick, new_value_ref[...])[:SLOTS_R], Q_PER_KV)
    query = by_head(queries[0][...].astype(F32), 1)
    score = jnp.sum(query * keys, axis=1, keepdims=True) * scale
    own_ref[:, :HD] = values
    own_ref[:, HD:] = jnp.broadcast_to(score, values.shape)


def combine_kernel(n, count, *refs):
    parts, own_ref, out_ref = refs[:n], refs[n], refs[n + 1]
    own_value = own_ref[:, :HD]
    own_score = own_ref[:, HD : HD + 1]
    mixes = []
    levels = []
    top = own_score
    for t in range(n):
        part = parts[t][...].astype(F32)
        stats = part[:, HD:]
        level = stats[:, 0:1] + stats[:, 32:33] + stats[:, 64:65]
        mixes.append(part[:, :HD])
        levels.append(level)
        top = jnp.maximum(top, level)
    own_weight = jnp.exp(own_score - top)
    total = own_weight
    mixed = own_weight.astype(BF16).astype(F32) * own_value
    for t in range(n):
        weight = jnp.exp(levels[t] - top)
        total = total + weight
        mixed = mixed + weight * mixes[t]
    result = mixed / total
    for h in range(out_ref.shape[2] // HD):
        head = result[h * SLOTS_R : (h + 1) * SLOTS_R].astype(BF16)
        for g in range(count):
            out_ref[g, :, h * HD : (h + 1) * HD] = head


def start_all(pairs, sems):
    copies = [
        pltpu.make_async_copy(source, target, sems.at[i]) for i, (source, target) in enumerate(pairs)
    ]
    for copy in copies:
        copy.start()
    return copies


def project_kernel(count, steps, facts, parts_ref, weight_ref, out_ref, buffer_ref, sems):
    depth = weight_ref.shape[0] // steps
    blocks = [pl.ds(j * depth, depth) for j in range(steps)]
    copies = start_all([(weight_ref.at[b], buffer_ref.at[b]) for b in blocks], sems)
    reqs = out_ref.shape[0]
    row = lax.broadcasted_iota(jnp.int32, (reqs, count * SLOTS_R), 0)
    column = lax.broadcasted_iota(jnp.int32, (reqs, count * SLOTS_R), 1)
    place = jnp.zeros((reqs, count * SLOTS_R), jnp.int32)
    for r in range(reqs):
        rank = jnp.int32(0)
        for before in range(r):
            rank = rank + jnp.where(facts[2 + before] == facts[2 + r], 1, 0)
        place = jnp.where(row == r, facts[2 + r] * SLOTS_R + rank, place)
    pick = jnp.where(column == place, 1.0, 0.0).astype(BF16)
    stacked = jnp.concatenate([parts_ref[g].astype(F32) for g in range(count)], axis=0)
    att = dot(pick, stacked.astype(BF16)).astype(BF16)
    total = jnp.zeros(out_ref.shape, F32)
    for j in range(steps):
        copies[j].wait()
        total = total + dot(att[:, j * depth : (j + 1) * depth], buffer_ref[blocks[j]])
    out_ref[...] = total.astype(out_ref.dtype)


def gate_up_kernel(n, count, *refs):
    parts = refs[:n]
    hidden_ref, gain_ref, gate_ref, up_ref, resid_ref, send_ref, gates_ref, ups_ref, sems = refs[n:]
    width = gate_ref.shape[1] // count
    blocks = [pl.ds(g * width, width) for g in range(count)]
    pairs = []
    for b in blocks:
        pairs.append((gate_ref.at[:, b], gates_ref.at[:, b]))
        pairs.append((up_ref.at[:, b], ups_ref.at[:, b]))
    copies = start_all(pairs, sems)
    resid = parts[0][...].astype(F32)
    for part in parts[1:]:
        resid = resid + part[...].astype(F32)
    resid = resid + hidden_ref[...].astype(F32)
    resid_ref[...] = resid
    scaled = (resid * gain_ref[...].astype(F32)).astype(BF16)
    squares = jnp.sum(resid * resid, axis=1, keepdims=True)
    rows = resid.shape[0]
    hi, mid, low = split3(jnp.broadcast_to(squares, (rows, HD)))
    lane = lax.broadcasted_iota(jnp.int32, (rows, HD), 1)
    stats = jnp.where(
        lane < 32, hi.astype(F32), jnp.where(lane < 64, mid.astype(F32), low.astype(F32))
    ).astype(BF16)
    for g in range(count):
        send_ref[g, :, 2 * width :] = stats
    for g in range(count):
        copies[2 * g].wait()
        send_ref[g, :, :width] = dot(scaled, gates_ref[:, blocks[g]]).astype(BF16)
        copies[2 * g + 1].wait()
        send_ref[g, :, width : 2 * width] = dot(scaled, ups_ref[:, blocks[g]]).astype(BF16)


def hidden_kernel(count, features, parts_ref, out_ref):
    width = out_ref.shape[2]
    total = parts_ref[0].astype(F32)
    for g in range(1, count):
        total = total + parts_ref[g].astype(F32)
    stats = total[:, 2 * width :]
    squares = stats[:, 0:1] + stats[:, 32:33] + stats[:, 64:65]
    inverse = lax.rsqrt(squares / features + 1e-05)
    gate = total[:, :width] * inverse
    upper = total[:, width : 2 * width] * inverse
    hidden = (gate / (1.0 + jnp.exp(-gate)) * upper).astype(BF16)
    for g in range(count):
        out_ref[g] = hidden


def down_kernel(count, n, facts, parts_ref, weight_ref, *refs):
    sends, buffer_ref, sems = refs[:n], refs[n], refs[n + 1]
    depth = weight_ref.shape[0] // count
    width = sends[0].shape[1]
    blocks = [pl.ds(g * depth, depth) for g in range(count)]
    copies = start_all([(weight_ref.at[b], buffer_ref.at[b]) for b in blocks], sems)
    total = jnp.zeros((sends[0].shape[0], weight_ref.shape[1]), F32)
    for g in range(count):
        copies[g].wait()
        total = total + dot(parts_ref[g], buffer_ref[blocks[g]])
    for own in range(n):

        @pl.when(facts[1] == own)
        def _():
            for t in range(n):
                target = (own + t) % n
                sends[t][...] = total[:, target * width : (target + 1) * width]


def row_facts(facts, tokens):
    _, first, end = plan(facts)
    return facts[1] * tokens, facts[facts.shape[0] - 1], first, end


def live_rows(row_first, first, end, tokens):
    row = row_first + lax.broadcasted_iota(jnp.int32, (tokens, HD), 0)
    live = row < 0
    for k in range(MAX_IN_GROUP):
        live = live | ((row >= first[k]) & (row < end[k]))
    return live


def store_bias(bias_ref, row_first, first, end, pieces):
    tokens = bias_ref.shape[0]
    row = row_first + lax.broadcasted_iota(jnp.int32, (tokens, tokens), 0)
    column = lax.broadcasted_iota(jnp.int32, (tokens, tokens), 1)
    low = jnp.full((tokens, tokens), 1 << 30, jnp.int32)
    for k in range(MAX_IN_GROUP):
        low = jnp.where((row >= first[k]) & (row < end[k]), first[k], low)
    for place, t in enumerate(pieces):
        slot = row_first - t * tokens + column
        bias_ref[:, place * tokens : (place + 1) * tokens] = jnp.where(
            (slot >= low) & (slot <= row), 0.0, NEGATIVE
        )


STACK = 4
EXP2 = LOG2E / math.sqrt(HD)
SHIFT = 2.0


def inverse_of(x):
    guess = pl.reciprocal(x, approx=True)
    return guess * (2.0 - x * guess)


def attend(query_ref, keys, biases, values):
    tokens = query_ref.shape[0]
    lane = lax.broadcasted_iota(jnp.int32, (tokens, Q_PER_KV), 1)
    tops = jnp.zeros((tokens, Q_PER_KV), F32)
    totals = jnp.ones((tokens, Q_PER_KV), F32)
    heads = []
    for at in range(0, Q_PER_KV, STACK):
        query = jnp.concatenate(
            [query_ref[:, h * HD : (h + 1) * HD] for h in range(at, at + STACK)], axis=0
        )
        scores = []
        for key_ref, bias in zip(keys, biases):
            score = dot_t(query, key_ref[...])
            if bias is not None:
                score = (score.reshape(STACK, tokens, tokens) + bias[None]).reshape(
                    STACK * tokens, tokens
                )
            scores.append(score)
        most = scores[0]
        for score in scores[1:]:
            most = jnp.maximum(most, score)
        top = jnp.max(most, axis=1, keepdims=True) * EXP2 - SHIFT
        weights = []
        for score, bias in zip(scores, biases):
            power = score * EXP2 - top
            if bias is not None:
                power = jnp.minimum(power, SHIFT)
            weights.append(jnp.exp2(power.astype(BF16)))
        mixed = dot(jnp.concatenate(weights, axis=1), values)
        for h in range(STACK):
            head = mixed[h * tokens : (h + 1) * tokens]
            tops = jnp.where(lane == at + h, top[h * tokens : (h + 1) * tokens], tops)
            totals = jnp.where(lane == at + h, head[:, HD : HD + Q_PER_KV], totals)
            heads.append(head[:, :HD])
    return heads, tops, totals


def near_kernel(m, facts, *refs):
    query_ref, keys, values = refs[0], refs[1 : 1 + m], refs[1 + m : 1 + 2 * m]
    out_ref, level_ref, bias_ref, value_ref = refs[1 + 2 * m :]
    tokens = query_ref.shape[0]
    row_first, needed, first, end = row_facts(facts, tokens)

    @pl.when(pl.program_id(0) == 0)
    def _():
        store_bias(bias_ref, row_first, first, end, range(m))
        value_ref[:, HD:] = jnp.ones((m * tokens, HD), BF16)

    @pl.when(needed == 0)
    def _():
        out_ref[...] = jnp.zeros_like(out_ref)

    def run(count, lone):
        for t in range(count):
            value_ref[t * tokens : (t + 1) * tokens, :HD] = values[t][...]
        biases = [
            None if lone and t > 0 else bias_ref[:, t * tokens : (t + 1) * tokens]
            for t in range(count)
        ]
        heads, tops, totals = attend(query_ref, keys[:count], biases, value_ref[: count * tokens])
        inverse = inverse_of(totals)
        if count == m:
            level_ref[...] = tops + jnp.log2(totals)
        live = None if lone else live_rows(row_first, first, end, tokens)
        for h, head in enumerate(heads):
            head = head * inverse[:, h : h + 1]
            if not lone:
                head = jnp.where(live, head, 0.0)
            out_ref[:, h * HD : (h + 1) * HD] = head.astype(BF16)

    lone = needed < 0
    for k in range(MAX_IN_GROUP):
        lone = lone | (
            (first[k] <= row_first - (jnp.minimum(needed, m) - 1) * tokens)
            & (end[k] >= row_first + tokens)
        )
    for count in range(1, m + 1):
        here = (needed >= count) if count == m else (needed == count)

        @pl.when(here & lone)
        def _():
            run(count, True)

        @pl.when(here & jnp.logical_not(lone))
        def _():
            run(count, False)


def join_kernel(t, facts, near_ref, level_ref, query_ref, key_ref, value_ref, *refs):
    out_ref, out_level_ref, bias_ref, wide_ref = refs
    tokens = query_ref.shape[0]
    row_first, needed, first, end = row_facts(facts, tokens)

    @pl.when(needed <= t)
    def _():
        out_ref[...] = near_ref[...]
        out_level_ref[...] = level_ref[...]

    @pl.when(needed > t)
    def _():
        @pl.when(pl.program_id(0) == 0)
        def _():
            store_bias(bias_ref, row_first, first, end, (t,))
            wide_ref[:, HD:] = jnp.ones((tokens, HD), BF16)

        wide_ref[:, :HD] = value_ref[...]

        def run(lone):
            bias = None if lone else bias_ref[...]
            heads, tops, totals = attend(query_ref, [key_ref], [bias], wide_ref[...])
            level = level_ref[...]
            base = jnp.maximum(tops, level)
            near_weight = jnp.exp2(level - base)
            far_weight = jnp.exp2(tops - base)
            total = near_weight + far_weight * totals
            inverse = inverse_of(total)
            out_level_ref[...] = base + jnp.log2(total)
            near_weight = near_weight * inverse
            far_weight = far_weight * inverse
            live = None if lone else live_rows(row_first, first, end, tokens)
            for h, head in enumerate(heads):
                columns = slice(h * HD, (h + 1) * HD)
                near = near_ref[:, columns].astype(F32) * near_weight[:, h : h + 1]
                result = near + head * far_weight[:, h : h + 1]
                if not lone:
                    result = jnp.where(live, result, 0.0)
                out_ref[:, columns] = result.astype(BF16)

        lone = needed < 0
        for k in range(MAX_IN_GROUP):
            lone = lone | ((first[k] <= row_first - t * tokens) & (end[k] >= row_first + tokens))

        @pl.when(lone)
        def _():
            run(True)

        @pl.when(jnp.logical_not(lone))
        def _():
            run(False)


def call(body, scalars, args, outs, *, grid=None, in_specs=None, out_specs=None, scratch=(), cost, vmem=6, aliases=None):
    whole = pl.BlockSpec(memory_space=pltpu.VMEM)
    if grid is None:
        grid = (1,)
    flops, exps = cost
    moved = sum(a.size * a.dtype.itemsize for a in args) + sum(
        o.size * o.dtype.itemsize for o in outs
    )
    return pl.pallas_call(
        body,
        out_shape=list(outs),
        grid_spec=pltpu.PrefetchScalarGridSpec(
            num_scalar_prefetch=len(scalars),
            grid=grid,
            in_specs=in_specs or [whole] * len(args),
            out_specs=out_specs or [whole] * len(outs),
            scratch_shapes=list(scratch),
        ),
        compiler_params=pltpu.CompilerParams(
            dimension_semantics=("arbitrary",) * len(grid), vmem_limit_bytes=vmem * MIB
        ),
        input_output_aliases=aliases or {},
        cost_estimate=pl.CostEstimate(flops=flops, bytes_accessed=moved, transcendentals=exps),
    )(*scalars, *args)


def shift(x, axis, count, t):
    return lax.ppermute(x, axis, [(i, (i + t) % count) for i in range(count)])


def shards(
    lengths,
    group_of,
    query_pre,
    key_pre,
    value_pre,
    query_new,
    key_new,
    value_new,
    hidden_new,
    out_weight,
    norm_gain,
    gate_weight,
    up_weight,
    down_weight,
):
    n = lax.axis_size("seq")
    count = lax.axis_size("grp")
    seq = lax.axis_index("seq").astype(jnp.int32)
    group = lax.axis_index("grp").astype(jnp.int32)
    tokens = query_pre.shape[0]
    reqs = query_new.shape[0]
    kv_heads = key_pre.shape[1] // HD
    shard_width = query_new.shape[1]
    shard_heads = shard_width // HD
    columns = out_weight.shape[1]
    shape = jax.ShapeDtypeStruct
    vmem = pl.BlockSpec(memory_space=pltpu.VMEM)
    anywhere = pl.BlockSpec(memory_space=pl.ANY)
    dma = pltpu.SemaphoreType.DMA
    facts = jnp.concatenate([jnp.stack([group, seq]), group_of, lengths])
    scalars = (facts,)

    def to_seq(x):
        return [x] + [shift(x, "seq", n, t) for t in range(1, n)]

    def to_grp(x):
        return lax.all_to_all(x, "grp", split_axis=0, concat_axis=0, tiled=True)

    def tie(x, after):
        return lax.optimization_barrier((x, after))[0]

    def up(x, step, after):
        return lax.ppermute(tie(x, after), "seq", [(i, i + 1) for i in range(step - 1, n - 1)])

    keys, values = [key_pre], [value_pre]

    (query,) = call(
        select_kernel,
        scalars,
        (query_new,),
        (shape((SLOTS_R, shard_width), BF16),),
        cost=(2 * 8 * reqs * shard_width, 0),
    )
    queries = to_seq(query)
    keys.append(up(keys[-1], 1, queries[1:]))
    rows = shard_heads * SLOTS_R
    *partials, own = call(
        functools.partial(partial_kernel, n),
        scalars,
        (*queries, key_pre, value_pre, key_new, value_new),
        [shape((rows, 2 * HD), BF16)] * n + [shape((rows, 2 * HD), F32)],
        in_specs=[vmem] * n + [anywhere] * 4,
        scratch=[pltpu.VMEM(a.shape, BF16) for a in (key_pre, value_pre, key_new, value_new)]
        + [dma((4,))],
        cost=(4 * n * rows * tokens * HD, n * rows * tokens),
    )
    partials = [partials[0]] + [shift(partials[t], "seq", n, n - t) for t in range(1, n)]
    values.append(up(values[-1], 1, partials[1:]))
    (att,) = call(
        functools.partial(combine_kernel, n, count),
        (),
        (*partials, own),
        (shape((count, SLOTS_R, shard_width), BF16),),
        cost=(8 * n * rows * HD, n * rows),
    )
    atts = to_grp(att)

    atts = tie(atts, (keys[1], values[1]))
    if n > 2:
        keys.append(up(keys[-1], 2, values[1]))
    steps = 4
    (proj,) = call(
        functools.partial(project_kernel, count, steps),
        scalars,
        (atts, out_weight),
        (shape((reqs, columns), BF16),),
        in_specs=[vmem, anywhere],
        scratch=(pltpu.VMEM(out_weight.shape, BF16), dma((steps,))),
        cost=(2 * reqs * shard_width * columns, 0),
        vmem=STREAM + 3,
    )
    projs = to_seq(proj)
    if n > 2:
        values.append(up(values[-1], 2, projs[1:]))

    hidden_shard = gate_weight.shape[1]
    width = hidden_shard // count
    resid, terms = call(
        functools.partial(gate_up_kernel, n, count),
        (),
        (*projs, hidden_new, norm_gain.reshape(1, -1), gate_weight, up_weight),
        [shape((reqs, columns), F32), shape((count, reqs, 2 * width + HD), BF16)],
        in_specs=[vmem] * (n + 2) + [anywhere] * 2,
        scratch=(
            pltpu.VMEM(gate_weight.shape, BF16),
            pltpu.VMEM(up_weight.shape, BF16),
            dma((2 * count,)),
        ),
        cost=(4 * reqs * columns * hidden_shard, 0),
        vmem=STREAM,
    )
    gated = terms
    terms = tie(to_grp(terms), (keys[-1], values[-1]))
    (hidden,) = call(
        functools.partial(hidden_kernel, count, columns * count),
        (),
        (terms,),
        (shape((count, reqs, width), BF16),),
        cost=(8 * count * reqs * width, reqs * width),
    )
    if n > 3:
        keys.append(up(keys[-1], 3, values[-1]))
    hiddens = to_grp(hidden)
    if n > 3:
        values.append(up(values[-1], 3, hiddens))
    share = columns // n
    downs = call(
        functools.partial(down_kernel, count, n),
        scalars,
        (hiddens, down_weight),
        [shape((reqs, share), F32)] * n,
        in_specs=[vmem, anywhere],
        scratch=(pltpu.VMEM(down_weight.shape, BF16), dma((count,))),
        cost=(2 * reqs * columns * hidden_shard, 0),
        vmem=STREAM,
    )
    total = lax.dynamic_slice_in_dim(resid, seq * share, share, 1) + downs[0]
    for t in range(1, n):
        total = total + shift(downs[t], "seq", n, t)
    decode_hidden = total.astype(BF16)
    for step in range(len(keys), n):
        keys.append(up(keys[-1], step, values[-1]))
        values.append(up(values[-1], step, keys[-1]))

    index = jnp.arange(reqs, dtype=jnp.int32)
    same = group_of[None, :] == group_of[:, None]
    first = jnp.sum(jnp.where(same & (index[None, :] < index[:, None]), lengths[None, :], 0), axis=1)
    row_first = seq * tokens
    meets = (group_of == group) & (first + lengths > row_first) & (first < row_first + tokens)
    lowest = jnp.min(jnp.where(meets, first, row_first + tokens))
    scalars = (jnp.concatenate([facts, (seq - lax.div(lowest, tokens) + 1)[None]]),)
    m = min(2, n)
    wide = Q_PER_KV * HD
    wide_block = pl.BlockSpec((tokens, wide), lambda h, *_: (0, h))
    head_block = pl.BlockSpec((tokens, HD), lambda h, *_: (0, h))
    level_block = pl.BlockSpec((None, tokens, Q_PER_KV), lambda h, *_: (h, 0, 0))
    levels_shape = shape((kv_heads, tokens, Q_PER_KV), F32)
    prefill, levels = call(
        functools.partial(near_kernel, m),
        scalars,
        (tie(query_pre, gated), *keys[:m], *values[:m]),
        (shape(query_pre.shape, BF16), levels_shape),
        grid=(kv_heads,),
        in_specs=[wide_block] + [head_block] * (2 * m),
        out_specs=[wide_block, level_block],
        scratch=(
            pltpu.VMEM((tokens, m * tokens), F32),
            pltpu.VMEM((m * tokens, 2 * HD), BF16),
        ),
        cost=(8 * m * tokens * query_pre.size, m * tokens * query_pre.size // HD),
        vmem=STREAM + 3,
    )
    for t in range(m, n):

        def step(h, known, t=t):
            return jnp.where(known[known.shape[0] - 1] > t, h, 0)

        wide_block = pl.BlockSpec((tokens, wide), lambda h, known, step=step: (0, step(h, known)))
        head_block = pl.BlockSpec((tokens, HD), lambda h, known, step=step: (0, step(h, known)))
        level_block = pl.BlockSpec(
            (None, tokens, Q_PER_KV), lambda h, known, step=step: (step(h, known), 0, 0)
        )
        prefill, levels = call(
            functools.partial(join_kernel, t),
            scalars,
            (prefill, levels, query_pre, keys[t], values[t]),
            (shape(query_pre.shape, BF16), levels_shape),
            grid=(kv_heads,),
            in_specs=[wide_block, level_block, wide_block, head_block, head_block],
            out_specs=[wide_block, level_block],
            scratch=(
                pltpu.VMEM((tokens, tokens), F32),
                pltpu.VMEM((tokens, 2 * HD), BF16),
            ),
            cost=(8 * tokens * query_pre.size, tokens * query_pre.size // HD),
            vmem=STREAM + 3,
            aliases={1: 0, 2: 1},
        )
    return (prefill, decode_hidden)


def solution(mesh):
    return jax.shard_map(
        shards,
        mesh=mesh,
        in_specs=(
            P(),
            P(),
            P(("grp", "seq"), None),
            P(("grp", "seq"), None),
            P(("grp", "seq"), None),
            P(None, "seq"),
            P(None, "seq"),
            P(None, "seq"),
            P(None, "grp"),
            P("seq", "grp"),
            P("grp"),
            P("grp", "seq"),
            P("grp", "seq"),
            P("seq", "grp"),
        ),
        out_specs=(P(("grp", "seq"), None), P(None, ("grp", "seq"))),
        check_vma=False,
    )
```

```python
import functools
import math

import jax
import jax.numpy as jnp
from jax import lax
from jax.experimental import pallas as pl
from jax.experimental.pallas import tpu as pltpu
from jax.sharding import PartitionSpec as P

HD = 128
Q_PER_KV = 8
MAX_IN_GROUP = 3
SLOTS_R = 4
NEGATIVE = -1e30
LOG2E = 1.4426950408889634
MIB = 1 << 20
STREAM = 57

F32 = jnp.float32
BF16 = jnp.bfloat16


def dot(a, b):
    return jnp.dot(a, b, preferred_element_type=F32)


def dot_t(a, b):
    return lax.dot_general(a, b, (((1,), (1,)), ((), ())), preferred_element_type=F32)


def plan(facts):
    group = facts[0]
    reqs = (facts.shape[0] - 2) // 2
    ids = [jnp.int32(-1)] * MAX_IN_GROUP
    first = [jnp.int32(0)] * MAX_IN_GROUP
    end = [jnp.int32(0)] * MAX_IN_GROUP
    count = jnp.int32(0)
    used = jnp.int32(0)
    for r in range(reqs):
        mine = facts[2 + r] == group
        length = facts[2 + reqs + r]
        for k in range(MAX_IN_GROUP):
            here = mine & (count == k)
            ids[k] = jnp.where(here, r, ids[k])
            first[k] = jnp.where(here, used, first[k])
            end[k] = jnp.where(here, used + length, end[k])
        count = count + jnp.where(mine, 1, 0)
        used = used + jnp.where(mine, length, 0)
    return ids, first, end


def pick_rows(ids, rows, columns):
    row = lax.broadcasted_iota(jnp.int32, (rows, columns), 0)
    column = lax.broadcasted_iota(jnp.int32, (rows, columns), 1)
    target = jnp.full((rows, columns), -1, jnp.int32)
    for k in range(MAX_IN_GROUP):
        target = jnp.where(row == k, ids[k], target)
    return jnp.where(column == target, 1.0, 0.0).astype(BF16)


def split3(x):
    hi = x.astype(BF16)
    rest = x - hi.astype(F32)
    mid = rest.astype(BF16)
    low = (rest - mid.astype(F32)).astype(BF16)
    return hi, mid, low


def by_head(array, group):
    heads = array.shape[1] // HD * group
    return jnp.concatenate([array[:, (h // group) * HD :][:, :HD] for h in range(heads)], axis=0)


def select_kernel(facts, new_ref, query_ref, own_ref):
    ids, _, _ = plan(facts)
    width = query_ref.shape[1]
    kv_width = (new_ref.shape[1] - width) // 2
    new = dot(pick_rows(ids, 8, new_ref.shape[0]), new_ref[...])[:SLOTS_R]
    query_ref[...] = new[:, :width].astype(BF16)
    keys = by_head(new[:, width : width + kv_width], Q_PER_KV)
    values = by_head(new[:, width + kv_width :], Q_PER_KV)
    score = jnp.sum(by_head(new[:, :width], 1) * keys, axis=1, keepdims=True)
    own_ref[:, :HD] = values
    own_ref[:, HD:] = jnp.broadcast_to(score * (1.0 / math.sqrt(HD)), values.shape)


def partial_kernel(n, facts, *refs):
    queries, sources, outs = refs[:n], refs[n : n + 2], refs[n + 2 : 2 * n + 2]
    key_ref, value_ref, sems = refs[2 * n + 2 :]
    copies = start_all(list(zip(sources, (key_ref, value_ref))), sems)
    _, first, end = plan(facts)
    tokens = key_ref.shape[0]
    kv_per = queries[0].shape[1] // (HD * Q_PER_KV)
    rows = Q_PER_KV * SLOTS_R
    slot = facts[1] * tokens + lax.broadcasted_iota(jnp.int32, (rows, tokens), 1)
    rank = lax.broadcasted_iota(jnp.int32, (rows, tokens), 0) & (SLOTS_R - 1)
    low = jnp.zeros((rows, tokens), jnp.int32)
    high = jnp.zeros((rows, tokens), jnp.int32)
    for k in range(MAX_IN_GROUP):
        low = jnp.where(rank == k, first[k], low)
        high = jnp.where(rank == k, end[k], high)
    allowed = (slot >= low) & (slot < high)
    lane = lax.broadcasted_iota(jnp.int32, (rows, HD), 1)
    scale = 1.0 / math.sqrt(HD)
    for copy in copies:
        copy.wait()
    for t in range(n):
        shard = lax.rem(facts[1] - t + n, n)
        query = queries[t][...].astype(F32)
        for i in range(kv_per):
            columns = pl.ds(pl.multiple_of((shard * kv_per + i) * HD, HD), HD)
            keys = key_ref[:, columns]
            values = value_ref[:, columns]
            stacked = by_head(query[:, i * Q_PER_KV * HD : (i + 1) * Q_PER_KV * HD], 1).astype(BF16)
            scores = jnp.where(allowed, dot_t(stacked, keys) * scale, NEGATIVE)
            top = jnp.max(scores, axis=1, keepdims=True)
            weights = jnp.where(allowed, jnp.exp(scores - top), 0.0)
            total = jnp.sum(weights, axis=1, keepdims=True)
            some = total > 0.0
            mixed = dot(weights.astype(BF16), values) / jnp.where(some, total, 1.0)
            level = jnp.where(some, top + jnp.log(jnp.where(some, total, 1.0)), NEGATIVE)
            hi, mid, rest = split3(jnp.broadcast_to(level, (rows, HD)))
            stats = jnp.where(
                lane < 32, hi.astype(F32), jnp.where(lane < 64, mid.astype(F32), rest.astype(F32))
            )
            outs[t][i * rows : (i + 1) * rows, :] = jnp.concatenate([mixed, stats], axis=1).astype(
                BF16
            )


def combine_kernel(n, count, *refs):
    parts, own_ref, out_ref = refs[:n], refs[n], refs[n + 1]
    own_value = own_ref[:, :HD]
    own_score = own_ref[:, HD : HD + 1]
    mixes = []
    levels = []
    top = own_score
    for t in range(n):
        part = parts[t][...].astype(F32)
        stats = part[:, HD:]
        level = stats[:, 0:1] + stats[:, 32:33] + stats[:, 64:65]
        mixes.append(part[:, :HD])
        levels.append(level)
        top = jnp.maximum(top, level)
    own_weight = jnp.exp(own_score - top)
    total = own_weight
    mixed = own_weight.astype(BF16).astype(F32) * own_value
    for t in range(n):
        weight = jnp.exp(levels[t] - top)
        total = total + weight
        mixed = mixed + weight * mixes[t]
    result = mixed / total
    for h in range(out_ref.shape[2] // HD):
        head = result[h * SLOTS_R : (h + 1) * SLOTS_R].astype(BF16)
        for g in range(count):
            out_ref[g, :, h * HD : (h + 1) * HD] = head


def start_all(pairs, sems):
    copies = [
        pltpu.make_async_copy(source, target, sems.at[i]) for i, (source, target) in enumerate(pairs)
    ]
    for copy in copies:
        copy.start()
    return copies


class Stream:
    def __init__(self, pairs, sems, ahead):
        self.copies = [
            pltpu.make_async_copy(source, target, sems.at[i])
            for i, (source, target) in enumerate(pairs)
        ]
        self.ahead = ahead
        self.done = 0
        for copy in self.copies[:ahead]:
            copy.start()

    def next(self):
        self.copies[self.done].wait()
        later = self.done + self.ahead
        if later < len(self.copies):
            self.copies[later].start()
        self.done += 1


def project_kernel(count, steps, facts, parts_ref, weight_ref, out_ref, buffer_ref, sems):
    depth = weight_ref.shape[0] // steps
    blocks = [pl.ds(j * depth, depth) for j in range(steps)]
    stream = Stream([(weight_ref.at[b], buffer_ref.at[b]) for b in blocks], sems, 3)
    reqs = out_ref.shape[0]
    row = lax.broadcasted_iota(jnp.int32, (reqs, count * SLOTS_R), 0)
    column = lax.broadcasted_iota(jnp.int32, (reqs, count * SLOTS_R), 1)
    place = jnp.zeros((reqs, count * SLOTS_R), jnp.int32)
    for r in range(reqs):
        rank = jnp.int32(0)
        for before in range(r):
            rank = rank + jnp.where(facts[2 + before] == facts[2 + r], 1, 0)
        place = jnp.where(row == r, facts[2 + r] * SLOTS_R + rank, place)
    pick = jnp.where(column == place, 1.0, 0.0).astype(BF16)
    stacked = jnp.concatenate([parts_ref[g].astype(F32) for g in range(count)], axis=0)
    att = dot(pick, stacked.astype(BF16)).astype(BF16)
    total = jnp.zeros(out_ref.shape, F32)
    for j in range(steps):
        stream.next()
        total = total + dot(att[:, j * depth : (j + 1) * depth], buffer_ref[blocks[j]])
    out_ref[...] = total.astype(out_ref.dtype)


def gate_up_kernel(n, count, *refs):
    parts = refs[:n]
    hidden_ref, gain_ref, gate_ref, up_ref, resid_ref, send_ref, gates_ref, ups_ref, sems = refs[n:]
    width = gate_ref.shape[1] // count
    blocks = [pl.ds(g * width, width) for g in range(count)]
    pairs = []
    for b in blocks:
        pairs.append((gate_ref.at[:, b], gates_ref.at[:, b]))
        pairs.append((up_ref.at[:, b], ups_ref.at[:, b]))
    stream = Stream(pairs, sems, 4)
    resid = parts[0][...].astype(F32)
    for part in parts[1:]:
        resid = resid + part[...].astype(F32)
    resid = resid + hidden_ref[...].astype(F32)
    resid_ref[...] = resid
    scaled = (resid * gain_ref[...].astype(F32)).astype(BF16)
    squares = jnp.sum(resid * resid, axis=1, keepdims=True)
    rows = resid.shape[0]
    hi, mid, low = split3(jnp.broadcast_to(squares, (rows, HD)))
    lane = lax.broadcasted_iota(jnp.int32, (rows, HD), 1)
    stats = jnp.where(
        lane < 32, hi.astype(F32), jnp.where(lane < 64, mid.astype(F32), low.astype(F32))
    ).astype(BF16)
    for g in range(count):
        send_ref[g, :, 2 * width :] = stats
    for g in range(count):
        stream.next()
        send_ref[g, :, :width] = dot(scaled, gates_ref[:, blocks[g]]).astype(BF16)
        stream.next()
        send_ref[g, :, width : 2 * width] = dot(scaled, ups_ref[:, blocks[g]]).astype(BF16)


def hidden_kernel(count, features, parts_ref, out_ref):
    width = out_ref.shape[2]
    total = parts_ref[0].astype(F32)
    for g in range(1, count):
        total = total + parts_ref[g].astype(F32)
    stats = total[:, 2 * width :]
    squares = stats[:, 0:1] + stats[:, 32:33] + stats[:, 64:65]
    inverse = lax.rsqrt(squares / features + 1e-05)
    gate = total[:, :width] * inverse
    upper = total[:, width : 2 * width] * inverse
    hidden = (gate / (1.0 + jnp.exp(-gate)) * upper).astype(BF16)
    for g in range(count):
        out_ref[g] = hidden


def down_kernel(count, n, facts, parts_ref, weight_ref, *refs):
    sends, buffer_ref, sems = refs[:n], refs[n], refs[n + 1]
    depth = weight_ref.shape[0] // count
    width = sends[0].shape[1]
    blocks = [pl.ds(g * depth, depth) for g in range(count)]
    stream = Stream([(weight_ref.at[b], buffer_ref.at[b]) for b in blocks], sems, 3)
    total = jnp.zeros((sends[0].shape[0], weight_ref.shape[1]), F32)
    for g in range(count):
        stream.next()
        total = total + dot(parts_ref[g], buffer_ref[blocks[g]])
    for own in range(n):

        @pl.when(facts[1] == own)
        def _():
            for t in range(n):
                target = (own + t) % n
                sends[t][...] = total[:, target * width : (target + 1) * width]


def row_facts(facts, tokens):
    _, first, end = plan(facts)
    return facts[1] * tokens, facts[facts.shape[0] - 1], first, end


def live_rows(row_first, first, end, tokens):
    row = row_first + lax.broadcasted_iota(jnp.int32, (tokens, HD), 0)
    live = row < 0
    for k in range(MAX_IN_GROUP):
        live = live | ((row >= first[k]) & (row < end[k]))
    return live


def store_bias(bias_ref, row_first, first, end, pieces):
    tokens = bias_ref.shape[0]
    row = row_first + lax.broadcasted_iota(jnp.int32, (tokens, tokens), 0)
    column = lax.broadcasted_iota(jnp.int32, (tokens, tokens), 1)
    low = jnp.full((tokens, tokens), 1 << 30, jnp.int32)
    for k in range(MAX_IN_GROUP):
        low = jnp.where((row >= first[k]) & (row < end[k]), first[k], low)
    for place, t in enumerate(pieces):
        slot = row_first - t * tokens + column
        bias_ref[:, place * tokens : (place + 1) * tokens] = jnp.where(
            (slot >= low) & (slot <= row), 0.0, NEGATIVE
        )


EXP2 = LOG2E / math.sqrt(HD)


def inverse_of(x):
    guess = pl.reciprocal(x, approx=True)
    return guess * (2.0 - x * guess)


def interleave(*tasks):
    order = sorted(
        ((k + 0.5) / len(task), which, step)
        for which, task in enumerate(tasks)
        for k, step in enumerate(range(len(task)))
    )
    for _, which, step in order:
        tasks[which][step]()


def prefill_kernel(n, kv_step, facts, *refs):
    query_ref, keys, values = refs[0], refs[1 : 1 + n], refs[1 + n : 1 + 2 * n]
    out_ref, bias_ref, wide_ref, score_a, score_b, weight_a, weight_b = refs[1 + 2 * n :]
    scores, weights = (score_a, score_b), (weight_a, weight_b)
    tokens = query_ref.shape[0]
    heads = kv_step * Q_PER_KV
    row_first, needed, first, end = row_facts(facts, tokens)

    @pl.when(pl.program_id(0) == 0)
    def _():
        store_bias(bias_ref, row_first, first, end, range(n))
        wide_ref[:, :, HD:] = jnp.ones((kv_step, n * tokens, HD), BF16)

    @pl.when(needed == 0)
    def _():
        out_ref[...] = jnp.zeros_like(out_ref)

    def run(count, lone):
        slots = count * tokens
        chunk = {1: 128, 2: 64}.get(count, 32)
        for i in range(kv_step):
            for t in range(count):
                wide_ref[i, t * tokens : (t + 1) * tokens, :HD] = values[t][:, i * HD : (i + 1) * HD]
        live = None if lone else live_rows(row_first, first, end, tokens)

        def lanes(h, width=HD):
            return pl.ds(pl.multiple_of(h * width, HD), width)

        def score_steps(h, slot):
            def step(t):
                scores[slot][:, t * tokens : (t + 1) * tokens] = dot_t(
                    query_ref[:, lanes(h)], keys[t][:, lanes(h // Q_PER_KV)]
                )

            return [functools.partial(step, t) for t in range(count)]

        def weight_steps(slot):
            def step(at):
                rows = slice(at, at + chunk)
                parts = []
                for t in range(count):
                    columns = slice(t * tokens, (t + 1) * tokens)
                    part = scores[slot][rows, columns]
                    parts.append(part if lone and t > 0 else part + bias_ref[rows, columns])
                most = parts[0]
                for part in parts[1:]:
                    most = jnp.maximum(most, part)
                top = jnp.max(most, axis=1, keepdims=True)
                for t, part in enumerate(parts):
                    weights[slot][rows, t * tokens : (t + 1) * tokens] = jnp.exp2(
                        (part - top) * EXP2
                    ).astype(BF16)

            return [functools.partial(step, at) for at in range(0, tokens, chunk)]

        def value_steps(h, slot):
            def step(at):
                rows = slice(at, at + tokens // 2)
                mixed = dot(weights[slot][rows, :slots], wide_ref[h // Q_PER_KV, :slots])
                result = mixed[:, :HD] * inverse_of(mixed[:, HD:])
                if not lone:
                    result = jnp.where(live[rows], result, 0.0)
                out_ref[rows, lanes(h)] = result.astype(BF16)

            return [functools.partial(step, at) for at in range(0, tokens, tokens // 2)]

        interleave(score_steps(0, 0))
        interleave(score_steps(1, 1), weight_steps(0))

        def pair(j, carry):
            for slot in range(2):
                h = 2 * j + slot
                interleave(
                    score_steps(h + 2, slot), weight_steps(1 - slot), value_steps(h, slot)
                )
            return carry

        lax.fori_loop(0, heads // 2 - 1, pair, 0)
        interleave(weight_steps(1), value_steps(heads - 2, 0))
        interleave(value_steps(heads - 1, 1))

    lone = needed < 0
    for k in range(MAX_IN_GROUP):
        lone = lone | (
            (first[k] <= row_first - (needed - 1) * tokens) & (end[k] >= row_first + tokens)
        )
    before = 0
    for count in sorted({c for c in (1, 2, 3, n) if c <= n}):
        here = (needed > before) & (needed <= count)
        exact = (needed == count) & lone
        before = count

        @pl.when(exact)
        def _():
            run(count, True)

        @pl.when(here & jnp.logical_not(exact))
        def _():
            run(count, False)


def call(body, scalars, args, outs, *, grid=None, in_specs=None, out_specs=None, scratch=(), cost, vmem=6, aliases=None):
    whole = pl.BlockSpec(memory_space=pltpu.VMEM)
    if grid is None:
        grid = (1,)
    flops, exps = cost
    moved = sum(a.size * a.dtype.itemsize for a in args) + sum(
        o.size * o.dtype.itemsize for o in outs
    )
    return pl.pallas_call(
        body,
        out_shape=list(outs),
        grid_spec=pltpu.PrefetchScalarGridSpec(
            num_scalar_prefetch=len(scalars),
            grid=grid,
            in_specs=in_specs or [whole] * len(args),
            out_specs=out_specs or [whole] * len(outs),
            scratch_shapes=list(scratch),
        ),
        compiler_params=pltpu.CompilerParams(
            dimension_semantics=("arbitrary",) * len(grid), vmem_limit_bytes=int(vmem * MIB)
        ),
        input_output_aliases=aliases or {},
        cost_estimate=pl.CostEstimate(flops=flops, bytes_accessed=moved, transcendentals=exps),
    )(*scalars, *args)


def shift(x, axis, count, t):
    return lax.ppermute(x, axis, [(i, (i + t) % count) for i in range(count)])


def shards(
    lengths,
    group_of,
    query_pre,
    key_pre,
    value_pre,
    query_new,
    key_new,
    value_new,
    hidden_new,
    out_weight,
    norm_gain,
    gate_weight,
    up_weight,
    down_weight,
):
    n = lax.axis_size("seq")
    count = lax.axis_size("grp")
    seq = lax.axis_index("seq").astype(jnp.int32)
    group = lax.axis_index("grp").astype(jnp.int32)
    tokens = query_pre.shape[0]
    reqs = query_new.shape[0]
    kv_heads = key_pre.shape[1] // HD
    shard_width = query_new.shape[1]
    shard_heads = shard_width // HD
    columns = out_weight.shape[1]
    shape = jax.ShapeDtypeStruct
    vmem = pl.BlockSpec(memory_space=pltpu.VMEM)
    anywhere = pl.BlockSpec(memory_space=pl.ANY)
    dma = pltpu.SemaphoreType.DMA
    facts = jnp.concatenate([jnp.stack([group, seq]), group_of, lengths])
    scalars = (facts,)

    def to_seq(x):
        return [x] + [shift(x, "seq", n, t) for t in range(1, n)]

    def to_grp(x):
        return lax.all_to_all(x, "grp", split_axis=0, concat_axis=0, tiled=True)

    def tie(x, after):
        return lax.optimization_barrier((x, after))[0]

    def up(x, step, after):
        return lax.ppermute(tie(x, after), "seq", [(i, i + 1) for i in range(step - 1, n - 1)])

    keys, values = [key_pre], [value_pre]

    query, own = call(
        select_kernel,
        scalars,
        (jnp.concatenate([query_new, key_new, value_new], axis=1),),
        (shape((SLOTS_R, shard_width), BF16), shape((shard_heads * SLOTS_R, 2 * HD), F32)),
        cost=(2 * 8 * reqs * shard_width, 0),
    )
    queries = to_seq(query)
    keys.append(up(keys[-1], 1, queries[1:]))
    rows = shard_heads * SLOTS_R
    partials = call(
        functools.partial(partial_kernel, n),
        scalars,
        (*queries, key_pre, value_pre),
        [shape((rows, 2 * HD), BF16)] * n,
        in_specs=[vmem] * n + [anywhere] * 2,
        scratch=[pltpu.VMEM(a.shape, BF16) for a in (key_pre, value_pre)] + [dma((2,))],
        vmem=63.4,
        cost=(4 * n * rows * tokens * HD, n * rows * tokens),
    )
    partials = [partials[0]] + [shift(partials[t], "seq", n, n - t) for t in range(1, n)]
    values.append(up(values[-1], 1, partials[1:]))
    (att,) = call(
        functools.partial(combine_kernel, n, count),
        (),
        (*partials, own),
        (shape((count, SLOTS_R, shard_width), BF16),),
        cost=(8 * n * rows * HD, n * rows),
    )
    atts = to_grp(att)

    steps = 4
    (proj,) = call(
        functools.partial(project_kernel, count, steps),
        scalars,
        (atts, out_weight),
        (shape((reqs, columns), BF16),),
        in_specs=[vmem, anywhere],
        scratch=(pltpu.VMEM(out_weight.shape, BF16), dma((steps,))),
        cost=(2 * reqs * shard_width * columns, 0),
        vmem=STREAM + 3,
    )
    projs = to_seq(proj)
    if n > 2:
        keys.append(up(keys[-1], 2, (projs[1:], values[1])))

    hidden_shard = gate_weight.shape[1]
    width = hidden_shard // count
    resid, terms = call(
        functools.partial(gate_up_kernel, n, count),
        (),
        (*projs, hidden_new, norm_gain.reshape(1, -1), gate_weight, up_weight),
        [shape((reqs, columns), F32), shape((count, reqs, 2 * width + HD), BF16)],
        in_specs=[vmem] * (n + 2) + [anywhere] * 2,
        scratch=(
            pltpu.VMEM(gate_weight.shape, BF16),
            pltpu.VMEM(up_weight.shape, BF16),
            dma((2 * count,)),
        ),
        cost=(4 * reqs * columns * hidden_shard, 0),
        vmem=STREAM,
    )
    terms = tie(to_grp(terms), keys[-1])
    (hidden,) = call(
        functools.partial(hidden_kernel, count, columns * count),
        (),
        (terms,),
        (shape((count, reqs, width), BF16),),
        cost=(8 * count * reqs * width, reqs * width),
    )
    if n > 2:
        values.append(up(values[-1], 2, hidden))
    hiddens = to_grp(hidden)
    if n > 3:
        keys.append(up(keys[-1], 3, (values[-1], hiddens)))
    share = columns // n
    downs = call(
        functools.partial(down_kernel, count, n),
        scalars,
        (hiddens, down_weight),
        [shape((reqs, share), F32)] * n,
        in_specs=[vmem, anywhere],
        scratch=(pltpu.VMEM(down_weight.shape, BF16), dma((count,))),
        cost=(2 * reqs * columns * hidden_shard, 0),
        vmem=STREAM,
    )
    total = lax.dynamic_slice_in_dim(resid, seq * share, share, 1) + downs[0]
    arrived = [shift(downs[t], "seq", n, t) for t in range(1, n)]
    for part in arrived:
        total = total + part
    decode_hidden = total.astype(BF16)
    for step in range(len(values), n):
        if step == len(keys):
            keys.append(up(keys[-1], step, values[-1]))
        values.append(up(values[-1], step, (keys[-1], arrived)))

    index = jnp.arange(reqs, dtype=jnp.int32)
    same = group_of[None, :] == group_of[:, None]
    first = jnp.sum(jnp.where(same & (index[None, :] < index[:, None]), lengths[None, :], 0), axis=1)
    row_first = seq * tokens
    meets = (group_of == group) & (first + lengths > row_first) & (first < row_first + tokens)
    lowest = jnp.min(jnp.where(meets, first, row_first + tokens))
    scalars = (jnp.concatenate([facts, (seq - lax.div(lowest, tokens) + 1)[None]]),)
    kv_step = 2
    wide_block = pl.BlockSpec((tokens, kv_step * Q_PER_KV * HD), lambda h, *_: (0, h))
    head_block = pl.BlockSpec((tokens, kv_step * HD), lambda h, *_: (0, h))
    (prefill,) = call(
        functools.partial(prefill_kernel, n, kv_step),
        scalars,
        (query_pre, *keys, *values),
        (shape(query_pre.shape, BF16),),
        grid=(kv_heads // kv_step,),
        in_specs=[wide_block] + [head_block] * (2 * n),
        out_specs=[wide_block],
        scratch=[
            pltpu.VMEM((tokens, n * tokens), F32),
            pltpu.VMEM((kv_step, n * tokens, 2 * HD), BF16),
        ]
        + [pltpu.VMEM((tokens, n * tokens), F32)] * 2
        + [pltpu.VMEM((tokens, n * tokens), BF16)] * 2,
        cost=(8 * n * tokens * query_pre.size, n * tokens * query_pre.size // HD),
        vmem=STREAM + 3,
    )
    return (prefill, decode_hidden)


def solution(mesh):
    return jax.shard_map(
        shards,
        mesh=mesh,
        in_specs=(
            P(),
            P(),
            P(("grp", "seq"), None),
            P(("grp", "seq"), None),
            P(("grp", "seq"), None),
            P(None, "seq"),
            P(None, "seq"),
            P(None, "seq"),
            P(None, "grp"),
            P("seq", "grp"),
            P("grp"),
            P("grp", "seq"),
            P("grp", "seq"),
            P("seq", "grp"),
        ),
        out_specs=(P(("grp", "seq"), None), P(None, ("grp", "seq"))),
        check_vma=False,
    )
```

```python
import functools
import math

import jax
import jax.numpy as jnp
from jax import lax
from jax.experimental import pallas as pl
from jax.experimental.pallas import tpu as pltpu
from jax.sharding import PartitionSpec as P

HD = 128
Q_PER_KV = 8
MAX_IN_GROUP = 3
SLOTS_R = 4
NEGATIVE = -1e30
LOG2E = 1.4426950408889634
MIB = 1 << 20
STREAM = 57

F32 = jnp.float32
BF16 = jnp.bfloat16


def dot(a, b):
    return jnp.dot(a, b, preferred_element_type=F32)


def dot_t(a, b):
    return lax.dot_general(a, b, (((1,), (1,)), ((), ())), preferred_element_type=F32)


def plan(facts):
    group = facts[0]
    reqs = (facts.shape[0] - 2) // 2
    ids = [jnp.int32(-1)] * MAX_IN_GROUP
    first = [jnp.int32(0)] * MAX_IN_GROUP
    end = [jnp.int32(0)] * MAX_IN_GROUP
    count = jnp.int32(0)
    used = jnp.int32(0)
    for r in range(reqs):
        mine = facts[2 + r] == group
        length = facts[2 + reqs + r]
        for k in range(MAX_IN_GROUP):
            here = mine & (count == k)
            ids[k] = jnp.where(here, r, ids[k])
            first[k] = jnp.where(here, used, first[k])
            end[k] = jnp.where(here, used + length, end[k])
        count = count + jnp.where(mine, 1, 0)
        used = used + jnp.where(mine, length, 0)
    return ids, first, end


def pick_rows(ids, rows, columns):
    row = lax.broadcasted_iota(jnp.int32, (rows, columns), 0)
    column = lax.broadcasted_iota(jnp.int32, (rows, columns), 1)
    target = jnp.full((rows, columns), -1, jnp.int32)
    for k in range(MAX_IN_GROUP):
        target = jnp.where(row == k, ids[k], target)
    return jnp.where(column == target, 1.0, 0.0).astype(BF16)


def split3(x):
    hi = x.astype(BF16)
    rest = x - hi.astype(F32)
    mid = rest.astype(BF16)
    low = (rest - mid.astype(F32)).astype(BF16)
    return hi, mid, low


def by_head(array, group):
    heads = array.shape[1] // HD * group
    return jnp.concatenate([array[:, (h // group) * HD :][:, :HD] for h in range(heads)], axis=0)


def spread(x, lane):
    hi, mid, low = split3(jnp.broadcast_to(x, x.shape[:-1] + (HD,)))
    return jnp.where(
        lane < 32, hi.astype(F32), jnp.where(lane < 64, mid.astype(F32), low.astype(F32))
    ).astype(BF16)


def gathered(stats):
    return stats[..., 0:1] + stats[..., 32:33] + stats[..., 64:65]


def select_kernel(facts, new_ref, query_ref, own_ref):
    ids, _, _ = plan(facts)
    width = query_ref.shape[1]
    kv_width = (new_ref.shape[1] - width) // 2
    new = dot(pick_rows(ids, 8, new_ref.shape[0]), new_ref[...])[:SLOTS_R]
    query_ref[...] = new[:, :width].astype(BF16)
    keys = by_head(new[:, width : width + kv_width], Q_PER_KV)
    values = by_head(new[:, width + kv_width :], Q_PER_KV)
    score = jnp.sum(by_head(new[:, :width], 1) * keys, axis=1, keepdims=True)
    own_ref[:, :HD] = values
    own_ref[:, HD:] = jnp.broadcast_to(score * (1.0 / math.sqrt(HD)), values.shape)


def partial_kernel(n, facts, *refs):
    queries, sources, outs = refs[:n], refs[n : n + 2], refs[n + 2 : 2 * n + 2]
    key_ref, value_ref, query_ref, out_ref, sems = refs[2 * n + 2 :]
    copies = start_all(list(zip(sources, (key_ref, value_ref))), sems)
    _, first, end = plan(facts)
    tokens = key_ref.shape[0]
    kv_per = queries[0].shape[1] // (HD * Q_PER_KV)
    rows = Q_PER_KV * SLOTS_R
    slot = facts[1] * tokens + lax.broadcasted_iota(jnp.int32, (rows, tokens), 1)
    rank = lax.broadcasted_iota(jnp.int32, (rows, tokens), 0) & (SLOTS_R - 1)
    low = jnp.zeros((rows, tokens), jnp.int32)
    high = jnp.zeros((rows, tokens), jnp.int32)
    for k in range(MAX_IN_GROUP):
        low = jnp.where(rank == k, first[k], low)
        high = jnp.where(rank == k, end[k], high)
    allowed = (slot >= low) & (slot < high)
    lane = lax.broadcasted_iota(jnp.int32, (rows, HD), 1)
    scale = 1.0 / math.sqrt(HD)
    for t in range(n):
        query_ref[t] = queries[t][...].astype(F32)
    for copy in copies:
        copy.wait()

    def head(j, carry):
        t = j // kv_per
        i = j - t * kv_per
        shard = lax.rem(facts[1] - t + n, n)
        columns = pl.ds(pl.multiple_of((shard * kv_per + i) * HD, HD), HD)
        width = Q_PER_KV * HD
        query = query_ref[t, :, pl.ds(pl.multiple_of(i * width, width), width)]
        scores = dot_t(by_head(query, 1).astype(BF16), key_ref[:, columns]) * scale
        scores = jnp.where(allowed, scores, NEGATIVE)
        top = jnp.max(scores, axis=1, keepdims=True)
        weights = jnp.where(allowed, jnp.exp(scores - top), 0.0)
        total = jnp.sum(weights, axis=1, keepdims=True)
        some = total > 0.0
        mixed = dot(weights.astype(BF16), value_ref[:, columns]) / jnp.where(some, total, 1.0)
        level = jnp.where(some, top + jnp.log(jnp.where(some, total, 1.0)), NEGATIVE)
        out_ref[t, pl.ds(pl.multiple_of(i * rows, rows), rows), :] = jnp.concatenate(
            [mixed.astype(BF16), spread(level, lane)], axis=1
        )
        return carry

    lax.fori_loop(0, n * kv_per, head, 0)
    for t in range(n):
        outs[t][...] = out_ref[t]


def combine_kernel(n, *refs):
    parts, own_ref, out_ref = refs[:n], refs[n], refs[n + 1]
    own_value = own_ref[:, :HD]
    own_score = own_ref[:, HD : HD + 1]
    mixes = []
    levels = []
    top = own_score
    for t in range(n):
        part = parts[t][...].astype(F32)
        level = gathered(part[:, HD:])
        mixes.append(part[:, :HD])
        levels.append(level)
        top = jnp.maximum(top, level)
    own_weight = jnp.exp(own_score - top)
    total = own_weight
    mixed = own_weight.astype(BF16).astype(F32) * own_value
    for t in range(n):
        weight = jnp.exp(levels[t] - top)
        total = total + weight
        mixed = mixed + weight * mixes[t]
    result = mixed / total
    for h in range(out_ref.shape[2] // HD):
        head = result[h * SLOTS_R : (h + 1) * SLOTS_R].astype(BF16)
        out_ref[0, :, h * HD : (h + 1) * HD] = head


def append_kernel(first_ref, second_ref, out_ref):
    count = first_ref.shape[0]
    out_ref[:count] = first_ref[...]
    out_ref[count:] = second_ref[...]


def add_kernel(first_ref, second_ref, out_ref):
    out_ref[...] = (first_ref[...].astype(F32) + second_ref[...].astype(F32)).astype(out_ref.dtype)


def add_split_kernel(first_ref, second_ref, even_ref, odd_ref):
    for i in range(first_ref.shape[0]):
        (even_ref, odd_ref)[i % 2][i // 2] = first_ref[i] + second_ref[i]


def add_terms(first, second):
    total = first.astype(F32) + second.astype(F32)
    return total, gathered(total[:, -HD:])


def add_terms_kernel(first_ref, second_ref, *outs):
    rows, width = first_ref.shape[1:]
    lane = lax.broadcasted_iota(jnp.int32, (rows, HD), 1)
    for i in range(first_ref.shape[0]):
        total, squares = add_terms(first_ref[i], second_ref[i])
        out_ref, place = outs[i % len(outs)], i // len(outs)
        out_ref[place, :, : width - HD] = total[:, : width - HD].astype(BF16)
        out_ref[place, :, width - HD :] = spread(squares, lane)


def start_all(pairs, sems):
    copies = [
        pltpu.make_async_copy(source, target, sems.at[i]) for i, (source, target) in enumerate(pairs)
    ]
    for copy in copies:
        copy.start()
    return copies


def place_of(distance, count):
    place = distance * 0
    bits = count.bit_length() - 1
    for i in range(bits):
        place = place | (((distance >> i) & 1) << (bits - 1 - i))
    return place


def project_kernel(count, facts, near_ref, far_ref, weight_ref, out_ref, buffer_ref, att_ref, sems):
    steps, reqs, depth = att_ref.shape

    def copy(j):
        rows = pl.ds(pl.multiple_of(j * depth, depth), depth)
        return pltpu.make_async_copy(weight_ref.at[rows], buffer_ref.at[j], sems.at[j])

    for j in range(steps):
        copy(j).start()
    row = lax.broadcasted_iota(jnp.int32, (reqs, count * SLOTS_R), 0)
    column = lax.broadcasted_iota(jnp.int32, (reqs, count * SLOTS_R), 1)

    def request(r, place):
        def earlier(before, rank):
            return rank + jnp.where(facts[2 + before] == facts[2 + r], 1, 0)

        rank = lax.fori_loop(0, r, earlier, jnp.int32(0))
        group_place = place_of(facts[0] ^ facts[2 + r], count)
        return jnp.where(row == r, group_place * SLOTS_R + rank, place)

    place = lax.fori_loop(0, reqs, request, jnp.zeros(row.shape, jnp.int32))
    pick = jnp.where(column == place, 1.0, 0.0).astype(BF16)
    stacked = jnp.concatenate(
        [ref[g].astype(F32) for ref in (near_ref, far_ref) for g in range(count // 2)], axis=0
    )
    att = dot(pick, stacked.astype(BF16)).astype(BF16)
    for j in range(steps):
        att_ref[j] = att[:, j * depth : (j + 1) * depth]

    def block(j, total):
        copy(j).wait()
        return total + dot(att_ref[j], buffer_ref[j])

    total = lax.fori_loop(0, steps, block, jnp.zeros(out_ref.shape, F32))
    out_ref[...] = total.astype(out_ref.dtype)


def gate_up_kernel(count, facts, *refs):
    first_ref, second_ref, hidden_ref, gain_ref, gate_ref, up_ref = refs[:6]
    resid_ref, even_ref, odd_ref, gates_ref, ups_ref, send_ref, sems = refs[6:]
    width = gates_ref.shape[2]

    def copies(j):
        columns = pl.ds(pl.multiple_of((facts[0] ^ j) * width, width), width)
        return [
            pltpu.make_async_copy(gate_ref.at[:, columns], gates_ref.at[j], sems.at[0, j]),
            pltpu.make_async_copy(up_ref.at[:, columns], ups_ref.at[j], sems.at[1, j]),
        ]

    for j in range(count):
        for copy in copies(j):
            copy.start()
    resid = first_ref[...].astype(F32) + second_ref[...].astype(F32) + hidden_ref[...].astype(F32)
    resid_ref[...] = resid
    scaled = (resid * gain_ref[...].astype(F32)).astype(BF16)
    squares = jnp.sum(resid * resid, axis=1, keepdims=True)
    lane = lax.broadcasted_iota(jnp.int32, (resid.shape[0], HD), 1)
    stats = spread(squares, lane)

    def block(j, carry):
        for copy in copies(j):
            copy.wait()
        send_ref[j, :, :width] = dot(scaled, gates_ref[j]).astype(BF16)
        send_ref[j, :, width : 2 * width] = dot(scaled, ups_ref[j]).astype(BF16)
        send_ref[j, :, 2 * width :] = stats
        return carry

    lax.fori_loop(0, count, block, 0)
    for j in range(count):
        (even_ref, odd_ref)[j % 2][j // 2] = send_ref[j]


def hidden_kernel(features, own_ref, partner_ref, out_ref):
    width = out_ref.shape[2]
    for i in range(2):
        total, squares = add_terms(own_ref[i], partner_ref[1 - i])
        inverse = lax.rsqrt(squares / features + 1e-05)
        gate = total[:, :width] * inverse
        upper = total[:, width : 2 * width] * inverse
        out_ref[i] = (gate / (1.0 + jnp.exp(-gate)) * upper).astype(BF16)


def down_kernel(count, n, facts, near_ref, far_ref, weight_ref, *refs):
    even_ref, odd_ref, buffer_ref, hidden_ref, sems = refs
    depth = buffer_ref.shape[1]
    width = even_ref.shape[2]

    def copy(p):
        rows = pl.ds(pl.multiple_of((facts[0] ^ place_of(p, count)) * depth, depth), depth)
        return pltpu.make_async_copy(weight_ref.at[rows], buffer_ref.at[p], sems.at[p])

    for p in range(count):
        copy(jnp.int32(p)).start()
    hidden_ref[: count // 2] = near_ref[...]
    hidden_ref[count // 2 :] = far_ref[...]

    def block(p, total):
        copy(p).wait()
        return total + dot(hidden_ref[p], buffer_ref[p])

    shape = (hidden_ref.shape[1], weight_ref.shape[1])
    total = lax.fori_loop(0, count, block, jnp.zeros(shape, F32))
    for own in range(n):

        @pl.when(facts[1] == own)
        def _():
            for j in range(n):
                target = own ^ j
                (even_ref, odd_ref)[j % 2][j // 2] = total[:, target * width : (target + 1) * width]


def row_facts(facts, tokens):
    _, first, end = plan(facts)
    return facts[1] * tokens, facts[facts.shape[0] - 1], first, end


def live_rows(row_first, first, end, tokens):
    row = row_first + lax.broadcasted_iota(jnp.int32, (tokens, HD), 0)
    live = row < 0
    for k in range(MAX_IN_GROUP):
        live = live | ((row >= first[k]) & (row < end[k]))
    return live


def store_bias(bias_ref, row_first, first, end, pieces):
    tokens = bias_ref.shape[0]
    row = row_first + lax.broadcasted_iota(jnp.int32, (tokens, tokens), 0)
    column = lax.broadcasted_iota(jnp.int32, (tokens, tokens), 1)
    low = jnp.full((tokens, tokens), 1 << 30, jnp.int32)
    for k in range(MAX_IN_GROUP):
        low = jnp.where((row >= first[k]) & (row < end[k]), first[k], low)
    for place, t in enumerate(pieces):
        slot = row_first - t * tokens + column
        bias_ref[:, place * tokens : (place + 1) * tokens] = jnp.where(
            (slot >= low) & (slot <= row), 0.0, NEGATIVE
        )


EXP2 = LOG2E / math.sqrt(HD)


def inverse_of(x):
    guess = pl.reciprocal(x, approx=True)
    return guess * (2.0 - x * guess)


def interleave(*tasks):
    order = sorted(
        ((k + 0.5) / len(task), which, step)
        for which, task in enumerate(tasks)
        for k, step in enumerate(range(len(task)))
    )
    for _, which, step in order:
        tasks[which][step]()


def prefill_kernel(n, kv_step, facts, *refs):
    query_ref, keys, values = refs[0], refs[1 : 1 + n], refs[1 + n : 1 + 2 * n]
    out_ref, bias_ref, wide_ref, score_a, score_b, weight_a, weight_b = refs[1 + 2 * n :]
    scores, weights = (score_a, score_b), (weight_a, weight_b)
    tokens = query_ref.shape[0]
    heads = kv_step * Q_PER_KV
    row_first, needed, first, end = row_facts(facts, tokens)

    @pl.when(pl.program_id(0) == 0)
    def _():
        store_bias(bias_ref, row_first, first, end, range(n))
        wide_ref[:, :, HD:] = jnp.ones((kv_step, n * tokens, HD), BF16)

    @pl.when(needed == 0)
    def _():
        out_ref[...] = jnp.zeros_like(out_ref)

    def run(count, lone):
        slots = count * tokens
        chunk = {1: 128, 2: 64}.get(count, 32)
        for i in range(kv_step):
            for t in range(count):
                wide_ref[i, t * tokens : (t + 1) * tokens, :HD] = values[t][:, i * HD : (i + 1) * HD]
        live = None if lone else live_rows(row_first, first, end, tokens)

        def lanes(h, width=HD):
            return pl.ds(pl.multiple_of(h * width, HD), width)

        def score_steps(h, slot):
            def step(t):
                scores[slot][:, t * tokens : (t + 1) * tokens] = dot_t(
                    query_ref[:, lanes(h)], keys[t][:, lanes(h // Q_PER_KV)]
                )

            return [functools.partial(step, t) for t in range(count)]

        def weight_steps(slot):
            def step(at):
                rows = slice(at, at + chunk)
                parts = []
                for t in range(count):
                    columns = slice(t * tokens, (t + 1) * tokens)
                    part = scores[slot][rows, columns]
                    parts.append(part if lone and t > 0 else part + bias_ref[rows, columns])
                most = parts[0]
                for part in parts[1:]:
                    most = jnp.maximum(most, part)
                top = jnp.max(most, axis=1, keepdims=True)
                for t, part in enumerate(parts):
                    weights[slot][rows, t * tokens : (t + 1) * tokens] = jnp.exp2(
                        (part - top) * EXP2
                    ).astype(BF16)

            return [functools.partial(step, at) for at in range(0, tokens, chunk)]

        def value_steps(h, slot):
            def step(at):
                rows = slice(at, at + tokens // 2)
                mixed = dot(weights[slot][rows, :slots], wide_ref[h // Q_PER_KV, :slots])
                result = mixed[:, :HD] * inverse_of(mixed[:, HD:])
                if not lone:
                    result = jnp.where(live[rows], result, 0.0)
                out_ref[rows, lanes(h)] = result.astype(BF16)

            return [functools.partial(step, at) for at in range(0, tokens, tokens // 2)]

        interleave(score_steps(0, 0))
        interleave(score_steps(1, 1), weight_steps(0))

        def pair(j, carry):
            for slot in range(2):
                h = 2 * j + slot
                interleave(
                    score_steps(h + 2, slot), weight_steps(1 - slot), value_steps(h, slot)
                )
            return carry

        lax.fori_loop(0, heads // 2 - 1, pair, 0)
        interleave(weight_steps(1), value_steps(heads - 2, 0))
        interleave(value_steps(heads - 1, 1))

    lone = needed < 0
    for k in range(MAX_IN_GROUP):
        lone = lone | (
            (first[k] <= row_first - (needed - 1) * tokens) & (end[k] >= row_first + tokens)
        )
    before = 0
    for count in sorted({c for c in (1, 2, 3, n) if c <= n}):
        here = (needed > before) & (needed <= count)
        exact = (needed == count) & lone
        before = count

        @pl.when(exact)
        def _():
            run(count, True)

        @pl.when(here & jnp.logical_not(exact))
        def _():
            run(count, False)


def call(body, scalars, args, outs, *, grid=None, in_specs=None, out_specs=None, scratch=(), cost, vmem=6, aliases=None):
    whole = pl.BlockSpec(memory_space=pltpu.VMEM)
    if grid is None:
        grid = (1,)
    flops, exps = cost
    moved = sum(a.size * a.dtype.itemsize for a in args) + sum(
        o.size * o.dtype.itemsize for o in outs
    )
    return pl.pallas_call(
        body,
        out_shape=list(outs),
        grid_spec=pltpu.PrefetchScalarGridSpec(
            num_scalar_prefetch=len(scalars),
            grid=grid,
            in_specs=in_specs or [whole] * len(args),
            out_specs=out_specs or [whole] * len(outs),
            scratch_shapes=list(scratch),
        ),
        compiler_params=pltpu.CompilerParams(
            dimension_semantics=("arbitrary",) * len(grid), vmem_limit_bytes=int(vmem * MIB)
        ),
        input_output_aliases=aliases or {},
        cost_estimate=pl.CostEstimate(flops=flops, bytes_accessed=moved, transcendentals=exps),
    )(*scalars, *args)


def shift(x, axis, count, t):
    return lax.ppermute(x, axis, [(i, (i + t) % count) for i in range(count)])


def shards(
    lengths,
    group_of,
    query_pre,
    key_pre,
    value_pre,
    query_new,
    key_new,
    value_new,
    hidden_new,
    out_weight,
    norm_gain,
    gate_weight,
    up_weight,
    down_weight,
):
    n = lax.axis_size("seq")
    count = lax.axis_size("grp")
    seq = lax.axis_index("seq").astype(jnp.int32)
    group = lax.axis_index("grp").astype(jnp.int32)
    tokens = query_pre.shape[0]
    reqs = query_new.shape[0]
    kv_heads = key_pre.shape[1] // HD
    shard_width = query_new.shape[1]
    shard_heads = shard_width // HD
    columns = out_weight.shape[1]
    shape = jax.ShapeDtypeStruct
    vmem = pl.BlockSpec(memory_space=pltpu.VMEM)
    anywhere = pl.BlockSpec(memory_space=pl.ANY)
    dma = pltpu.SemaphoreType.DMA
    facts = jnp.concatenate([jnp.stack([group, seq]), group_of, lengths])
    scalars = (facts,)

    def to_seq(x):
        return [x] + [shift(x, "seq", n, t) for t in range(1, n)]

    def swap(x, axis, bit):
        size = n if axis == "seq" else count
        return lax.ppermute(x, axis, [(i, i ^ bit) for i in range(size)])

    def small(body, args, outs):
        size = sum(a.size for a in args)
        return call(body, (), args, outs, cost=(size, 0))

    def gather(x, bits):
        for bit in bits:
            other = swap(x, "grp", bit)
            if bit == 1:
                return x, other
            (x,) = small(append_kernel, (x, other), (shape((2 * x.shape[0],) + x.shape[1:], BF16),))

    def tie(x, after):
        return lax.optimization_barrier((x, after))[0]

    def up(x, step, after):
        return lax.ppermute(tie(x, after), "seq", [(i, i + 1) for i in range(step - 1, n - 1)])

    keys, values = [key_pre], [value_pre]

    query, own = call(
        select_kernel,
        scalars,
        (jnp.concatenate([query_new, key_new, value_new], axis=1),),
        (shape((SLOTS_R, shard_width), BF16), shape((shard_heads * SLOTS_R, 2 * HD), F32)),
        cost=(2 * 8 * reqs * shard_width, 0),
    )
    queries = to_seq(query)
    keys.append(up(keys[-1], 1, queries[1:]))
    rows = shard_heads * SLOTS_R
    partials = call(
        functools.partial(partial_kernel, n),
        scalars,
        (*queries, key_pre, value_pre),
        [shape((rows, 2 * HD), BF16)] * n,
        in_specs=[vmem] * n + [anywhere] * 2,
        scratch=[pltpu.VMEM(a.shape, BF16) for a in (key_pre, value_pre)]
        + [
            pltpu.VMEM((n, SLOTS_R, shard_width), F32),
            pltpu.VMEM((n, rows, 2 * HD), BF16),
            dma((2,)),
        ],
        cost=(4 * n * rows * tokens * HD, n * rows * tokens),
    )
    partials = [partials[0]] + [shift(partials[t], "seq", n, n - t) for t in range(1, n)]
    values.append(up(values[-1], 1, partials[1:]))
    (att,) = call(
        functools.partial(combine_kernel, n),
        (),
        (*partials, own),
        (shape((1, SLOTS_R, shard_width), BF16),),
        cost=(8 * n * rows * HD, n * rows),
    )
    bits = [1 << b for b in reversed(range(count.bit_length() - 1))]
    near_atts, far_atts = gather(att, bits)

    near_atts = tie(near_atts, (keys[1], values[1]))
    if n > 2:
        keys.append(up(keys[-1], 2, values[1]))
    steps = 8
    depth = shard_width // steps
    (proj,) = call(
        functools.partial(project_kernel, count),
        scalars,
        (near_atts, far_atts, out_weight),
        (shape((reqs, columns), BF16),),
        in_specs=[vmem, vmem, anywhere],
        scratch=(
            pltpu.VMEM((steps, depth, columns), BF16),
            pltpu.VMEM((steps, reqs, depth), BF16),
            dma((steps,)),
        ),
        cost=(2 * reqs * shard_width * columns, 0),
        vmem=STREAM + 3,
    )
    bit = 1
    while 2 * bit < n:
        (proj,) = small(add_kernel, (proj, swap(proj, "seq", bit)), (shape(proj.shape, BF16),))
        bit *= 2
    other = swap(proj, "seq", bit)
    if n > 2:
        values.append(up(values[-1], 2, (other, keys[-1])))

    hidden_shard = gate_weight.shape[1]
    width = hidden_shard // count
    block = (reqs, 2 * width + HD)
    resid, even, odd = call(
        functools.partial(gate_up_kernel, count),
        scalars,
        (proj, other, hidden_new, norm_gain.reshape(1, -1), gate_weight, up_weight),
        [shape((reqs, columns), F32)] + [shape((count // 2,) + block, BF16)] * 2,
        in_specs=[vmem] * 4 + [anywhere] * 2,
        scratch=(
            pltpu.VMEM((count, columns, width), BF16),
            pltpu.VMEM((count, columns, width), BF16),
            pltpu.VMEM((count,) + block, BF16),
            dma((2, count)),
        ),
        cost=(4 * reqs * columns * hidden_shard, 0),
        vmem=STREAM,
    )
    bit = 1
    while 2 * bit < count:
        other = swap(odd, "grp", bit)
        bit *= 2
        blocks = even.shape[0]
        if 2 * bit < count:
            outs = [shape((blocks // 2,) + block, BF16)] * 2
            even, odd = small(add_terms_kernel, (even, other), outs)
        else:
            (even,) = small(add_terms_kernel, (even, other), (shape((blocks,) + block, BF16),))
    other = swap(even, "grp", bit)
    (hidden,) = call(
        functools.partial(hidden_kernel, columns * count),
        (),
        (even, other),
        (shape((2, reqs, width), BF16),),
        cost=(32 * reqs * width, 2 * reqs * width),
    )
    if n > 3:
        keys.append(up(keys[-1], 3, (values[-1], hidden)))
        values.append(up(values[-1], 3, (values[-1], hidden)))
    near_hidden, far_hidden = gather(hidden, bits[1:])
    share = columns // n
    even, odd = call(
        functools.partial(down_kernel, count, n),
        scalars,
        (near_hidden, far_hidden, down_weight),
        [shape((n // 2, reqs, share), F32)] * 2,
        in_specs=[vmem, vmem, anywhere],
        scratch=(
            pltpu.VMEM((count, width, columns), BF16),
            pltpu.VMEM((count, reqs, width), BF16),
            dma((count,)),
        ),
        cost=(2 * reqs * columns * hidden_shard, 0),
        vmem=STREAM,
    )
    bit = 1
    while 2 * bit < n:
        outs = [shape((n // (4 * bit), reqs, share), F32)] * 2
        even, odd = small(add_split_kernel, (even, swap(odd, "seq", bit)), outs)
        bit *= 2
    total = lax.dynamic_slice_in_dim(resid, seq * share, share, 1)
    decode_hidden = (total + even[0] + swap(odd, "seq", bit)[0]).astype(BF16)
    for step in range(len(values), n):
        keys.append(up(keys[-1], step, values[-1]))
        values.append(up(values[-1], step, keys[-1]))

    index = jnp.arange(reqs, dtype=jnp.int32)
    same = group_of[None, :] == group_of[:, None]
    first = jnp.sum(jnp.where(same & (index[None, :] < index[:, None]), lengths[None, :], 0), axis=1)
    row_first = seq * tokens
    meets = (group_of == group) & (first + lengths > row_first) & (first < row_first + tokens)
    lowest = jnp.min(jnp.where(meets, first, row_first + tokens))
    scalars = (jnp.concatenate([facts, (seq - lax.div(lowest, tokens) + 1)[None]]),)
    kv_step = 2
    wide_block = pl.BlockSpec((tokens, kv_step * Q_PER_KV * HD), lambda h, *_: (0, h))
    head_block = pl.BlockSpec((tokens, kv_step * HD), lambda h, *_: (0, h))
    (prefill,) = call(
        functools.partial(prefill_kernel, n, kv_step),
        scalars,
        (query_pre, *keys, *values),
        (shape(query_pre.shape, BF16),),
        grid=(kv_heads // kv_step,),
        in_specs=[wide_block] + [head_block] * (2 * n),
        out_specs=[wide_block],
        scratch=[
            pltpu.VMEM((tokens, n * tokens), F32),
            pltpu.VMEM((kv_step, n * tokens, 2 * HD), BF16),
        ]
        + [pltpu.VMEM((tokens, n * tokens), F32)] * 2
        + [pltpu.VMEM((tokens, n * tokens), BF16)] * 2,
        cost=(8 * n * tokens * query_pre.size, n * tokens * query_pre.size // HD),
        vmem=STREAM + 3,
    )
    return (prefill, decode_hidden)


def solution(mesh):
    return jax.shard_map(
        shards,
        mesh=mesh,
        in_specs=(
            P(),
            P(),
            P(("grp", "seq"), None),
            P(("grp", "seq"), None),
            P(("grp", "seq"), None),
            P(None, "seq"),
            P(None, "seq"),
            P(None, "seq"),
            P(None, "grp"),
            P("seq", "grp"),
            P("grp"),
            P("grp", "seq"),
            P("grp", "seq"),
            P("seq", "grp"),
        ),
        out_specs=(P(("grp", "seq"), None), P(None, ("grp", "seq"))),
        check_vma=False,
    )
```

```python
import functools
import math

import jax
import jax.numpy as jnp
from jax import lax
from jax.experimental import pallas as pl
from jax.experimental.pallas import tpu as pltpu
from jax.sharding import PartitionSpec as P

HD = 128
Q_PER_KV = 8
MAX_IN_GROUP = 3
SLOTS_R = 4
NEGATIVE = -1e30
LOG2E = 1.4426950408889634
MIB = 1 << 20
STREAM = 57

F32 = jnp.float32
BF16 = jnp.bfloat16


def dot(a, b):
    return jnp.dot(a, b, preferred_element_type=F32)


def dot_t(a, b):
    return lax.dot_general(a, b, (((1,), (1,)), ((), ())), preferred_element_type=F32)


def plan(facts):
    group = facts[0]
    reqs = (facts.shape[0] - 2) // 2
    ids = [jnp.int32(-1)] * MAX_IN_GROUP
    first = [jnp.int32(0)] * MAX_IN_GROUP
    end = [jnp.int32(0)] * MAX_IN_GROUP
    count = jnp.int32(0)
    used = jnp.int32(0)
    for r in range(reqs):
        mine = facts[2 + r] == group
        length = facts[2 + reqs + r]
        for k in range(MAX_IN_GROUP):
            here = mine & (count == k)
            ids[k] = jnp.where(here, r, ids[k])
            first[k] = jnp.where(here, used, first[k])
            end[k] = jnp.where(here, used + length, end[k])
        count = count + jnp.where(mine, 1, 0)
        used = used + jnp.where(mine, length, 0)
    return ids, first, end


def pick_rows(ids, rows, columns):
    row = lax.broadcasted_iota(jnp.int32, (rows, columns), 0)
    column = lax.broadcasted_iota(jnp.int32, (rows, columns), 1)
    target = jnp.full((rows, columns), -1, jnp.int32)
    for k in range(MAX_IN_GROUP):
        target = jnp.where(row == k, ids[k], target)
    return jnp.where(column == target, 1.0, 0.0).astype(BF16)


def split3(x):
    hi = x.astype(BF16)
    rest = x - hi.astype(F32)
    mid = rest.astype(BF16)
    low = (rest - mid.astype(F32)).astype(BF16)
    return hi, mid, low


def by_head(array, group):
    heads = array.shape[1] // HD * group
    return jnp.concatenate([array[:, (h // group) * HD :][:, :HD] for h in range(heads)], axis=0)


def spread(x, lane):
    hi, mid, low = split3(jnp.broadcast_to(x, x.shape[:-1] + (HD,)))
    return jnp.where(
        lane < 32, hi.astype(F32), jnp.where(lane < 64, mid.astype(F32), low.astype(F32))
    ).astype(BF16)


def gathered(stats):
    return stats[..., 0:1] + stats[..., 32:33] + stats[..., 64:65]


def select_kernel(facts, new_ref, query_ref, own_ref):
    ids, _, _ = plan(facts)
    width = query_ref.shape[1]
    kv_width = (new_ref.shape[1] - width) // 2
    new = dot(pick_rows(ids, 8, new_ref.shape[0]), new_ref[...])[:SLOTS_R]
    query_ref[...] = new[:, :width].astype(BF16)
    keys = by_head(new[:, width : width + kv_width], Q_PER_KV)
    values = by_head(new[:, width + kv_width :], Q_PER_KV)
    score = jnp.sum(by_head(new[:, :width], 1) * keys, axis=1, keepdims=True)
    own_ref[:, :HD] = values
    own_ref[:, HD:] = jnp.broadcast_to(score * (1.0 / math.sqrt(HD)), values.shape)


def partial_kernel(n, facts, *refs):
    queries, sources, outs = refs[:n], refs[n : n + 2], refs[n + 2 : 2 * n + 2]
    key_ref, value_ref, query_ref, out_ref, sems = refs[2 * n + 2 :]
    copies = start_all(list(zip(sources, (key_ref, value_ref))), sems)
    _, first, end = plan(facts)
    tokens = key_ref.shape[0]
    kv_per = queries[0].shape[1] // (HD * Q_PER_KV)
    rows = Q_PER_KV * SLOTS_R
    slot = facts[1] * tokens + lax.broadcasted_iota(jnp.int32, (rows, tokens), 1)
    rank = lax.broadcasted_iota(jnp.int32, (rows, tokens), 0) & (SLOTS_R - 1)
    low = jnp.zeros((rows, tokens), jnp.int32)
    high = jnp.zeros((rows, tokens), jnp.int32)
    for k in range(MAX_IN_GROUP):
        low = jnp.where(rank == k, first[k], low)
        high = jnp.where(rank == k, end[k], high)
    allowed = (slot >= low) & (slot < high)
    lane = lax.broadcasted_iota(jnp.int32, (rows, HD), 1)
    scale = 1.0 / math.sqrt(HD)
    for t in range(n):
        query_ref[t] = queries[t][...].astype(F32)
    for copy in copies:
        copy.wait()

    def head(j, carry):
        t = j // kv_per
        i = j - t * kv_per
        shard = lax.rem(facts[1] - t + n, n)
        columns = pl.ds(pl.multiple_of((shard * kv_per + i) * HD, HD), HD)
        width = Q_PER_KV * HD
        query = query_ref[t, :, pl.ds(pl.multiple_of(i * width, width), width)]
        scores = dot_t(by_head(query, 1).astype(BF16), key_ref[:, columns]) * scale
        scores = jnp.where(allowed, scores, NEGATIVE)
        top = jnp.max(scores, axis=1, keepdims=True)
        weights = jnp.where(allowed, jnp.exp(scores - top), 0.0)
        total = jnp.sum(weights, axis=1, keepdims=True)
        some = total > 0.0
        mixed = dot(weights.astype(BF16), value_ref[:, columns]) / jnp.where(some, total, 1.0)
        level = jnp.where(some, top + jnp.log(jnp.where(some, total, 1.0)), NEGATIVE)
        out_ref[t, pl.ds(pl.multiple_of(i * rows, rows), rows), :] = jnp.concatenate(
            [mixed.astype(BF16), spread(level, lane)], axis=1
        )
        return carry

    lax.fori_loop(0, n * kv_per, head, 0)
    for t in range(n):
        outs[t][...] = out_ref[t]


def combine_kernel(n, count, *refs):
    parts, own_ref, out_ref = refs[:n], refs[n], refs[n + 1]
    own_value = own_ref[:, :HD]
    own_score = own_ref[:, HD : HD + 1]
    mixes = []
    levels = []
    top = own_score
    for t in range(n):
        part = parts[t][...].astype(F32)
        stats = part[:, HD:]
        level = stats[:, 0:1] + stats[:, 32:33] + stats[:, 64:65]
        mixes.append(part[:, :HD])
        levels.append(level)
        top = jnp.maximum(top, level)
    own_weight = jnp.exp(own_score - top)
    total = own_weight
    mixed = own_weight.astype(BF16).astype(F32) * own_value
    for t in range(n):
        weight = jnp.exp(levels[t] - top)
        total = total + weight
        mixed = mixed + weight * mixes[t]
    result = mixed / total
    for h in range(out_ref.shape[2] // HD):
        head = result[h * SLOTS_R : (h + 1) * SLOTS_R].astype(BF16)
        for g in range(count):
            out_ref[g, :, h * HD : (h + 1) * HD] = head


def start_all(pairs, sems):
    copies = [
        pltpu.make_async_copy(source, target, sems.at[i]) for i, (source, target) in enumerate(pairs)
    ]
    for copy in copies:
        copy.start()
    return copies


def project_kernel(count, pick_ref, parts_ref, weight_ref, out_ref, buffer_ref, att_ref, sems):
    steps, _, depth = att_ref.shape

    def copy(j):
        rows = pl.ds(pl.multiple_of(j * depth, depth), depth)
        return pltpu.make_async_copy(weight_ref.at[rows], buffer_ref.at[j], sems.at[j])

    for j in range(steps):
        copy(j).start()
    stacked = jnp.concatenate([parts_ref[g].astype(F32) for g in range(count)], axis=0)
    att = dot(pick_ref[...], stacked.astype(BF16)).astype(BF16)
    for j in range(steps):
        att_ref[j] = att[:, j * depth : (j + 1) * depth]

    def block(j, total):
        copy(j).wait()
        return total + dot(att_ref[j], buffer_ref[j])

    total = lax.fori_loop(0, steps, block, jnp.zeros(out_ref.shape, F32))
    out_ref[...] = total.astype(out_ref.dtype)


def gate_up_kernel(n, count, *refs):
    parts = refs[:n]
    hidden_ref, gain_ref, gate_ref, up_ref, resid_ref, send_ref, gates_ref, ups_ref, sems = refs[n:]
    width = gate_ref.shape[1] // count
    blocks = [pl.ds(g * width, width) for g in range(count)]
    pairs = []
    for b in blocks:
        pairs.append((gate_ref.at[:, b], gates_ref.at[:, b]))
        pairs.append((up_ref.at[:, b], ups_ref.at[:, b]))
    copies = start_all(pairs, sems)
    resid = parts[0][...].astype(F32)
    for part in parts[1:]:
        resid = resid + part[...].astype(F32)
    resid = resid + hidden_ref[...].astype(F32)
    resid_ref[...] = resid
    scaled = (resid * gain_ref[...].astype(F32)).astype(BF16)
    squares = jnp.sum(resid * resid, axis=1, keepdims=True)
    rows = resid.shape[0]
    hi, mid, low = split3(jnp.broadcast_to(squares, (rows, HD)))
    lane = lax.broadcasted_iota(jnp.int32, (rows, HD), 1)
    stats = jnp.where(
        lane < 32, hi.astype(F32), jnp.where(lane < 64, mid.astype(F32), low.astype(F32))
    ).astype(BF16)
    for g in range(count):
        send_ref[g, :, 2 * width :] = stats
    for g in range(count):
        copies[2 * g].wait()
        send_ref[g, :, :width] = dot(scaled, gates_ref[:, blocks[g]]).astype(BF16)
        copies[2 * g + 1].wait()
        send_ref[g, :, width : 2 * width] = dot(scaled, ups_ref[:, blocks[g]]).astype(BF16)


def hidden_kernel(count, features, parts_ref, out_ref):
    width = out_ref.shape[2]
    total = parts_ref[0].astype(F32)
    for g in range(1, count):
        total = total + parts_ref[g].astype(F32)
    stats = total[:, 2 * width :]
    squares = stats[:, 0:1] + stats[:, 32:33] + stats[:, 64:65]
    inverse = lax.rsqrt(squares / features + 1e-05)
    gate = total[:, :width] * inverse
    upper = total[:, width : 2 * width] * inverse
    hidden = (gate / (1.0 + jnp.exp(-gate)) * upper).astype(BF16)
    for g in range(count):
        out_ref[g] = hidden


def down_kernel(count, n, facts, parts_ref, weight_ref, *refs):
    sends, buffer_ref, sems = refs[:n], refs[n], refs[n + 1]
    depth = buffer_ref.shape[1]
    width = sends[0].shape[1]

    def copy(g):
        rows = pl.ds(pl.multiple_of(g * depth, depth), depth)
        return pltpu.make_async_copy(weight_ref.at[rows], buffer_ref.at[g], sems.at[g])

    for g in range(count):
        copy(g).start()

    def block(g, total):
        copy(g).wait()
        return total + dot(parts_ref[g], buffer_ref[g])

    shape = (sends[0].shape[0], weight_ref.shape[1])
    total = lax.fori_loop(0, count, block, jnp.zeros(shape, F32))
    for own in range(n):

        @pl.when(facts[1] == own)
        def _():
            for t in range(n):
                target = (own + t) % n
                sends[t][...] = total[:, target * width : (target + 1) * width]


def row_facts(facts, tokens):
    _, first, end = plan(facts)
    return facts[1] * tokens, facts[facts.shape[0] - 1], first, end


def live_rows(row_first, first, end, tokens):
    row = row_first + lax.broadcasted_iota(jnp.int32, (tokens, HD), 0)
    live = row < 0
    for k in range(MAX_IN_GROUP):
        live = live | ((row >= first[k]) & (row < end[k]))
    return live


def store_bias(bias_ref, row_first, first, end, pieces):
    tokens = bias_ref.shape[0]
    row = row_first + lax.broadcasted_iota(jnp.int32, (tokens, tokens), 0)
    column = lax.broadcasted_iota(jnp.int32, (tokens, tokens), 1)
    low = jnp.full((tokens, tokens), 1 << 30, jnp.int32)
    for k in range(MAX_IN_GROUP):
        low = jnp.where((row >= first[k]) & (row < end[k]), first[k], low)
    for place, t in enumerate(pieces):
        slot = row_first - t * tokens + column
        bias_ref[:, place * tokens : (place + 1) * tokens] = jnp.where(
            (slot >= low) & (slot <= row), 0.0, NEGATIVE
        )


EXP2 = LOG2E / math.sqrt(HD)


def inverse_of(x):
    guess = pl.reciprocal(x, approx=True)
    return guess * (2.0 - x * guess)


def interleave(*tasks):
    order = sorted(
        ((k + 0.5) / len(task), which, step)
        for which, task in enumerate(tasks)
        for k, step in enumerate(range(len(task)))
    )
    for _, which, step in order:
        tasks[which][step]()


def prefill_kernel(n, kv_step, facts, *refs):
    query_ref, keys, values = refs[0], refs[1 : 1 + n], refs[1 + n : 1 + 2 * n]
    out_ref, bias_ref, wide_ref, score_a, score_b, weight_a, weight_b = refs[1 + 2 * n :]
    scores, weights = (score_a, score_b), (weight_a, weight_b)
    tokens = query_ref.shape[0]
    heads = kv_step * Q_PER_KV
    row_first, needed, first, end = row_facts(facts, tokens)

    @pl.when(pl.program_id(0) == 0)
    def _():
        store_bias(bias_ref, row_first, first, end, range(n))
        wide_ref[:, :, HD:] = jnp.ones((kv_step, n * tokens, HD), BF16)

    @pl.when(needed == 0)
    def _():
        out_ref[...] = jnp.zeros_like(out_ref)

    def run(count, lone):
        slots = count * tokens
        chunk = 64
        for i in range(kv_step):
            for t in range(count):
                wide_ref[i, t * tokens : (t + 1) * tokens, :HD] = values[t][:, i * HD : (i + 1) * HD]
        live = None if lone else live_rows(row_first, first, end, tokens)

        def lanes(h, width=HD):
            return pl.ds(pl.multiple_of(h * width, HD), width)

        def score_steps(h, slot):
            def step(t):
                scores[slot][:, t * tokens : (t + 1) * tokens] = dot_t(
                    query_ref[:, lanes(h)], keys[t][:, lanes(h // Q_PER_KV)]
                )

            return [functools.partial(step, t) for t in range(count)]

        def weight_steps(slot):
            tops = {}

            def part(at, t):
                rows, columns = slice(at, at + chunk), slice(t * tokens, (t + 1) * tokens)
                score = scores[slot][rows, columns]
                return score if lone and t > 0 else score + bias_ref[rows, columns]

            def top_step(at):
                most = part(at, 0)
                for t in range(1, count):
                    most = jnp.maximum(most, part(at, t))
                tops[at] = jnp.max(most, axis=1, keepdims=True)

            def weight_step(at):
                top = tops.pop(at)
                for t in range(count):
                    weights[slot][at : at + chunk, t * tokens : (t + 1) * tokens] = jnp.exp2(
                        (part(at, t) - top) * EXP2
                    ).astype(BF16)

            starts = list(range(0, tokens, chunk))
            steps = [functools.partial(top_step, at) for at in starts[:2]]
            for i, at in enumerate(starts):
                steps.append(functools.partial(weight_step, at))
                if i + 2 < len(starts):
                    steps.append(functools.partial(top_step, starts[i + 2]))
            return steps

        def value_steps(h, slot):
            def step(at):
                rows = slice(at, at + tokens // 2)
                mixed = dot(weights[slot][rows, :slots], wide_ref[h // Q_PER_KV, :slots])
                result = mixed[:, :HD] * inverse_of(mixed[:, HD:])
                if not lone:
                    result = jnp.where(live[rows], result, 0.0)
                out_ref[rows, lanes(h)] = result.astype(BF16)

            return [functools.partial(step, at) for at in range(0, tokens, tokens // 2)]

        interleave(score_steps(0, 0))
        interleave(score_steps(1, 1), weight_steps(0))

        def pair(j, carry):
            for slot in range(2):
                h = 2 * j + slot
                interleave(
                    score_steps(h + 2, slot), weight_steps(1 - slot), value_steps(h, slot)
                )
            return carry

        lax.fori_loop(0, heads // 2 - 1, pair, 0)
        interleave(weight_steps(1), value_steps(heads - 2, 0))
        interleave(value_steps(heads - 1, 1))

    lone = needed < 0
    for k in range(MAX_IN_GROUP):
        lone = lone | (
            (first[k] <= row_first - (needed - 1) * tokens) & (end[k] >= row_first + tokens)
        )
    before = 0
    for count in sorted({c for c in (1, 2, 3, n) if c <= n}):
        here = (needed > before) & (needed <= count)
        exact = (needed == count) & lone
        before = count

        @pl.when(exact)
        def _():
            run(count, True)

        @pl.when(here & jnp.logical_not(exact))
        def _():
            run(count, False)


def call(body, scalars, args, outs, *, grid=None, in_specs=None, out_specs=None, scratch=(), cost, vmem=6, aliases=None):
    whole = pl.BlockSpec(memory_space=pltpu.VMEM)
    if grid is None:
        grid = (1,)
    flops, exps = cost
    moved = sum(a.size * a.dtype.itemsize for a in args) + sum(
        o.size * o.dtype.itemsize for o in outs
    )
    return pl.pallas_call(
        body,
        out_shape=list(outs),
        grid_spec=pltpu.PrefetchScalarGridSpec(
            num_scalar_prefetch=len(scalars),
            grid=grid,
            in_specs=in_specs or [whole] * len(args),
            out_specs=out_specs or [whole] * len(outs),
            scratch_shapes=list(scratch),
        ),
        compiler_params=pltpu.CompilerParams(
            dimension_semantics=("arbitrary",) * len(grid), vmem_limit_bytes=int(vmem * MIB)
        ),
        input_output_aliases=aliases or {},
        cost_estimate=pl.CostEstimate(flops=flops, bytes_accessed=moved, transcendentals=exps),
    )(*scalars, *args)


def shift(x, axis, count, t):
    return lax.ppermute(x, axis, [(i, (i + t) % count) for i in range(count)])


def shards(
    lengths,
    group_of,
    query_pre,
    key_pre,
    value_pre,
    query_new,
    key_new,
    value_new,
    hidden_new,
    out_weight,
    norm_gain,
    gate_weight,
    up_weight,
    down_weight,
):
    n = lax.axis_size("seq")
    count = lax.axis_size("grp")
    seq = lax.axis_index("seq").astype(jnp.int32)
    group = lax.axis_index("grp").astype(jnp.int32)
    tokens = query_pre.shape[0]
    reqs = query_new.shape[0]
    kv_heads = key_pre.shape[1] // HD
    shard_width = query_new.shape[1]
    shard_heads = shard_width // HD
    columns = out_weight.shape[1]
    shape = jax.ShapeDtypeStruct
    vmem = pl.BlockSpec(memory_space=pltpu.VMEM)
    anywhere = pl.BlockSpec(memory_space=pl.ANY)
    dma = pltpu.SemaphoreType.DMA
    facts = jnp.concatenate([jnp.stack([group, seq]), group_of, lengths])
    scalars = (facts,)

    def to_seq(x):
        return [x] + [shift(x, "seq", n, t) for t in range(1, n)]

    def to_grp(x):
        return lax.all_to_all(x, "grp", split_axis=0, concat_axis=0, tiled=True)

    def tie(x, after):
        return lax.optimization_barrier((x, after))[0]

    def up(x, step, after):
        return lax.ppermute(tie(x, after), "seq", [(i, i + 1) for i in range(step - 1, n - 1)])

    keys, values = [key_pre], [value_pre]

    query, own = call(
        select_kernel,
        scalars,
        (jnp.concatenate([query_new, key_new, value_new], axis=1),),
        (shape((SLOTS_R, shard_width), BF16), shape((shard_heads * SLOTS_R, 2 * HD), F32)),
        cost=(2 * 8 * reqs * shard_width, 0),
    )
    queries = to_seq(query)
    keys.append(up(keys[-1], 1, queries[1:]))
    rows = shard_heads * SLOTS_R
    partials = call(
        functools.partial(partial_kernel, n),
        scalars,
        (*queries, key_pre, value_pre),
        [shape((rows, 2 * HD), BF16)] * n,
        in_specs=[vmem] * n + [anywhere] * 2,
        scratch=[pltpu.VMEM(a.shape, BF16) for a in (key_pre, value_pre)]
        + [
            pltpu.VMEM((n, SLOTS_R, shard_width), F32),
            pltpu.VMEM((n, rows, 2 * HD), BF16),
            dma((2,)),
        ],
        cost=(4 * n * rows * tokens * HD, n * rows * tokens),
    )
    partials = [partials[0]] + [shift(partials[t], "seq", n, n - t) for t in range(1, n)]
    values.append(up(values[-1], 1, partials[1:]))
    (att,) = call(
        functools.partial(combine_kernel, n, count),
        (),
        (*partials, own),
        (shape((count, SLOTS_R, shard_width), BF16),),
        cost=(8 * n * rows * HD, n * rows),
    )
    atts = to_grp(att)

    index = jnp.arange(reqs, dtype=jnp.int32)
    same = group_of[None, :] == group_of[:, None]
    rank = jnp.sum(jnp.where(same & (index[None, :] < index[:, None]), 1, 0), axis=1)
    place = group_of * SLOTS_R + rank
    pick = (place[:, None] == jnp.arange(count * SLOTS_R, dtype=jnp.int32)[None, :]).astype(BF16)
    steps = 8
    depth = shard_width // steps
    (proj,) = call(
        functools.partial(project_kernel, count),
        (),
        (pick, atts, out_weight),
        (shape((reqs, columns), BF16),),
        in_specs=[vmem, vmem, anywhere],
        scratch=(
            pltpu.VMEM((steps, depth, columns), BF16),
            pltpu.VMEM((steps, reqs, depth), BF16),
            dma((steps,)),
        ),
        cost=(2 * reqs * shard_width * columns, 0),
        vmem=STREAM + 3,
    )
    projs = to_seq(proj)
    if n > 2:
        keys.append(up(keys[-1], 2, (projs[1:], values[1])))

    hidden_shard = gate_weight.shape[1]
    width = hidden_shard // count
    resid, terms = call(
        functools.partial(gate_up_kernel, n, count),
        (),
        (*projs, hidden_new, norm_gain.reshape(1, -1), gate_weight, up_weight),
        [shape((reqs, columns), F32), shape((count, reqs, 2 * width + HD), BF16)],
        in_specs=[vmem] * (n + 2) + [anywhere] * 2,
        scratch=(
            pltpu.VMEM(gate_weight.shape, BF16),
            pltpu.VMEM(up_weight.shape, BF16),
            dma((2 * count,)),
        ),
        cost=(4 * reqs * columns * hidden_shard, 0),
        vmem=STREAM,
    )
    if n > 2:
        values.append(up(values[-1], 2, terms))
    terms = tie(to_grp(terms), keys[-1])
    (hidden,) = call(
        functools.partial(hidden_kernel, count, columns * count),
        (),
        (terms,),
        (shape((count, reqs, width), BF16),),
        cost=(8 * count * reqs * width, reqs * width),
    )
    if n > 3:
        keys.append(up(keys[-1], 3, (values[-1], hidden)))
    hiddens = to_grp(hidden)
    share = columns // n
    downs = call(
        functools.partial(down_kernel, count, n),
        scalars,
        (hiddens, down_weight),
        [shape((reqs, share), F32)] * n,
        in_specs=[vmem, anywhere],
        scratch=(pltpu.VMEM((count, width, columns), BF16), dma((count,))),
        cost=(2 * reqs * columns * hidden_shard, 0),
        vmem=STREAM,
    )
    total = lax.dynamic_slice_in_dim(resid, seq * share, share, 1) + downs[0]
    arrived = [shift(downs[t], "seq", n, t) for t in range(1, n)]
    for part in arrived:
        total = total + part
    decode_hidden = total.astype(BF16)
    for step in range(len(values), n):
        if step == len(keys):
            keys.append(up(keys[-1], step, values[-1]))
        values.append(up(values[-1], step, (keys[-1], downs)))

    first = jnp.sum(jnp.where(same & (index[None, :] < index[:, None]), lengths[None, :], 0), axis=1)
    row_first = seq * tokens
    meets = (group_of == group) & (first + lengths > row_first) & (first < row_first + tokens)
    lowest = jnp.min(jnp.where(meets, first, row_first + tokens))
    scalars = (jnp.concatenate([facts, (seq - lax.div(lowest, tokens) + 1)[None]]),)
    kv_step = 2
    wide_block = pl.BlockSpec((tokens, kv_step * Q_PER_KV * HD), lambda h, *_: (0, h))
    head_block = pl.BlockSpec((tokens, kv_step * HD), lambda h, *_: (0, h))
    (prefill,) = call(
        functools.partial(prefill_kernel, n, kv_step),
        scalars,
        (query_pre, *keys, *values),
        (shape(query_pre.shape, BF16),),
        grid=(kv_heads // kv_step,),
        in_specs=[wide_block] + [head_block] * (2 * n),
        out_specs=[wide_block],
        scratch=[
            pltpu.VMEM((tokens, n * tokens), F32),
            pltpu.VMEM((kv_step, n * tokens, 2 * HD), BF16),
        ]
        + [pltpu.VMEM((tokens, n * tokens), F32)] * 2
        + [pltpu.VMEM((tokens, n * tokens), BF16)] * 2,
        cost=(8 * n * tokens * query_pre.size, n * tokens * query_pre.size // HD),
        vmem=STREAM + 3,
    )
    return (prefill, decode_hidden)


def solution(mesh):
    return jax.shard_map(
        shards,
        mesh=mesh,
        in_specs=(
            P(),
            P(),
            P(("grp", "seq"), None),
            P(("grp", "seq"), None),
            P(("grp", "seq"), None),
            P(None, "seq"),
            P(None, "seq"),
            P(None, "seq"),
            P(None, "grp"),
            P("seq", "grp"),
            P("grp"),
            P("grp", "seq"),
            P("grp", "seq"),
            P("seq", "grp"),
        ),
        out_specs=(P(("grp", "seq"), None), P(None, ("grp", "seq"))),
        check_vma=False,
    )
```

```python
import functools
import math

import jax
import jax.numpy as jnp
from jax import lax
from jax.experimental import pallas as pl
from jax.experimental.pallas import tpu as pltpu
from jax.sharding import PartitionSpec as P

HD = 128
Q_PER_KV = 8
MAX_IN_GROUP = 3
SLOTS_R = 4
NEGATIVE = -1e30
LOG2E = 1.4426950408889634
MIB = 1 << 20
STREAM = 57

F32 = jnp.float32
BF16 = jnp.bfloat16


def dot(a, b):
    return jnp.dot(a, b, preferred_element_type=F32)


def dot_t(a, b):
    return lax.dot_general(a, b, (((1,), (1,)), ((), ())), preferred_element_type=F32)


def plan(facts):
    group = facts[0]
    reqs = (facts.shape[0] - 2) // 2
    ids = [jnp.int32(-1)] * MAX_IN_GROUP
    first = [jnp.int32(0)] * MAX_IN_GROUP
    end = [jnp.int32(0)] * MAX_IN_GROUP
    count = jnp.int32(0)
    used = jnp.int32(0)
    for r in range(reqs):
        mine = facts[2 + r] == group
        length = facts[2 + reqs + r]
        for k in range(MAX_IN_GROUP):
            here = mine & (count == k)
            ids[k] = jnp.where(here, r, ids[k])
            first[k] = jnp.where(here, used, first[k])
            end[k] = jnp.where(here, used + length, end[k])
        count = count + jnp.where(mine, 1, 0)
        used = used + jnp.where(mine, length, 0)
    return ids, first, end


def pick_rows(ids, rows, columns):
    row = lax.broadcasted_iota(jnp.int32, (rows, columns), 0)
    column = lax.broadcasted_iota(jnp.int32, (rows, columns), 1)
    target = jnp.full((rows, columns), -1, jnp.int32)
    for k in range(MAX_IN_GROUP):
        target = jnp.where(row == k, ids[k], target)
    return jnp.where(column == target, 1.0, 0.0).astype(BF16)


def split3(x):
    hi = x.astype(BF16)
    rest = x - hi.astype(F32)
    mid = rest.astype(BF16)
    low = (rest - mid.astype(F32)).astype(BF16)
    return hi, mid, low


def by_head(array, group):
    heads = array.shape[1] // HD * group
    return jnp.concatenate([array[:, (h // group) * HD :][:, :HD] for h in range(heads)], axis=0)


def spread(x, lane):
    hi, mid, low = split3(jnp.broadcast_to(x, x.shape[:-1] + (HD,)))
    return jnp.where(
        lane < 32, hi.astype(F32), jnp.where(lane < 64, mid.astype(F32), low.astype(F32))
    ).astype(BF16)


def gathered(stats):
    return stats[..., 0:1] + stats[..., 32:33] + stats[..., 64:65]


def select_kernel(facts, new_ref, query_ref, own_ref):
    ids, _, _ = plan(facts)
    width = query_ref.shape[1]
    kv_width = (new_ref.shape[1] - width) // 2
    new = dot(pick_rows(ids, 8, new_ref.shape[0]), new_ref[...])[:SLOTS_R]
    query_ref[...] = new[:, :width].astype(BF16)
    keys = by_head(new[:, width : width + kv_width], Q_PER_KV)
    values = by_head(new[:, width + kv_width :], Q_PER_KV)
    score = jnp.sum(by_head(new[:, :width], 1) * keys, axis=1, keepdims=True)
    own_ref[:, :HD] = values
    own_ref[:, HD:] = jnp.broadcast_to(score * (1.0 / math.sqrt(HD)), values.shape)


def partial_kernel(n, facts, *refs):
    queries, cache_ref, outs = refs[:n], refs[n], refs[n + 1 : 2 * n + 1]
    query_ref, out_ref = refs[2 * n + 1 :]
    _, first, end = plan(facts)
    tokens = cache_ref.shape[0] // 2
    kv_per = queries[0].shape[1] // (HD * Q_PER_KV)
    rows = Q_PER_KV * SLOTS_R
    slot = facts[1] * tokens + lax.broadcasted_iota(jnp.int32, (rows, tokens), 1)
    rank = lax.broadcasted_iota(jnp.int32, (rows, tokens), 0) & (SLOTS_R - 1)
    low = jnp.zeros((rows, tokens), jnp.int32)
    high = jnp.zeros((rows, tokens), jnp.int32)
    for k in range(MAX_IN_GROUP):
        low = jnp.where(rank == k, first[k], low)
        high = jnp.where(rank == k, end[k], high)
    allowed = (slot >= low) & (slot < high)
    lane = lax.broadcasted_iota(jnp.int32, (rows, HD), 1)
    scale = 1.0 / math.sqrt(HD)
    for t in range(n):
        query_ref[t] = queries[t][...].astype(F32)

    def head(j, carry):
        t = j // kv_per
        i = j - t * kv_per
        shard = lax.rem(facts[1] - t + n, n)
        columns = pl.ds(pl.multiple_of((shard * kv_per + i) * HD, HD), HD)
        width = Q_PER_KV * HD
        query = query_ref[t, :, pl.ds(pl.multiple_of(i * width, width), width)]
        scores = dot_t(by_head(query, 1).astype(BF16), cache_ref[:tokens, columns]) * scale
        scores = jnp.where(allowed, scores, NEGATIVE)
        top = jnp.max(scores, axis=1, keepdims=True)
        weights = jnp.where(allowed, jnp.exp(scores - top), 0.0)
        total = jnp.sum(weights, axis=1, keepdims=True)
        some = total > 0.0
        mixed = dot(weights.astype(BF16), cache_ref[tokens:, columns]) / jnp.where(some, total, 1.0)
        level = jnp.where(some, top + jnp.log(jnp.where(some, total, 1.0)), NEGATIVE)
        out_ref[t, pl.ds(pl.multiple_of(i * rows, rows), rows), :] = jnp.concatenate(
            [mixed.astype(BF16), spread(level, lane)], axis=1
        )
        return carry

    lax.fori_loop(0, n * kv_per, head, 0)
    for t in range(n):
        outs[t][...] = out_ref[t]


def combine_kernel(n, count, *refs):
    parts, own_ref, out_ref = refs[:n], refs[n], refs[n + 1]
    own_value = own_ref[:, :HD]
    own_score = own_ref[:, HD : HD + 1]
    mixes = []
    levels = []
    top = own_score
    for t in range(n):
        part = parts[t][...].astype(F32)
        stats = part[:, HD:]
        level = stats[:, 0:1] + stats[:, 32:33] + stats[:, 64:65]
        mixes.append(part[:, :HD])
        levels.append(level)
        top = jnp.maximum(top, level)
    own_weight = jnp.exp(own_score - top)
    total = own_weight
    mixed = own_weight.astype(BF16).astype(F32) * own_value
    for t in range(n):
        weight = jnp.exp(levels[t] - top)
        total = total + weight
        mixed = mixed + weight * mixes[t]
    result = mixed / total
    for h in range(out_ref.shape[2] // HD):
        head = result[h * SLOTS_R : (h + 1) * SLOTS_R].astype(BF16)
        for g in range(count):
            out_ref[g, :, h * HD : (h + 1) * HD] = head


def start_all(pairs, sems):
    copies = [
        pltpu.make_async_copy(source, target, sems.at[i]) for i, (source, target) in enumerate(pairs)
    ]
    for copy in copies:
        copy.start()
    return copies


def project_kernel(count, pick_ref, parts_ref, weight_ref, out_ref, buffer_ref, att_ref, sems):
    steps, _, depth = att_ref.shape

    def copy(j):
        rows = pl.ds(pl.multiple_of(j * depth, depth), depth)
        return pltpu.make_async_copy(weight_ref.at[rows], buffer_ref.at[j], sems.at[j])

    for j in range(steps):
        copy(j).start()
    stacked = jnp.concatenate([parts_ref[g].astype(F32) for g in range(count)], axis=0)
    att = dot(pick_ref[...], stacked.astype(BF16)).astype(BF16)
    for j in range(steps):
        att_ref[j] = att[:, j * depth : (j + 1) * depth]

    def block(j, total):
        copy(j).wait()
        return total + dot(att_ref[j], buffer_ref[j])

    total = lax.fori_loop(0, steps, block, jnp.zeros(out_ref.shape, F32))
    out_ref[...] = total.astype(out_ref.dtype)


def gate_up_kernel(n, count, *refs):
    parts = refs[:n]
    hidden_ref, gain_ref, gate_ref, up_ref, resid_ref, send_ref, gates_ref, ups_ref, sems = refs[n:]
    width = gate_ref.shape[1] // count
    blocks = [pl.ds(g * width, width) for g in range(count)]
    pairs = []
    for b in blocks:
        pairs.append((gate_ref.at[:, b], gates_ref.at[:, b]))
        pairs.append((up_ref.at[:, b], ups_ref.at[:, b]))
    copies = start_all(pairs, sems)
    resid = parts[0][...].astype(F32)
    for part in parts[1:]:
        resid = resid + part[...].astype(F32)
    resid = resid + hidden_ref[...].astype(F32)
    resid_ref[...] = resid
    scaled = (resid * gain_ref[...].astype(F32)).astype(BF16)
    squares = jnp.sum(resid * resid, axis=1, keepdims=True)
    rows = resid.shape[0]
    hi, mid, low = split3(jnp.broadcast_to(squares, (rows, HD)))
    lane = lax.broadcasted_iota(jnp.int32, (rows, HD), 1)
    stats = jnp.where(
        lane < 32, hi.astype(F32), jnp.where(lane < 64, mid.astype(F32), low.astype(F32))
    ).astype(BF16)
    for g in range(count):
        send_ref[g, :, 2 * width :] = stats
    for g in range(count):
        copies[2 * g].wait()
        send_ref[g, :, :width] = dot(scaled, gates_ref[:, blocks[g]]).astype(BF16)
        copies[2 * g + 1].wait()
        send_ref[g, :, width : 2 * width] = dot(scaled, ups_ref[:, blocks[g]]).astype(BF16)


def hidden_kernel(count, features, parts_ref, out_ref):
    width = out_ref.shape[2]
    total = parts_ref[0].astype(F32)
    for g in range(1, count):
        total = total + parts_ref[g].astype(F32)
    stats = total[:, 2 * width :]
    squares = stats[:, 0:1] + stats[:, 32:33] + stats[:, 64:65]
    inverse = lax.rsqrt(squares / features + 1e-05)
    gate = total[:, :width] * inverse
    upper = total[:, width : 2 * width] * inverse
    hidden = (gate / (1.0 + jnp.exp(-gate)) * upper).astype(BF16)
    for g in range(count):
        out_ref[g] = hidden


def down_kernel(count, n, facts, parts_ref, weight_ref, *refs):
    sends, buffer_ref, sems = refs[:n], refs[n], refs[n + 1]
    depth = buffer_ref.shape[1]
    width = sends[0].shape[1]

    def copy(g):
        rows = pl.ds(pl.multiple_of(g * depth, depth), depth)
        return pltpu.make_async_copy(weight_ref.at[rows], buffer_ref.at[g], sems.at[g])

    for g in range(count):
        copy(g).start()

    def block(g, total):
        copy(g).wait()
        return total + dot(parts_ref[g], buffer_ref[g])

    shape = (sends[0].shape[0], weight_ref.shape[1])
    total = lax.fori_loop(0, count, block, jnp.zeros(shape, F32))
    for own in range(n):

        @pl.when(facts[1] == own)
        def _():
            for t in range(n):
                target = (own + t) % n
                sends[t][...] = total[:, target * width : (target + 1) * width]


def row_facts(facts, tokens):
    _, first, end = plan(facts)
    return facts[1] * tokens, facts[facts.shape[0] - 1], first, end


def live_rows(row_first, first, end, tokens):
    row = row_first + lax.broadcasted_iota(jnp.int32, (tokens, HD), 0)
    live = row < 0
    for k in range(MAX_IN_GROUP):
        live = live | ((row >= first[k]) & (row < end[k]))
    return live


def store_bias(bias_ref, row_first, first, end, pieces):
    tokens = bias_ref.shape[0]
    row = row_first + lax.broadcasted_iota(jnp.int32, (tokens, tokens), 0)
    column = lax.broadcasted_iota(jnp.int32, (tokens, tokens), 1)
    low = jnp.full((tokens, tokens), 1 << 30, jnp.int32)
    for k in range(MAX_IN_GROUP):
        low = jnp.where((row >= first[k]) & (row < end[k]), first[k], low)
    for place, t in enumerate(pieces):
        slot = row_first - t * tokens + column
        bias_ref[:, place * tokens : (place + 1) * tokens] = jnp.where(
            (slot >= low) & (slot <= row), 0.0, NEGATIVE
        )


EXP2 = LOG2E / math.sqrt(HD)


def inverse_of(x):
    guess = pl.reciprocal(x, approx=True)
    return guess * (2.0 - x * guess)


def interleave(*tasks):
    order = sorted(
        ((k + 0.5) / len(task), which, step)
        for which, task in enumerate(tasks)
        for k, step in enumerate(range(len(task)))
    )
    for _, which, step in order:
        tasks[which][step]()


def prefill_kernel(n, facts, *refs):
    query_hbm, own, pieces, out_hbm = refs[0], refs[1:3], refs[3 : 2 + n], refs[2 + n]
    query_ref, key_ref, value_ref, wide_ref, bias_ref, out_ref = refs[3 + n : 9 + n]
    scores, weights, (query_sems, piece_sems, out_sems) = (
        refs[9 + n : 11 + n],
        refs[11 + n : 13 + n],
        refs[13 + n :],
    )
    tokens = query_ref.shape[1]
    kv_heads = query_ref.shape[0]
    pairs = Q_PER_KV // 2
    row_first, needed, first, end = row_facts(facts, tokens)

    def columns(kv):
        width = Q_PER_KV * HD
        return pl.ds(pl.multiple_of(kv * width, width), width)

    def query_copy(kv):
        return pltpu.make_async_copy(
            query_hbm.at[:, columns(kv)], query_ref.at[kv], query_sems.at[kv]
        )

    def out_copy(kv):
        return pltpu.make_async_copy(out_ref.at[kv], out_hbm.at[:, columns(kv)], out_sems.at[kv])

    @pl.when(needed == 0)
    def _():
        out_ref[...] = jnp.zeros_like(out_ref)
        for kv in range(kv_heads):
            out_copy(kv).start()
        for kv in range(kv_heads):
            out_copy(kv).wait()

    def run(count, lone):
        slots = count * tokens
        chunk = 64
        copies = []
        for t in range(count):
            for part, target in enumerate((key_ref, value_ref)):
                source = own[part] if t == 0 else pieces[t - 1].at[pl.ds(part * tokens, tokens)]
                copies.append(
                    pltpu.make_async_copy(source, target.at[t], piece_sems.at[part, t])
                )
        for copy in copies:
            copy.start()
        for kv in range(kv_heads):
            query_copy(kv).start()
        store_bias(bias_ref, row_first, first, end, range(count))
        live = None if lone else live_rows(row_first, first, end, tokens)
        for copy in copies:
            copy.wait()

        def widen(kv, carry):
            lanes = pl.ds(pl.multiple_of(kv * HD, HD), HD)
            for t in range(count):
                rows = slice(t * tokens, (t + 1) * tokens)
                wide_ref[kv, rows, :HD] = value_ref[t, :, lanes]
                wide_ref[kv, rows, HD:] = jnp.ones((tokens, HD), BF16)
            return carry

        lax.fori_loop(0, kv_heads, widen, 0)

        def score_steps(pair, slot):
            kv = pair // pairs
            at = pl.multiple_of((pair - kv * pairs) * (2 * HD), 2 * HD)
            lanes = pl.ds(pl.multiple_of(kv * HD, HD), HD)

            def step(t):
                query = jnp.concatenate(
                    [query_ref[kv, :, pl.ds(at + i * HD, HD)] for i in range(2)], axis=0
                )
                scores[slot][:, t * tokens : (t + 1) * tokens] = dot_t(
                    query, key_ref[t, :, lanes]
                )

            return [functools.partial(step, t) for t in range(count)]

        def weight_steps(slot):
            tops = {}

            def part(at, t):
                piece = slice(t * tokens, (t + 1) * tokens)
                score = scores[slot][at : at + chunk, piece]
                if lone and t > 0:
                    return score
                row = at % tokens
                return score + bias_ref[row : row + chunk, piece]

            def top_step(at):
                most = part(at, 0)
                for t in range(1, count):
                    most = jnp.maximum(most, part(at, t))
                tops[at] = jnp.max(most, axis=1, keepdims=True)

            def weight_step(at):
                top = tops.pop(at)
                for t in range(count):
                    weights[slot][at : at + chunk, t * tokens : (t + 1) * tokens] = jnp.exp2(
                        (part(at, t) - top) * EXP2
                    ).astype(BF16)

            starts = list(range(0, 2 * tokens, chunk))
            steps = [functools.partial(top_step, at) for at in starts[:2]]
            for i, at in enumerate(starts):
                steps.append(functools.partial(weight_step, at))
                if i + 2 < len(starts):
                    steps.append(functools.partial(top_step, starts[i + 2]))
            return steps

        def value_steps(pair, slot):
            kv = pair // pairs
            at = pl.multiple_of((pair - kv * pairs) * (2 * HD), 2 * HD)

            def step():
                mixed = dot(weights[slot][:, :slots], wide_ref[kv, :slots])
                result = mixed[:, :HD] * inverse_of(mixed[:, HD:])
                for i in range(2):
                    head = result[i * tokens : (i + 1) * tokens]
                    if not lone:
                        head = jnp.where(live, head, 0.0)
                    out_ref[kv, :, pl.ds(at + i * HD, HD)] = head.astype(BF16)

            return [step]

        last = kv_heads * pairs - 1
        query_copy(0).wait()
        interleave(score_steps(jnp.int32(0), 0))
        interleave(score_steps(jnp.int32(1), 1), weight_steps(0))

        def kv_step(kv, carry):
            @pl.when(kv + 1 < kv_heads)
            def _():
                query_copy(kv + 1).wait()

            def two_pairs(j, inner):
                for slot in range(2):
                    pair = kv * pairs + 2 * j + slot
                    interleave(
                        score_steps(jnp.minimum(pair + 2, last), slot),
                        weight_steps(1 - slot),
                        value_steps(pair, slot),
                    )
                return inner

            lax.fori_loop(0, pairs // 2, two_pairs, 0)
            out_copy(kv).start()
            return carry

        lax.fori_loop(0, kv_heads, kv_step, 0)
        for kv in range(kv_heads):
            out_copy(kv).wait()

    lone = needed < 0
    for k in range(MAX_IN_GROUP):
        lone = lone | (
            (first[k] <= row_first - (needed - 1) * tokens) & (end[k] >= row_first + tokens)
        )
    before = 0
    for count in sorted({c for c in (1, 2, 3, n) if c <= n}):
        here = (needed > before) & (needed <= count)
        exact = (needed == count) & lone
        before = count

        @pl.when(exact)
        def _():
            run(count, True)

        @pl.when(here & jnp.logical_not(exact))
        def _():
            run(count, False)


def call(body, scalars, args, outs, *, grid=None, in_specs=None, out_specs=None, scratch=(), cost, vmem=6, aliases=None):
    whole = pl.BlockSpec(memory_space=pltpu.VMEM)
    if grid is None:
        grid = (1,)
    flops, exps = cost
    moved = sum(a.size * a.dtype.itemsize for a in args) + sum(
        o.size * o.dtype.itemsize for o in outs
    )
    return pl.pallas_call(
        body,
        out_shape=list(outs),
        grid_spec=pltpu.PrefetchScalarGridSpec(
            num_scalar_prefetch=len(scalars),
            grid=grid,
            in_specs=in_specs or [whole] * len(args),
            out_specs=out_specs or [whole] * len(outs),
            scratch_shapes=list(scratch),
        ),
        compiler_params=pltpu.CompilerParams(
            dimension_semantics=("arbitrary",) * len(grid), vmem_limit_bytes=int(vmem * MIB)
        ),
        input_output_aliases=aliases or {},
        cost_estimate=pl.CostEstimate(flops=flops, bytes_accessed=moved, transcendentals=exps),
    )(*scalars, *args)


def shift(x, axis, count, t):
    return lax.ppermute(x, axis, [(i, (i + t) % count) for i in range(count)])


def shards(
    lengths,
    group_of,
    query_pre,
    key_pre,
    value_pre,
    query_new,
    key_new,
    value_new,
    hidden_new,
    out_weight,
    norm_gain,
    gate_weight,
    up_weight,
    down_weight,
):
    n = lax.axis_size("seq")
    count = lax.axis_size("grp")
    seq = lax.axis_index("seq").astype(jnp.int32)
    group = lax.axis_index("grp").astype(jnp.int32)
    tokens = query_pre.shape[0]
    reqs = query_new.shape[0]
    kv_heads = key_pre.shape[1] // HD
    shard_width = query_new.shape[1]
    shard_heads = shard_width // HD
    columns = out_weight.shape[1]
    shape = jax.ShapeDtypeStruct
    vmem = pl.BlockSpec(memory_space=pltpu.VMEM)
    anywhere = pl.BlockSpec(memory_space=pl.ANY)
    dma = pltpu.SemaphoreType.DMA
    facts = jnp.concatenate([jnp.stack([group, seq]), group_of, lengths])
    scalars = (facts,)

    def to_seq(x):
        return [x] + [shift(x, "seq", n, t) for t in range(1, n)]

    def to_grp(x):
        return lax.all_to_all(x, "grp", split_axis=0, concat_axis=0, tiled=True)

    def tie(x, after):
        return lax.optimization_barrier((x, after))[0]

    def up(x, step, after):
        return lax.ppermute(tie(x, after), "seq", [(i, i + 1) for i in range(step - 1, n - 1)])

    pieces = [jnp.concatenate([key_pre, value_pre], axis=0)]

    query, own = call(
        select_kernel,
        scalars,
        (jnp.concatenate([query_new, key_new, value_new], axis=1),),
        (shape((SLOTS_R, shard_width), BF16), shape((shard_heads * SLOTS_R, 2 * HD), F32)),
        cost=(2 * 8 * reqs * shard_width, 0),
    )
    queries = to_seq(query)
    rows = shard_heads * SLOTS_R
    partials = call(
        functools.partial(partial_kernel, n),
        scalars,
        (*queries, pieces[0]),
        [shape((rows, 2 * HD), BF16)] * n,
        scratch=(
            pltpu.VMEM((n, SLOTS_R, shard_width), F32),
            pltpu.VMEM((n, rows, 2 * HD), BF16),
        ),
        cost=(4 * n * rows * tokens * HD, n * rows * tokens),
    )
    partials = [partials[0]] + [shift(partials[t], "seq", n, n - t) for t in range(1, n)]
    pieces.append(up(pieces[-1], 1, partials[1:]))
    (att,) = call(
        functools.partial(combine_kernel, n, count),
        (),
        (*partials, own),
        (shape((count, SLOTS_R, shard_width), BF16),),
        cost=(8 * n * rows * HD, n * rows),
    )
    atts = to_grp(att)

    index = jnp.arange(reqs, dtype=jnp.int32)
    groups = tie(group_of, att)
    same = groups[None, :] == groups[:, None]
    rank = jnp.sum(jnp.where(same & (index[None, :] < index[:, None]), 1, 0), axis=1)
    place = groups * SLOTS_R + rank
    pick = (place[:, None] == jnp.arange(count * SLOTS_R, dtype=jnp.int32)[None, :]).astype(BF16)
    steps = 8
    depth = shard_width // steps
    (proj,) = call(
        functools.partial(project_kernel, count),
        (),
        (pick, atts, out_weight),
        (shape((reqs, columns), BF16),),
        in_specs=[vmem, vmem, anywhere],
        scratch=(
            pltpu.VMEM((steps, depth, columns), BF16),
            pltpu.VMEM((steps, reqs, depth), BF16),
            dma((steps,)),
        ),
        cost=(2 * reqs * shard_width * columns, 0),
        vmem=STREAM + 3,
    )
    projs = to_seq(proj)
    if n > 2:
        pieces.append(up(pieces[-1], 2, projs[1:]))

    hidden_shard = gate_weight.shape[1]
    width = hidden_shard // count
    resid, terms = call(
        functools.partial(gate_up_kernel, n, count),
        (),
        (*projs, hidden_new, norm_gain.reshape(1, -1), gate_weight, up_weight),
        [shape((reqs, columns), F32), shape((count, reqs, 2 * width + HD), BF16)],
        in_specs=[vmem] * (n + 2) + [anywhere] * 2,
        scratch=(
            pltpu.VMEM(gate_weight.shape, BF16),
            pltpu.VMEM(up_weight.shape, BF16),
            dma((2 * count,)),
        ),
        cost=(4 * reqs * columns * hidden_shard, 0),
        vmem=STREAM,
    )
    terms = to_grp(terms)
    (hidden,) = call(
        functools.partial(hidden_kernel, count, columns * count),
        (),
        (terms,),
        (shape((count, reqs, width), BF16),),
        cost=(8 * count * reqs * width, reqs * width),
    )
    hiddens = to_grp(hidden)
    if n > 3:
        pieces.append(up(pieces[-1], 3, hiddens))
    share = columns // n
    downs = call(
        functools.partial(down_kernel, count, n),
        scalars,
        (hiddens, down_weight),
        [shape((reqs, share), F32)] * n,
        in_specs=[vmem, anywhere],
        scratch=(pltpu.VMEM((count, width, columns), BF16), dma((count,))),
        cost=(2 * reqs * columns * hidden_shard, 0),
        vmem=STREAM,
    )
    total = lax.dynamic_slice_in_dim(resid, seq * share, share, 1) + downs[0]
    arrived = [shift(downs[t], "seq", n, t) for t in range(1, n)]
    for part in arrived:
        total = total + part
    decode_hidden = total.astype(BF16)
    for step in range(len(pieces), n):
        pieces.append(up(pieces[-1], step, pieces[-1]))

    first = jnp.sum(jnp.where(same & (index[None, :] < index[:, None]), lengths[None, :], 0), axis=1)
    row_first = seq * tokens
    meets = (group_of == group) & (first + lengths > row_first) & (first < row_first + tokens)
    lowest = jnp.min(jnp.where(meets, first, row_first + tokens))
    scalars = (jnp.concatenate([facts, (seq - lax.div(lowest, tokens) + 1)[None]]),)
    wide = Q_PER_KV * HD
    (prefill,) = call(
        functools.partial(prefill_kernel, n),
        scalars,
        (query_pre, key_pre, value_pre, *pieces[1:]),
        (shape(query_pre.shape, BF16),),
        in_specs=[anywhere] * (2 + n),
        out_specs=[anywhere],
        scratch=[
            pltpu.VMEM((kv_heads, tokens, wide), BF16),
            pltpu.VMEM((n, tokens, kv_heads * HD), BF16),
            pltpu.VMEM((n, tokens, kv_heads * HD), BF16),
            pltpu.VMEM((kv_heads, n * tokens, 2 * HD), BF16),
            pltpu.VMEM((tokens, n * tokens), F32),
            pltpu.VMEM((kv_heads, tokens, wide), BF16),
        ]
        + [pltpu.VMEM((2 * tokens, n * tokens), F32)] * 2
        + [pltpu.VMEM((2 * tokens, n * tokens), BF16)] * 2
        + [dma((kv_heads,)), dma((2, n)), dma((kv_heads,))],
        cost=(8 * n * tokens * query_pre.size, n * tokens * query_pre.size // HD),
        vmem=STREAM + 3,
    )
    return (prefill, decode_hidden)


def solution(mesh):
    return jax.shard_map(
        shards,
        mesh=mesh,
        in_specs=(
            P(),
            P(),
            P(("grp", "seq"), None),
            P(("grp", "seq"), None),
            P(("grp", "seq"), None),
            P(None, "seq"),
            P(None, "seq"),
            P(None, "seq"),
            P(None, "grp"),
            P("seq", "grp"),
            P("grp"),
            P("grp", "seq"),
            P("grp", "seq"),
            P("seq", "grp"),
        ),
        out_specs=(P(("grp", "seq"), None), P(None, ("grp", "seq"))),
        check_vma=False,
    )
```

```python
import functools
import math

import jax
import jax.numpy as jnp
from jax import lax
from jax.experimental import pallas as pl
from jax.experimental.pallas import tpu as pltpu
from jax.sharding import PartitionSpec as P

HD = 128
Q_PER_KV = 8
MAX_IN_GROUP = 3
SLOTS_R = 4
NEGATIVE = -1e30
LOG2E = 1.4426950408889634
MIB = 1 << 20
STREAM = 57

F32 = jnp.float32
BF16 = jnp.bfloat16


def dot(a, b):
    return jnp.dot(a, b, preferred_element_type=F32)


def dot_t(a, b):
    return lax.dot_general(a, b, (((1,), (1,)), ((), ())), preferred_element_type=F32)


def plan(facts):
    group = facts[0]
    reqs = (facts.shape[0] - 2) // 2
    ids = [jnp.int32(-1)] * MAX_IN_GROUP
    first = [jnp.int32(0)] * MAX_IN_GROUP
    end = [jnp.int32(0)] * MAX_IN_GROUP
    count = jnp.int32(0)
    used = jnp.int32(0)
    for r in range(reqs):
        mine = facts[2 + r] == group
        length = facts[2 + reqs + r]
        for k in range(MAX_IN_GROUP):
            here = mine & (count == k)
            ids[k] = jnp.where(here, r, ids[k])
            first[k] = jnp.where(here, used, first[k])
            end[k] = jnp.where(here, used + length, end[k])
        count = count + jnp.where(mine, 1, 0)
        used = used + jnp.where(mine, length, 0)
    return ids, first, end


def pick_rows(ids, rows, columns):
    row = lax.broadcasted_iota(jnp.int32, (rows, columns), 0)
    column = lax.broadcasted_iota(jnp.int32, (rows, columns), 1)
    target = jnp.full((rows, columns), -1, jnp.int32)
    for k in range(MAX_IN_GROUP):
        target = jnp.where(row == k, ids[k], target)
    return jnp.where(column == target, 1.0, 0.0).astype(BF16)


def split3(x):
    hi = x.astype(BF16)
    rest = x - hi.astype(F32)
    mid = rest.astype(BF16)
    low = (rest - mid.astype(F32)).astype(BF16)
    return hi, mid, low


def by_head(array, group):
    heads = array.shape[1] // HD * group
    return jnp.concatenate([array[:, (h // group) * HD :][:, :HD] for h in range(heads)], axis=0)


def spread(x, lane):
    hi, mid, low = split3(jnp.broadcast_to(x, x.shape[:-1] + (HD,)))
    return jnp.where(
        lane < 32, hi.astype(F32), jnp.where(lane < 64, mid.astype(F32), low.astype(F32))
    ).astype(BF16)


def gathered(stats):
    return stats[..., 0:1] + stats[..., 32:33] + stats[..., 64:65]


def select_kernel(facts, new_ref, query_ref, own_ref):
    ids, _, _ = plan(facts)
    width = query_ref.shape[1]
    kv_width = (new_ref.shape[1] - width) // 2
    new = dot(pick_rows(ids, 8, new_ref.shape[0]), new_ref[...])[:SLOTS_R]
    query_ref[...] = new[:, :width].astype(BF16)
    keys = by_head(new[:, width : width + kv_width], Q_PER_KV)
    values = by_head(new[:, width + kv_width :], Q_PER_KV)
    score = jnp.sum(by_head(new[:, :width], 1) * keys, axis=1, keepdims=True)
    own_ref[:, :HD] = values
    own_ref[:, HD:] = jnp.broadcast_to(score * (1.0 / math.sqrt(HD)), values.shape)


def pack_kernel(key_ref, value_ref, out_ref):
    tokens, width = key_ref.shape
    for at in range(0, width, HD):
        keys = key_ref[:, at : at + HD].astype(F32)
        out_ref[at : at + HD, :] = jnp.transpose(keys).astype(BF16)
    for at in range(0, width, tokens):
        out_ref[width + at : width + at + tokens, :] = value_ref[:, at : at + tokens]


def value_place(kv, tokens):
    side = tokens // HD
    row = pl.multiple_of(kv // side * tokens, tokens)
    return row, pl.multiple_of(lax.rem(kv, side) * HD, HD)


def partial_kernel(n, facts, *refs):
    queries, cache_ref, outs = refs[:n], refs[n], refs[n + 1 : 2 * n + 1]
    query_ref, out_ref = refs[2 * n + 1 :]
    _, first, end = plan(facts)
    kv_width, tokens = cache_ref.shape[0] // 2, cache_ref.shape[1]
    kv_per = queries[0].shape[1] // (HD * Q_PER_KV)
    rows = Q_PER_KV * SLOTS_R
    slot = facts[1] * tokens + lax.broadcasted_iota(jnp.int32, (rows, tokens), 1)
    rank = lax.broadcasted_iota(jnp.int32, (rows, tokens), 0) & (SLOTS_R - 1)
    low = jnp.zeros((rows, tokens), jnp.int32)
    high = jnp.zeros((rows, tokens), jnp.int32)
    for k in range(MAX_IN_GROUP):
        low = jnp.where(rank == k, first[k], low)
        high = jnp.where(rank == k, end[k], high)
    allowed = (slot >= low) & (slot < high)
    lane = lax.broadcasted_iota(jnp.int32, (rows, HD), 1)
    scale = 1.0 / math.sqrt(HD)
    for t in range(n):
        query_ref[t] = queries[t][...].astype(F32)

    def head(j, carry):
        t = j // kv_per
        i = j - t * kv_per
        shard = lax.rem(facts[1] - t + n, n)
        kv = shard * kv_per + i
        keys = cache_ref[pl.ds(pl.multiple_of(kv * HD, HD), HD), :]
        row, lanes = value_place(kv, tokens)
        values = cache_ref[pl.ds(kv_width + row, tokens), pl.ds(lanes, HD)]
        width = Q_PER_KV * HD
        query = query_ref[t, :, pl.ds(pl.multiple_of(i * width, width), width)]
        scores = dot(by_head(query, 1).astype(BF16), keys) * scale
        scores = jnp.where(allowed, scores, NEGATIVE)
        top = jnp.max(scores, axis=1, keepdims=True)
        weights = jnp.where(allowed, jnp.exp(scores - top), 0.0)
        total = jnp.sum(weights, axis=1, keepdims=True)
        some = total > 0.0
        mixed = dot(weights.astype(BF16), values) / jnp.where(some, total, 1.0)
        level = jnp.where(some, top + jnp.log(jnp.where(some, total, 1.0)), NEGATIVE)
        out_ref[t, pl.ds(pl.multiple_of(i * rows, rows), rows), :] = jnp.concatenate(
            [mixed.astype(BF16), spread(level, lane)], axis=1
        )
        return carry

    lax.fori_loop(0, n * kv_per, head, 0)
    for t in range(n):
        outs[t][...] = out_ref[t]


def combine_kernel(n, count, *refs):
    parts, own_ref, out_ref = refs[:n], refs[n], refs[n + 1]
    own_value = own_ref[:, :HD]
    own_score = own_ref[:, HD : HD + 1]
    mixes = []
    levels = []
    top = own_score
    for t in range(n):
        part = parts[t][...].astype(F32)
        stats = part[:, HD:]
        level = stats[:, 0:1] + stats[:, 32:33] + stats[:, 64:65]
        mixes.append(part[:, :HD])
        levels.append(level)
        top = jnp.maximum(top, level)
    own_weight = jnp.exp(own_score - top)
    total = own_weight
    mixed = own_weight.astype(BF16).astype(F32) * own_value
    for t in range(n):
        weight = jnp.exp(levels[t] - top)
        total = total + weight
        mixed = mixed + weight * mixes[t]
    result = mixed / total
    for h in range(out_ref.shape[2] // HD):
        head = result[h * SLOTS_R : (h + 1) * SLOTS_R].astype(BF16)
        for g in range(count):
            out_ref[g, :, h * HD : (h + 1) * HD] = head


def start_all(pairs, sems):
    copies = [
        pltpu.make_async_copy(source, target, sems.at[i]) for i, (source, target) in enumerate(pairs)
    ]
    for copy in copies:
        copy.start()
    return copies


def project_kernel(count, pick_ref, parts_ref, weight_ref, out_ref, buffer_ref, att_ref, sems):
    steps, _, depth = att_ref.shape

    def copy(j):
        rows = pl.ds(pl.multiple_of(j * depth, depth), depth)
        return pltpu.make_async_copy(weight_ref.at[rows], buffer_ref.at[j], sems.at[j])

    for j in range(steps):
        copy(j).start()
    stacked = jnp.concatenate([parts_ref[g].astype(F32) for g in range(count)], axis=0)
    att = dot(pick_ref[...], stacked.astype(BF16)).astype(BF16)
    for j in range(steps):
        att_ref[j] = att[:, j * depth : (j + 1) * depth]

    def block(j, total):
        copy(j).wait()
        return total + dot(att_ref[j], buffer_ref[j])

    total = lax.fori_loop(0, steps, block, jnp.zeros(out_ref.shape, F32))
    out_ref[...] = total.astype(out_ref.dtype)


def gate_up_kernel(n, count, *refs):
    parts = refs[:n]
    hidden_ref, gain_ref, gate_ref, up_ref, resid_ref, send_ref, gates_ref, ups_ref, sems = refs[n:]
    width = gate_ref.shape[1] // count
    blocks = [pl.ds(g * width, width) for g in range(count)]
    pairs = []
    for b in blocks:
        pairs.append((gate_ref.at[:, b], gates_ref.at[:, b]))
        pairs.append((up_ref.at[:, b], ups_ref.at[:, b]))
    copies = start_all(pairs, sems)
    resid = parts[0][...].astype(F32)
    for part in parts[1:]:
        resid = resid + part[...].astype(F32)
    resid = resid + hidden_ref[...].astype(F32)
    resid_ref[...] = resid
    scaled = (resid * gain_ref[...].astype(F32)).astype(BF16)
    squares = jnp.sum(resid * resid, axis=1, keepdims=True)
    rows = resid.shape[0]
    hi, mid, low = split3(jnp.broadcast_to(squares, (rows, HD)))
    lane = lax.broadcasted_iota(jnp.int32, (rows, HD), 1)
    stats = jnp.where(
        lane < 32, hi.astype(F32), jnp.where(lane < 64, mid.astype(F32), low.astype(F32))
    ).astype(BF16)
    for g in range(count):
        send_ref[g, :, 2 * width :] = stats
    for g in range(count):
        copies[2 * g].wait()
        send_ref[g, :, :width] = dot(scaled, gates_ref[:, blocks[g]]).astype(BF16)
        copies[2 * g + 1].wait()
        send_ref[g, :, width : 2 * width] = dot(scaled, ups_ref[:, blocks[g]]).astype(BF16)


def hidden_kernel(count, features, parts_ref, out_ref):
    width = out_ref.shape[2]
    total = parts_ref[0].astype(F32)
    for g in range(1, count):
        total = total + parts_ref[g].astype(F32)
    stats = total[:, 2 * width :]
    squares = stats[:, 0:1] + stats[:, 32:33] + stats[:, 64:65]
    inverse = lax.rsqrt(squares / features + 1e-05)
    gate = total[:, :width] * inverse
    upper = total[:, width : 2 * width] * inverse
    hidden = (gate / (1.0 + jnp.exp(-gate)) * upper).astype(BF16)
    for g in range(count):
        out_ref[g] = hidden


def down_kernel(count, n, facts, parts_ref, weight_ref, *refs):
    sends, buffer_ref, sems = refs[:n], refs[n], refs[n + 1]
    depth = buffer_ref.shape[1]
    width = sends[0].shape[1]

    def copy(g):
        rows = pl.ds(pl.multiple_of(g * depth, depth), depth)
        return pltpu.make_async_copy(weight_ref.at[rows], buffer_ref.at[g], sems.at[g])

    for g in range(count):
        copy(g).start()

    def block(g, total):
        copy(g).wait()
        return total + dot(parts_ref[g], buffer_ref[g])

    shape = (sends[0].shape[0], weight_ref.shape[1])
    total = lax.fori_loop(0, count, block, jnp.zeros(shape, F32))
    for own in range(n):

        @pl.when(facts[1] == own)
        def _():
            for t in range(n):
                target = (own + t) % n
                sends[t][...] = total[:, target * width : (target + 1) * width]


def row_facts(facts, tokens):
    _, first, end = plan(facts)
    return facts[1] * tokens, facts[facts.shape[0] - 1], first, end


def live_rows(row_first, first, end, tokens):
    row = row_first + lax.broadcasted_iota(jnp.int32, (tokens, HD), 0)
    live = row < 0
    for k in range(MAX_IN_GROUP):
        live = live | ((row >= first[k]) & (row < end[k]))
    return live


def store_bias(bias_ref, row_first, first, end, pieces):
    tokens = bias_ref.shape[0]
    row = row_first + lax.broadcasted_iota(jnp.int32, (tokens, tokens), 0)
    column = lax.broadcasted_iota(jnp.int32, (tokens, tokens), 1)
    low = jnp.full((tokens, tokens), 1 << 30, jnp.int32)
    for k in range(MAX_IN_GROUP):
        low = jnp.where((row >= first[k]) & (row < end[k]), first[k], low)
    for place, t in enumerate(pieces):
        slot = row_first - t * tokens + column
        bias_ref[:, place * tokens : (place + 1) * tokens] = jnp.where(
            (slot >= low) & (slot <= row), 0.0, NEGATIVE
        )


EXP2 = LOG2E / math.sqrt(HD)


def inverse_of(x):
    guess = pl.reciprocal(x, approx=True)
    return guess * (2.0 - x * guess)


def interleave(*tasks):
    order = sorted(
        ((k + 0.5) / len(task), which, step)
        for which, task in enumerate(tasks)
        for k, step in enumerate(range(len(task)))
    )
    for _, which, step in order:
        tasks[which][step]()


def prefill_kernel(n, facts, *refs):
    query_hbm, pieces, out_hbm = refs[0], refs[1 : 1 + n], refs[1 + n]
    query_ref, key_ref, value_ref, wide_ref, bias_ref, out_ref = refs[2 + n : 8 + n]
    scores, weights, (query_sems, piece_sems, out_sems) = (
        refs[8 + n : 10 + n],
        refs[10 + n : 12 + n],
        refs[12 + n :],
    )
    tokens = query_ref.shape[1]
    kv_heads = query_ref.shape[0]
    kv_width = key_ref.shape[1]
    row_first, needed, first, end = row_facts(facts, tokens)

    def columns(kv):
        width = Q_PER_KV * HD
        return pl.ds(pl.multiple_of(kv * width, width), width)

    def query_copy(kv):
        return pltpu.make_async_copy(
            query_hbm.at[:, columns(kv)], query_ref.at[kv], query_sems.at[kv]
        )

    def out_copy(kv):
        return pltpu.make_async_copy(out_ref.at[kv], out_hbm.at[:, columns(kv)], out_sems.at[kv])

    @pl.when(needed == 0)
    def _():
        out_ref[...] = jnp.zeros_like(out_ref)
        for kv in range(kv_heads):
            out_copy(kv).start()
        for kv in range(kv_heads):
            out_copy(kv).wait()

    def run(count, lone):
        slots = count * tokens
        chunk = 64
        copies = []
        for t in range(count):
            for part, target in enumerate((key_ref, value_ref)):
                source = pieces[t].at[pl.ds(part * kv_width, kv_width)]
                copies.append(
                    pltpu.make_async_copy(source, target.at[t], piece_sems.at[part, t])
                )
        for copy in copies:
            copy.start()
        for kv in range(kv_heads):
            query_copy(kv).start()
        store_bias(bias_ref, row_first, first, end, range(count))
        live = None if lone else live_rows(row_first, first, end, tokens)
        for copy in copies:
            copy.wait()

        def widen(kv, carry):
            row, lanes = value_place(kv, tokens)
            for t in range(count):
                rows = slice(t * tokens, (t + 1) * tokens)
                wide_ref[kv, rows, :HD] = value_ref[t, pl.ds(row, tokens), pl.ds(lanes, HD)]
                wide_ref[kv, rows, HD:] = jnp.ones((tokens, HD), BF16)
            return carry

        lax.fori_loop(0, kv_heads, widen, 0)

        def place(h):
            kv = h // Q_PER_KV
            return kv, pl.ds(pl.multiple_of((h - kv * Q_PER_KV) * HD, HD), HD)

        def score_steps(h, slot):
            kv, lanes = place(h)
            features = pl.ds(pl.multiple_of(kv * HD, HD), HD)

            def step(t):
                scores[slot][:, t * tokens : (t + 1) * tokens] = dot(
                    query_ref[kv, :, lanes], key_ref[t, features, :]
                )

            return [functools.partial(step, t) for t in range(count)]

        def weight_steps(slot):
            tops = {}

            def part(at, t):
                piece = slice(t * tokens, (t + 1) * tokens)
                score = scores[slot][at : at + chunk, piece]
                if lone and t > 0:
                    return score
                return score + bias_ref[at : at + chunk, piece]

            def top_step(at):
                most = part(at, 0)
                for t in range(1, count):
                    most = jnp.maximum(most, part(at, t))
                tops[at] = jnp.max(most, axis=1, keepdims=True)

            def weight_step(at):
                top = tops.pop(at)
                for t in range(count):
                    weights[slot][at : at + chunk, t * tokens : (t + 1) * tokens] = jnp.exp2(
                        (part(at, t) - top) * EXP2
                    ).astype(BF16)

            starts = list(range(0, tokens, chunk))
            steps = [functools.partial(top_step, at) for at in starts[:2]]
            for i, at in enumerate(starts):
                steps.append(functools.partial(weight_step, at))
                if i + 2 < len(starts):
                    steps.append(functools.partial(top_step, starts[i + 2]))
            return steps

        def value_steps(h, slot):
            kv, lanes = place(h)

            def step(at):
                rows = slice(at, at + tokens // 2)
                mixed = dot(weights[slot][rows, :slots], wide_ref[kv, :slots])
                result = mixed[:, :HD] * inverse_of(mixed[:, HD:])
                if not lone:
                    result = jnp.where(live[rows], result, 0.0)
                out_ref[kv, rows, lanes] = result.astype(BF16)

            return [functools.partial(step, at) for at in range(0, tokens, tokens // 2)]

        last = kv_heads * Q_PER_KV - 1
        query_copy(0).wait()
        interleave(score_steps(jnp.int32(0), 0))
        interleave(score_steps(jnp.int32(1), 1), weight_steps(0))

        def kv_step(kv, carry):
            @pl.when(kv + 1 < kv_heads)
            def _():
                query_copy(kv + 1).wait()

            def two_heads(j, inner):
                for slot in range(2):
                    h = kv * Q_PER_KV + 2 * j + slot
                    interleave(
                        score_steps(jnp.minimum(h + 2, last), slot),
                        weight_steps(1 - slot),
                        value_steps(h, slot),
                    )
                return inner

            lax.fori_loop(0, Q_PER_KV // 2, two_heads, 0)
            out_copy(kv).start()
            return carry

        lax.fori_loop(0, kv_heads, kv_step, 0)
        for kv in range(kv_heads):
            out_copy(kv).wait()

    lone = needed < 0
    for k in range(MAX_IN_GROUP):
        lone = lone | (
            (first[k] <= row_first - (needed - 1) * tokens) & (end[k] >= row_first + tokens)
        )
    before = 0
    for count in sorted({c for c in (1, 2, 3, n) if c <= n}):
        here = (needed > before) & (needed <= count)
        exact = (needed == count) & lone
        before = count

        @pl.when(exact)
        def _():
            run(count, True)

        @pl.when(here & jnp.logical_not(exact))
        def _():
            run(count, False)


def call(body, scalars, args, outs, *, grid=None, in_specs=None, out_specs=None, scratch=(), cost, vmem=6, aliases=None):
    whole = pl.BlockSpec(memory_space=pltpu.VMEM)
    if grid is None:
        grid = (1,)
    flops, exps = cost
    moved = sum(a.size * a.dtype.itemsize for a in args) + sum(
        o.size * o.dtype.itemsize for o in outs
    )
    return pl.pallas_call(
        body,
        out_shape=list(outs),
        grid_spec=pltpu.PrefetchScalarGridSpec(
            num_scalar_prefetch=len(scalars),
            grid=grid,
            in_specs=in_specs or [whole] * len(args),
            out_specs=out_specs or [whole] * len(outs),
            scratch_shapes=list(scratch),
        ),
        compiler_params=pltpu.CompilerParams(
            dimension_semantics=("arbitrary",) * len(grid), vmem_limit_bytes=int(vmem * MIB)
        ),
        input_output_aliases=aliases or {},
        cost_estimate=pl.CostEstimate(flops=flops, bytes_accessed=moved, transcendentals=exps),
    )(*scalars, *args)


def shift(x, axis, count, t):
    return lax.ppermute(x, axis, [(i, (i + t) % count) for i in range(count)])


def shards(
    lengths,
    group_of,
    query_pre,
    key_pre,
    value_pre,
    query_new,
    key_new,
    value_new,
    hidden_new,
    out_weight,
    norm_gain,
    gate_weight,
    up_weight,
    down_weight,
):
    n = lax.axis_size("seq")
    count = lax.axis_size("grp")
    seq = lax.axis_index("seq").astype(jnp.int32)
    group = lax.axis_index("grp").astype(jnp.int32)
    tokens = query_pre.shape[0]
    reqs = query_new.shape[0]
    kv_heads = key_pre.shape[1] // HD
    shard_width = query_new.shape[1]
    shard_heads = shard_width // HD
    columns = out_weight.shape[1]
    shape = jax.ShapeDtypeStruct
    vmem = pl.BlockSpec(memory_space=pltpu.VMEM)
    anywhere = pl.BlockSpec(memory_space=pl.ANY)
    dma = pltpu.SemaphoreType.DMA
    facts = jnp.concatenate([jnp.stack([group, seq]), group_of, lengths])
    scalars = (facts,)

    def to_seq(x):
        return [x] + [shift(x, "seq", n, t) for t in range(1, n)]

    def to_grp(x):
        return lax.all_to_all(x, "grp", split_axis=0, concat_axis=0, tiled=True)

    def tie(x, after):
        return lax.optimization_barrier((x, after))[0]

    def up(x, step, after):
        return lax.ppermute(tie(x, after), "seq", [(i, i + 1) for i in range(step - 1, n - 1)])

    pieces = call(
        pack_kernel,
        (),
        (key_pre, value_pre),
        (shape((2 * kv_heads * HD, tokens), BF16),),
        cost=(key_pre.size, 0),
    )
    pieces = list(pieces)

    query, own = call(
        select_kernel,
        scalars,
        (jnp.concatenate([query_new, key_new, value_new], axis=1),),
        (shape((SLOTS_R, shard_width), BF16), shape((shard_heads * SLOTS_R, 2 * HD), F32)),
        cost=(2 * 8 * reqs * shard_width, 0),
    )
    queries = to_seq(query)
    rows = shard_heads * SLOTS_R
    partials = call(
        functools.partial(partial_kernel, n),
        scalars,
        (*queries, pieces[0]),
        [shape((rows, 2 * HD), BF16)] * n,
        scratch=(
            pltpu.VMEM((n, SLOTS_R, shard_width), F32),
            pltpu.VMEM((n, rows, 2 * HD), BF16),
        ),
        cost=(4 * n * rows * tokens * HD, n * rows * tokens),
    )
    partials = [partials[0]] + [shift(partials[t], "seq", n, n - t) for t in range(1, n)]
    pieces.append(up(pieces[-1], 1, partials[1:]))
    (att,) = call(
        functools.partial(combine_kernel, n, count),
        (),
        (*partials, own),
        (shape((count, SLOTS_R, shard_width), BF16),),
        cost=(8 * n * rows * HD, n * rows),
    )
    atts = to_grp(att)

    index = jnp.arange(reqs, dtype=jnp.int32)
    groups = tie(group_of, att)
    same = groups[None, :] == groups[:, None]
    rank = jnp.sum(jnp.where(same & (index[None, :] < index[:, None]), 1, 0), axis=1)
    place = groups * SLOTS_R + rank
    pick = (place[:, None] == jnp.arange(count * SLOTS_R, dtype=jnp.int32)[None, :]).astype(BF16)
    steps = 8
    depth = shard_width // steps
    (proj,) = call(
        functools.partial(project_kernel, count),
        (),
        (pick, atts, out_weight),
        (shape((reqs, columns), BF16),),
        in_specs=[vmem, vmem, anywhere],
        scratch=(
            pltpu.VMEM((steps, depth, columns), BF16),
            pltpu.VMEM((steps, reqs, depth), BF16),
            dma((steps,)),
        ),
        cost=(2 * reqs * shard_width * columns, 0),
        vmem=STREAM + 3,
    )
    projs = to_seq(proj)
    if n > 2:
        pieces.append(up(pieces[-1], 2, projs[1:]))

    hidden_shard = gate_weight.shape[1]
    width = hidden_shard // count
    resid, terms = call(
        functools.partial(gate_up_kernel, n, count),
        (),
        (*projs, hidden_new, norm_gain.reshape(1, -1), gate_weight, up_weight),
        [shape((reqs, columns), F32), shape((count, reqs, 2 * width + HD), BF16)],
        in_specs=[vmem] * (n + 2) + [anywhere] * 2,
        scratch=(
            pltpu.VMEM(gate_weight.shape, BF16),
            pltpu.VMEM(up_weight.shape, BF16),
            dma((2 * count,)),
        ),
        cost=(4 * reqs * columns * hidden_shard, 0),
        vmem=STREAM,
    )
    terms = to_grp(terms)
    (hidden,) = call(
        functools.partial(hidden_kernel, count, columns * count),
        (),
        (terms,),
        (shape((count, reqs, width), BF16),),
        cost=(8 * count * reqs * width, reqs * width),
    )
    if n > 3:
        pieces.append(up(pieces[-1], 3, hidden))
    hiddens = to_grp(hidden)
    share = columns // n
    downs = call(
        functools.partial(down_kernel, count, n),
        scalars,
        (hiddens, down_weight),
        [shape((reqs, share), F32)] * n,
        in_specs=[vmem, anywhere],
        scratch=(pltpu.VMEM((count, width, columns), BF16), dma((count,))),
        cost=(2 * reqs * columns * hidden_shard, 0),
        vmem=STREAM,
    )
    total = lax.dynamic_slice_in_dim(resid, seq * share, share, 1) + downs[0]
    arrived = [shift(downs[t], "seq", n, t) for t in range(1, n)]
    for part in arrived:
        total = total + part
    decode_hidden = total.astype(BF16)
    for step in range(len(pieces), n):
        pieces.append(up(pieces[-1], step, pieces[-1]))

    first = jnp.sum(jnp.where(same & (index[None, :] < index[:, None]), lengths[None, :], 0), axis=1)
    row_first = seq * tokens
    meets = (group_of == group) & (first + lengths > row_first) & (first < row_first + tokens)
    lowest = jnp.min(jnp.where(meets, first, row_first + tokens))
    scalars = (jnp.concatenate([facts, (seq - lax.div(lowest, tokens) + 1)[None]]),)
    wide = Q_PER_KV * HD
    (prefill,) = call(
        functools.partial(prefill_kernel, n),
        scalars,
        (query_pre, *pieces),
        (shape(query_pre.shape, BF16),),
        in_specs=[anywhere] * (1 + n),
        out_specs=[anywhere],
        scratch=[
            pltpu.VMEM((kv_heads, tokens, wide), BF16),
            pltpu.VMEM((n, kv_heads * HD, tokens), BF16),
            pltpu.VMEM((n, kv_heads * HD, tokens), BF16),
            pltpu.VMEM((kv_heads, n * tokens, 2 * HD), BF16),
            pltpu.VMEM((tokens, n * tokens), F32),
            pltpu.VMEM((kv_heads, tokens, wide), BF16),
        ]
        + [pltpu.VMEM((tokens, n * tokens), F32)] * 2
        + [pltpu.VMEM((tokens, n * tokens), BF16)] * 2
        + [dma((kv_heads,)), dma((2, n)), dma((kv_heads,))],
        cost=(8 * n * tokens * query_pre.size, n * tokens * query_pre.size // HD),
        vmem=STREAM + 3,
    )
    return (prefill, decode_hidden)


def solution(mesh):
    return jax.shard_map(
        shards,
        mesh=mesh,
        in_specs=(
            P(),
            P(),
            P(("grp", "seq"), None),
            P(("grp", "seq"), None),
            P(("grp", "seq"), None),
            P(None, "seq"),
            P(None, "seq"),
            P(None, "seq"),
            P(None, "grp"),
            P("seq", "grp"),
            P("grp"),
            P("grp", "seq"),
            P("grp", "seq"),
            P("seq", "grp"),
        ),
        out_specs=(P(("grp", "seq"), None), P(None, ("grp", "seq"))),
        check_vma=False,
    )
```

```python
import functools
import math

import jax
import jax.numpy as jnp
from jax import lax
from jax.experimental import pallas as pl
from jax.experimental.pallas import tpu as pltpu
from jax.sharding import PartitionSpec as P

HD = 128
Q_PER_KV = 8
MAX_IN_GROUP = 3
SLOTS_R = 4
NEGATIVE = -1e30
LOG2E = 1.4426950408889634
MIB = 1 << 20
STREAM = 57

F32 = jnp.float32
BF16 = jnp.bfloat16


def dot(a, b):
    return jnp.dot(a, b, preferred_element_type=F32)


def dot_t(a, b):
    return lax.dot_general(a, b, (((1,), (1,)), ((), ())), preferred_element_type=F32)


def plan(facts):
    group = facts[0]
    reqs = (facts.shape[0] - 2) // 2
    ids = [jnp.int32(-1)] * MAX_IN_GROUP
    first = [jnp.int32(0)] * MAX_IN_GROUP
    end = [jnp.int32(0)] * MAX_IN_GROUP
    count = jnp.int32(0)
    used = jnp.int32(0)
    for r in range(reqs):
        mine = facts[2 + r] == group
        length = facts[2 + reqs + r]
        for k in range(MAX_IN_GROUP):
            here = mine & (count == k)
            ids[k] = jnp.where(here, r, ids[k])
            first[k] = jnp.where(here, used, first[k])
            end[k] = jnp.where(here, used + length, end[k])
        count = count + jnp.where(mine, 1, 0)
        used = used + jnp.where(mine, length, 0)
    return ids, first, end


def pick_rows(ids, rows, columns):
    row = lax.broadcasted_iota(jnp.int32, (rows, columns), 0)
    column = lax.broadcasted_iota(jnp.int32, (rows, columns), 1)
    target = jnp.full((rows, columns), -1, jnp.int32)
    for k in range(MAX_IN_GROUP):
        target = jnp.where(row == k, ids[k], target)
    return jnp.where(column == target, 1.0, 0.0).astype(BF16)


def split3(x):
    hi = x.astype(BF16)
    rest = x - hi.astype(F32)
    mid = rest.astype(BF16)
    low = (rest - mid.astype(F32)).astype(BF16)
    return hi, mid, low


def by_head(array, group):
    heads = array.shape[1] // HD * group
    return jnp.concatenate([array[:, (h // group) * HD :][:, :HD] for h in range(heads)], axis=0)


def spread(x, lane):
    hi, mid, low = split3(jnp.broadcast_to(x, x.shape[:-1] + (HD,)))
    return jnp.where(
        lane < 32, hi.astype(F32), jnp.where(lane < 64, mid.astype(F32), low.astype(F32))
    ).astype(BF16)


def gathered(stats):
    return stats[..., 0:1] + stats[..., 32:33] + stats[..., 64:65]


def select_kernel(facts, new_ref, query_ref, own_ref):
    ids, _, _ = plan(facts)
    width = query_ref.shape[1]
    kv_width = (new_ref.shape[1] - width) // 2
    new = dot(pick_rows(ids, 8, new_ref.shape[0]), new_ref[...])[:SLOTS_R]
    query_ref[...] = new[:, :width].astype(BF16)
    keys = by_head(new[:, width : width + kv_width], Q_PER_KV)
    values = by_head(new[:, width + kv_width :], Q_PER_KV)
    score = jnp.sum(by_head(new[:, :width], 1) * keys, axis=1, keepdims=True)
    own_ref[:, :HD] = values
    own_ref[:, HD:] = jnp.broadcast_to(score * (1.0 / math.sqrt(HD)), values.shape)


def pack_kernel(key_ref, value_ref, out_ref):
    tokens, width = key_ref.shape
    for at in range(0, width, HD):
        keys = key_ref[:, at : at + HD].astype(F32)
        out_ref[at : at + HD, :] = jnp.transpose(keys).astype(BF16)
    for at in range(0, width, tokens):
        out_ref[width + at : width + at + tokens, :] = value_ref[:, at : at + tokens]


def value_place(kv, tokens):
    side = tokens // HD
    row = pl.multiple_of(kv // side * tokens, tokens)
    return row, pl.multiple_of(lax.rem(kv, side) * HD, HD)


def partial_kernel(n, facts, *refs):
    queries, cache_ref, outs = refs[:n], refs[n], refs[n + 1 : 2 * n + 1]
    query_ref, out_ref = refs[2 * n + 1 :]
    _, first, end = plan(facts)
    kv_width, tokens = cache_ref.shape[0] // 2, cache_ref.shape[1]
    kv_per = queries[0].shape[1] // (HD * Q_PER_KV)
    rows = Q_PER_KV * SLOTS_R
    slot = facts[1] * tokens + lax.broadcasted_iota(jnp.int32, (rows, tokens), 1)
    rank = lax.broadcasted_iota(jnp.int32, (rows, tokens), 0) & (SLOTS_R - 1)
    low = jnp.zeros((rows, tokens), jnp.int32)
    high = jnp.zeros((rows, tokens), jnp.int32)
    for k in range(MAX_IN_GROUP):
        low = jnp.where(rank == k, first[k], low)
        high = jnp.where(rank == k, end[k], high)
    allowed = (slot >= low) & (slot < high)
    lane = lax.broadcasted_iota(jnp.int32, (rows, HD), 1)
    scale = 1.0 / math.sqrt(HD)
    for t in range(n):
        query_ref[t] = queries[t][...].astype(F32)

    def head(j, carry):
        t = j // kv_per
        i = j - t * kv_per
        shard = lax.rem(facts[1] - t + n, n)
        kv = shard * kv_per + i
        keys = cache_ref[pl.ds(pl.multiple_of(kv * HD, HD), HD), :]
        row, lanes = value_place(kv, tokens)
        values = cache_ref[pl.ds(kv_width + row, tokens), pl.ds(lanes, HD)]
        width = Q_PER_KV * HD
        query = query_ref[t, :, pl.ds(pl.multiple_of(i * width, width), width)]
        scores = dot(by_head(query, 1).astype(BF16), keys) * scale
        scores = jnp.where(allowed, scores, NEGATIVE)
        top = jnp.max(scores, axis=1, keepdims=True)
        weights = jnp.where(allowed, jnp.exp(scores - top), 0.0)
        total = jnp.sum(weights, axis=1, keepdims=True)
        some = total > 0.0
        mixed = dot(weights.astype(BF16), values) / jnp.where(some, total, 1.0)
        level = jnp.where(some, top + jnp.log(jnp.where(some, total, 1.0)), NEGATIVE)
        out_ref[t, pl.ds(pl.multiple_of(i * rows, rows), rows), :] = jnp.concatenate(
            [mixed.astype(BF16), spread(level, lane)], axis=1
        )
        return carry

    lax.fori_loop(0, n * kv_per, head, 0)
    for t in range(n):
        outs[t][...] = out_ref[t]


def combine_kernel(n, count, *refs):
    parts, own_ref, out_ref = refs[:n], refs[n], refs[n + 1]
    own_value = own_ref[:, :HD]
    own_score = own_ref[:, HD : HD + 1]
    mixes = []
    levels = []
    top = own_score
    for t in range(n):
        part = parts[t][...].astype(F32)
        stats = part[:, HD:]
        level = stats[:, 0:1] + stats[:, 32:33] + stats[:, 64:65]
        mixes.append(part[:, :HD])
        levels.append(level)
        top = jnp.maximum(top, level)
    own_weight = jnp.exp(own_score - top)
    total = own_weight
    mixed = own_weight.astype(BF16).astype(F32) * own_value
    for t in range(n):
        weight = jnp.exp(levels[t] - top)
        total = total + weight
        mixed = mixed + weight * mixes[t]
    result = mixed / total
    for h in range(out_ref.shape[2] // HD):
        head = result[h * SLOTS_R : (h + 1) * SLOTS_R].astype(BF16)
        for g in range(count):
            out_ref[g, :, h * HD : (h + 1) * HD] = head


def start_all(pairs, sems):
    copies = [
        pltpu.make_async_copy(source, target, sems.at[i]) for i, (source, target) in enumerate(pairs)
    ]
    for copy in copies:
        copy.start()
    return copies


def project_kernel(count, pick_ref, parts_ref, weight_ref, out_ref, buffer_ref, att_ref, sems):
    steps, _, depth = att_ref.shape

    def copy(j):
        rows = pl.ds(pl.multiple_of(j * depth, depth), depth)
        return pltpu.make_async_copy(weight_ref.at[rows], buffer_ref.at[j], sems.at[j])

    for j in range(steps):
        copy(j).start()
    stacked = jnp.concatenate([parts_ref[g].astype(F32) for g in range(count)], axis=0)
    att = dot(pick_ref[...], stacked.astype(BF16)).astype(BF16)
    for j in range(steps):
        att_ref[j] = att[:, j * depth : (j + 1) * depth]

    def block(j, total):
        copy(j).wait()
        return total + dot(att_ref[j], buffer_ref[j])

    total = lax.fori_loop(0, steps, block, jnp.zeros(out_ref.shape, F32))
    out_ref[...] = total.astype(out_ref.dtype)


def gate_up_kernel(n, count, *refs):
    parts = refs[:n]
    hidden_ref, gain_ref, gate_ref, up_ref, resid_ref, send_ref, gates_ref, ups_ref, sems = refs[n:]
    width = gate_ref.shape[1] // count
    blocks = [pl.ds(g * width, width) for g in range(count)]
    pairs = []
    for b in blocks:
        pairs.append((gate_ref.at[:, b], gates_ref.at[:, b]))
        pairs.append((up_ref.at[:, b], ups_ref.at[:, b]))
    copies = start_all(pairs, sems)
    resid = parts[0][...].astype(F32)
    for part in parts[1:]:
        resid = resid + part[...].astype(F32)
    resid = resid + hidden_ref[...].astype(F32)
    resid_ref[...] = resid
    scaled = (resid * gain_ref[...].astype(F32)).astype(BF16)
    squares = jnp.sum(resid * resid, axis=1, keepdims=True)
    rows = resid.shape[0]
    hi, mid, low = split3(jnp.broadcast_to(squares, (rows, HD)))
    lane = lax.broadcasted_iota(jnp.int32, (rows, HD), 1)
    stats = jnp.where(
        lane < 32, hi.astype(F32), jnp.where(lane < 64, mid.astype(F32), low.astype(F32))
    ).astype(BF16)
    for g in range(count):
        send_ref[g, :, 2 * width :] = stats
    for g in range(count):
        copies[2 * g].wait()
        send_ref[g, :, :width] = dot(scaled, gates_ref[:, blocks[g]]).astype(BF16)
        copies[2 * g + 1].wait()
        send_ref[g, :, width : 2 * width] = dot(scaled, ups_ref[:, blocks[g]]).astype(BF16)


def hidden_kernel(count, features, parts_ref, out_ref):
    width = out_ref.shape[2]
    total = parts_ref[0].astype(F32)
    for g in range(1, count):
        total = total + parts_ref[g].astype(F32)
    stats = total[:, 2 * width :]
    squares = stats[:, 0:1] + stats[:, 32:33] + stats[:, 64:65]
    inverse = lax.rsqrt(squares / features + 1e-05)
    gate = total[:, :width] * inverse
    upper = total[:, width : 2 * width] * inverse
    hidden = (gate / (1.0 + jnp.exp(-gate)) * upper).astype(BF16)
    for g in range(count):
        out_ref[g] = hidden


def down_kernel(count, n, facts, parts_ref, weight_ref, *refs):
    sends, buffer_ref, sems = refs[:n], refs[n], refs[n + 1]
    depth = buffer_ref.shape[1]
    width = sends[0].shape[1]

    def copy(g):
        rows = pl.ds(pl.multiple_of(g * depth, depth), depth)
        return pltpu.make_async_copy(weight_ref.at[rows], buffer_ref.at[g], sems.at[g])

    for g in range(count):
        copy(g).start()

    def block(g, total):
        copy(g).wait()
        return total + dot(parts_ref[g], buffer_ref[g])

    shape = (sends[0].shape[0], weight_ref.shape[1])
    total = lax.fori_loop(0, count, block, jnp.zeros(shape, F32))
    for own in range(n):

        @pl.when(facts[1] == own)
        def _():
            for t in range(n):
                target = (own + t) % n
                sends[t][...] = total[:, target * width : (target + 1) * width]


def row_facts(facts, tokens):
    _, first, end = plan(facts)
    return facts[1] * tokens, facts[facts.shape[0] - 1], first, end


def live_rows(row_first, first, end, tokens):
    row = row_first + lax.broadcasted_iota(jnp.int32, (tokens, HD), 0)
    live = row < 0
    for k in range(MAX_IN_GROUP):
        live = live | ((row >= first[k]) & (row < end[k]))
    return live


def store_bias(bias_ref, row_first, first, end, pieces):
    tokens = bias_ref.shape[0]
    row = row_first + lax.broadcasted_iota(jnp.int32, (tokens, tokens), 0)
    column = lax.broadcasted_iota(jnp.int32, (tokens, tokens), 1)
    low = jnp.full((tokens, tokens), 1 << 30, jnp.int32)
    for k in range(MAX_IN_GROUP):
        low = jnp.where((row >= first[k]) & (row < end[k]), first[k], low)
    for place, t in enumerate(pieces):
        slot = row_first - t * tokens + column
        bias_ref[:, place * tokens : (place + 1) * tokens] = jnp.where(
            (slot >= low) & (slot <= row), 0.0, NEGATIVE
        )


EXP2 = LOG2E / math.sqrt(HD)


def inverse_of(x):
    guess = pl.reciprocal(x, approx=True)
    return guess * (2.0 - x * guess)


DEPTH = 30
CUBIC = (0.99992498, 0.69583478, 0.22606662, 0.07802355)


def power_of_two(x):
    y = x + float(DEPTH)
    whole = y.astype(jnp.int32)
    rest = y - whole.astype(F32)
    value = CUBIC[3] * 2.0**-DEPTH
    for factor in reversed(CUBIC[:3]):
        value = value * rest + factor * 2.0**-DEPTH
    value = value * jnp.left_shift(jnp.ones_like(whole), whole).astype(F32)
    return jnp.where(y < 0.0, 0.0, value)


def by_products(count, t, half, odd):
    if t == 1:
        return True
    if count == 2:
        return False
    if count == 3:
        return t == 2 and half == 0 and odd
    return t % 2 == 0 and t > 0 and half == 0


def interleave(*tasks):
    order = sorted(
        ((k + 0.5) / len(task), which, step)
        for which, task in enumerate(tasks)
        for k, step in enumerate(range(len(task)))
    )
    for _, which, step in order:
        tasks[which][step]()


def prefill_kernel(n, facts, *refs):
    query_hbm, pieces, out_hbm = refs[0], refs[1 : 1 + n], refs[1 + n]
    query_ref, key_ref, value_ref, wide_ref, bias_ref, out_ref = refs[2 + n : 8 + n]
    scores, weights, (query_sems, piece_sems, out_sems) = (
        refs[8 + n : 10 + n],
        refs[10 + n : 12 + n],
        refs[12 + n :],
    )
    tokens = query_ref.shape[1]
    kv_heads = query_ref.shape[0]
    kv_width = key_ref.shape[1]
    row_first, needed, first, end = row_facts(facts, tokens)

    def columns(kv):
        width = Q_PER_KV * HD
        return pl.ds(pl.multiple_of(kv * width, width), width)

    def query_copy(kv):
        return pltpu.make_async_copy(
            query_hbm.at[:, columns(kv)], query_ref.at[kv], query_sems.at[kv]
        )

    def out_copy(kv):
        return pltpu.make_async_copy(out_ref.at[kv], out_hbm.at[:, columns(kv)], out_sems.at[kv])

    @pl.when(needed == 0)
    def _():
        out_ref[...] = jnp.zeros_like(out_ref)
        for kv in range(kv_heads):
            out_copy(kv).start()
        for kv in range(kv_heads):
            out_copy(kv).wait()

    def run(count, lone):
        slots = count * tokens
        chunk = 64
        copies = []
        for t in range(count):
            for part, target in enumerate((key_ref, value_ref)):
                source = pieces[t].at[pl.ds(part * kv_width, kv_width)]
                copies.append(
                    pltpu.make_async_copy(source, target.at[t], piece_sems.at[part, t])
                )
        for copy in copies:
            copy.start()
        for kv in range(kv_heads):
            query_copy(kv).start()
        store_bias(bias_ref, row_first, first, end, range(count))
        live = None if lone else live_rows(row_first, first, end, tokens)
        for copy in copies:
            copy.wait()

        def widen(kv, carry):
            row, lanes = value_place(kv, tokens)
            for t in range(count):
                rows = slice(t * tokens, (t + 1) * tokens)
                wide_ref[kv, rows, :HD] = value_ref[t, pl.ds(row, tokens), pl.ds(lanes, HD)]
                wide_ref[kv, rows, HD:] = jnp.ones((tokens, HD), BF16)
            return carry

        lax.fori_loop(0, kv_heads, widen, 0)

        def place(h):
            kv = h // Q_PER_KV
            return kv, pl.ds(pl.multiple_of((h - kv * Q_PER_KV) * HD, HD), HD)

        def score_steps(h, slot):
            kv, lanes = place(h)
            features = pl.ds(pl.multiple_of(kv * HD, HD), HD)

            def step(t):
                scores[slot][:, t * tokens : (t + 1) * tokens] = dot(
                    query_ref[kv, :, lanes], key_ref[t, features, :]
                )

            return [functools.partial(step, t) for t in range(count)]

        def weight_steps(slot):
            tops = {}

            half = tokens // 2

            def blocks(at):
                for t in range(count):
                    for side in range(2):
                        if t > 0 or side == 0 or at + chunk > half:
                            yield t, side

            def part(at, t, side):
                rows = slice(at, at + chunk)
                lanes = slice(t * tokens + side * half, t * tokens + (side + 1) * half)
                score = scores[slot][rows, lanes]
                return score if lone and t > 0 else score + bias_ref[rows, lanes]

            def top_step(at):
                most = None
                for t, side in blocks(at):
                    block = part(at, t, side)
                    most = block if most is None else jnp.maximum(most, block)
                tops[at] = jnp.max(most, axis=1, keepdims=True)

            def weight_step(at):
                top = tops.pop(at)
                for t, side in blocks(at):
                    power = (part(at, t, side) - top) * EXP2
                    if by_products(count, t, side, at // chunk % 2 == 1):
                        weight = power_of_two(power)
                    else:
                        weight = jnp.exp2(power)
                    lanes = slice(t * tokens + side * half, t * tokens + (side + 1) * half)
                    weights[slot][at : at + chunk, lanes] = weight.astype(BF16)

            starts = list(range(0, tokens, chunk))
            steps = [functools.partial(top_step, at) for at in starts[:2]]
            for i, at in enumerate(starts):
                steps.append(functools.partial(weight_step, at))
                if i + 2 < len(starts):
                    steps.append(functools.partial(top_step, starts[i + 2]))
            return steps

        def value_steps(h, slot):
            kv, lanes = place(h)

            def step(at):
                rows = slice(at, at + tokens // 2)
                mixed = dot(weights[slot][rows, :slots], wide_ref[kv, :slots])
                result = mixed[:, :HD] * inverse_of(mixed[:, HD:])
                if not lone:
                    result = jnp.where(live[rows], result, 0.0)
                out_ref[kv, rows, lanes] = result.astype(BF16)

            return [functools.partial(step, at) for at in range(0, tokens, tokens // 2)]

        for slot in range(2):
            weights[slot][: tokens // 2, tokens // 2 : tokens] = jnp.zeros(
                (tokens // 2, tokens // 2), BF16
            )
        last = kv_heads * Q_PER_KV - 1
        query_copy(0).wait()
        interleave(score_steps(jnp.int32(0), 0))
        interleave(score_steps(jnp.int32(1), 1), weight_steps(0))

        def kv_step(kv, carry):
            @pl.when(kv + 1 < kv_heads)
            def _():
                query_copy(kv + 1).wait()

            def two_heads(j, inner):
                for slot in range(2):
                    h = kv * Q_PER_KV + 2 * j + slot
                    interleave(
                        score_steps(jnp.minimum(h + 2, last), slot),
                        weight_steps(1 - slot),
                        value_steps(h, slot),
                    )
                return inner

            lax.fori_loop(0, Q_PER_KV // 2, two_heads, 0)
            out_copy(kv).start()
            return carry

        lax.fori_loop(0, kv_heads, kv_step, 0)
        for kv in range(kv_heads):
            out_copy(kv).wait()

    lone = needed < 0
    for k in range(MAX_IN_GROUP):
        lone = lone | (
            (first[k] <= row_first - (needed - 1) * tokens) & (end[k] >= row_first + tokens)
        )
    before = 0
    for count in sorted({c for c in (1, 2, 3, n) if c <= n}):
        here = (needed > before) & (needed <= count)
        exact = (needed == count) & lone
        before = count

        @pl.when(exact)
        def _():
            run(count, True)

        @pl.when(here & jnp.logical_not(exact))
        def _():
            run(count, False)


def call(body, scalars, args, outs, *, grid=None, in_specs=None, out_specs=None, scratch=(), cost, vmem=6, aliases=None):
    whole = pl.BlockSpec(memory_space=pltpu.VMEM)
    if grid is None:
        grid = (1,)
    flops, exps = cost
    moved = sum(a.size * a.dtype.itemsize for a in args) + sum(
        o.size * o.dtype.itemsize for o in outs
    )
    return pl.pallas_call(
        body,
        out_shape=list(outs),
        grid_spec=pltpu.PrefetchScalarGridSpec(
            num_scalar_prefetch=len(scalars),
            grid=grid,
            in_specs=in_specs or [whole] * len(args),
            out_specs=out_specs or [whole] * len(outs),
            scratch_shapes=list(scratch),
        ),
        compiler_params=pltpu.CompilerParams(
            dimension_semantics=("arbitrary",) * len(grid), vmem_limit_bytes=int(vmem * MIB)
        ),
        input_output_aliases=aliases or {},
        cost_estimate=pl.CostEstimate(flops=flops, bytes_accessed=moved, transcendentals=exps),
    )(*scalars, *args)


def shift(x, axis, count, t):
    return lax.ppermute(x, axis, [(i, (i + t) % count) for i in range(count)])


def shards(
    lengths,
    group_of,
    query_pre,
    key_pre,
    value_pre,
    query_new,
    key_new,
    value_new,
    hidden_new,
    out_weight,
    norm_gain,
    gate_weight,
    up_weight,
    down_weight,
):
    n = lax.axis_size("seq")
    count = lax.axis_size("grp")
    seq = lax.axis_index("seq").astype(jnp.int32)
    group = lax.axis_index("grp").astype(jnp.int32)
    tokens = query_pre.shape[0]
    reqs = query_new.shape[0]
    kv_heads = key_pre.shape[1] // HD
    shard_width = query_new.shape[1]
    shard_heads = shard_width // HD
    columns = out_weight.shape[1]
    shape = jax.ShapeDtypeStruct
    vmem = pl.BlockSpec(memory_space=pltpu.VMEM)
    anywhere = pl.BlockSpec(memory_space=pl.ANY)
    dma = pltpu.SemaphoreType.DMA
    facts = jnp.concatenate([jnp.stack([group, seq]), group_of, lengths])
    scalars = (facts,)

    def to_seq(x):
        return [x] + [shift(x, "seq", n, t) for t in range(1, n)]

    def to_grp(x):
        return lax.all_to_all(x, "grp", split_axis=0, concat_axis=0, tiled=True)

    def tie(x, after):
        return lax.optimization_barrier((x, after))[0]

    def up(x, step, after):
        return lax.ppermute(tie(x, after), "seq", [(i, i + 1) for i in range(step - 1, n - 1)])

    pieces = call(
        pack_kernel,
        (),
        (key_pre, value_pre),
        (shape((2 * kv_heads * HD, tokens), BF16),),
        cost=(key_pre.size, 0),
    )
    pieces = list(pieces)

    query, own = call(
        select_kernel,
        scalars,
        (jnp.concatenate([query_new, key_new, value_new], axis=1),),
        (shape((SLOTS_R, shard_width), BF16), shape((shard_heads * SLOTS_R, 2 * HD), F32)),
        cost=(2 * 8 * reqs * shard_width, 0),
    )
    queries = to_seq(query)
    rows = shard_heads * SLOTS_R
    partials = call(
        functools.partial(partial_kernel, n),
        scalars,
        (*queries, pieces[0]),
        [shape((rows, 2 * HD), BF16)] * n,
        scratch=(
            pltpu.VMEM((n, SLOTS_R, shard_width), F32),
            pltpu.VMEM((n, rows, 2 * HD), BF16),
        ),
        cost=(4 * n * rows * tokens * HD, n * rows * tokens),
    )
    partials = [partials[0]] + [shift(partials[t], "seq", n, n - t) for t in range(1, n)]
    pieces.append(up(pieces[-1], 1, partials[1:]))
    (att,) = call(
        functools.partial(combine_kernel, n, count),
        (),
        (*partials, own),
        (shape((count, SLOTS_R, shard_width), BF16),),
        cost=(8 * n * rows * HD, n * rows),
    )
    atts = to_grp(att)

    index = jnp.arange(reqs, dtype=jnp.int32)
    groups = tie(group_of, att)
    same = groups[None, :] == groups[:, None]
    rank = jnp.sum(jnp.where(same & (index[None, :] < index[:, None]), 1, 0), axis=1)
    place = groups * SLOTS_R + rank
    pick = (place[:, None] == jnp.arange(count * SLOTS_R, dtype=jnp.int32)[None, :]).astype(BF16)
    steps = 8
    depth = shard_width // steps
    (proj,) = call(
        functools.partial(project_kernel, count),
        (),
        (pick, atts, out_weight),
        (shape((reqs, columns), BF16),),
        in_specs=[vmem, vmem, anywhere],
        scratch=(
            pltpu.VMEM((steps, depth, columns), BF16),
            pltpu.VMEM((steps, reqs, depth), BF16),
            dma((steps,)),
        ),
        cost=(2 * reqs * shard_width * columns, 0),
        vmem=STREAM + 3,
    )
    projs = to_seq(proj)
    if n > 2:
        pieces.append(up(pieces[-1], 2, projs[1:]))

    hidden_shard = gate_weight.shape[1]
    width = hidden_shard // count
    resid, terms = call(
        functools.partial(gate_up_kernel, n, count),
        (),
        (*projs, hidden_new, norm_gain.reshape(1, -1), gate_weight, up_weight),
        [shape((reqs, columns), F32), shape((count, reqs, 2 * width + HD), BF16)],
        in_specs=[vmem] * (n + 2) + [anywhere] * 2,
        scratch=(
            pltpu.VMEM(gate_weight.shape, BF16),
            pltpu.VMEM(up_weight.shape, BF16),
            dma((2 * count,)),
        ),
        cost=(4 * reqs * columns * hidden_shard, 0),
        vmem=STREAM,
    )
    terms = to_grp(terms)
    (hidden,) = call(
        functools.partial(hidden_kernel, count, columns * count),
        (),
        (terms,),
        (shape((count, reqs, width), BF16),),
        cost=(8 * count * reqs * width, reqs * width),
    )
    if n > 3:
        pieces.append(up(pieces[-1], 3, hidden))
    hiddens = to_grp(hidden)
    share = columns // n
    downs = call(
        functools.partial(down_kernel, count, n),
        scalars,
        (hiddens, down_weight),
        [shape((reqs, share), F32)] * n,
        in_specs=[vmem, anywhere],
        scratch=(pltpu.VMEM((count, width, columns), BF16), dma((count,))),
        cost=(2 * reqs * columns * hidden_shard, 0),
        vmem=STREAM,
    )
    total = lax.dynamic_slice_in_dim(resid, seq * share, share, 1) + downs[0]
    arrived = [shift(downs[t], "seq", n, t) for t in range(1, n)]
    for part in arrived:
        total = total + part
    decode_hidden = total.astype(BF16)
    for step in range(len(pieces), n):
        pieces.append(up(pieces[-1], step, pieces[-1]))

    first = jnp.sum(jnp.where(same & (index[None, :] < index[:, None]), lengths[None, :], 0), axis=1)
    row_first = seq * tokens
    meets = (group_of == group) & (first + lengths > row_first) & (first < row_first + tokens)
    lowest = jnp.min(jnp.where(meets, first, row_first + tokens))
    scalars = (jnp.concatenate([facts, (seq - lax.div(lowest, tokens) + 1)[None]]),)
    wide = Q_PER_KV * HD
    (prefill,) = call(
        functools.partial(prefill_kernel, n),
        scalars,
        (query_pre, *pieces),
        (shape(query_pre.shape, BF16),),
        in_specs=[anywhere] * (1 + n),
        out_specs=[anywhere],
        scratch=[
            pltpu.VMEM((kv_heads, tokens, wide), BF16),
            pltpu.VMEM((n, kv_heads * HD, tokens), BF16),
            pltpu.VMEM((n, kv_heads * HD, tokens), BF16),
            pltpu.VMEM((kv_heads, n * tokens, 2 * HD), BF16),
            pltpu.VMEM((tokens, n * tokens), F32),
            pltpu.VMEM((kv_heads, tokens, wide), BF16),
        ]
        + [pltpu.VMEM((tokens, n * tokens), F32)] * 2
        + [pltpu.VMEM((tokens, n * tokens), BF16)] * 2
        + [dma((kv_heads,)), dma((2, n)), dma((kv_heads,))],
        cost=(8 * n * tokens * query_pre.size, n * tokens * query_pre.size // HD),
        vmem=STREAM + 3,
    )
    return (prefill, decode_hidden)


def solution(mesh):
    return jax.shard_map(
        shards,
        mesh=mesh,
        in_specs=(
            P(),
            P(),
            P(("grp", "seq"), None),
            P(("grp", "seq"), None),
            P(("grp", "seq"), None),
            P(None, "seq"),
            P(None, "seq"),
            P(None, "seq"),
            P(None, "grp"),
            P("seq", "grp"),
            P("grp"),
            P("grp", "seq"),
            P("grp", "seq"),
            P("seq", "grp"),
        ),
        out_specs=(P(("grp", "seq"), None), P(None, ("grp", "seq"))),
        check_vma=False,
    )
```

```python
import functools
import math

import jax
import jax.numpy as jnp
from jax import lax
from jax.experimental import pallas as pl
from jax.experimental.pallas import tpu as pltpu
from jax.sharding import PartitionSpec as P

HD = 128
Q_PER_KV = 8
MAX_IN_GROUP = 3
SLOTS_R = 4
NEGATIVE = -1e30
MIB = 1 << 20
STREAM = 57

F32 = jnp.float32
BF16 = jnp.bfloat16


def dot(a, b):
    return jnp.dot(a, b, preferred_element_type=F32)


def dot_t(a, b):
    return lax.dot_general(a, b, (((1,), (1,)), ((), ())), preferred_element_type=F32)


def plan(facts):
    group = facts[0]
    reqs = (facts.shape[0] - 2) // 2
    ids = [jnp.int32(-1)] * MAX_IN_GROUP
    first = [jnp.int32(0)] * MAX_IN_GROUP
    end = [jnp.int32(0)] * MAX_IN_GROUP
    count = jnp.int32(0)
    used = jnp.int32(0)
    for r in range(reqs):
        mine = facts[2 + r] == group
        length = facts[2 + reqs + r]
        for k in range(MAX_IN_GROUP):
            here = mine & (count == k)
            ids[k] = jnp.where(here, r, ids[k])
            first[k] = jnp.where(here, used, first[k])
            end[k] = jnp.where(here, used + length, end[k])
        count = count + jnp.where(mine, 1, 0)
        used = used + jnp.where(mine, length, 0)
    return ids, first, end


def pick_rows(ids, rows, columns):
    row = lax.broadcasted_iota(jnp.int32, (rows, columns), 0)
    column = lax.broadcasted_iota(jnp.int32, (rows, columns), 1)
    target = jnp.full((rows, columns), -1, jnp.int32)
    for k in range(MAX_IN_GROUP):
        target = jnp.where(row == k, ids[k], target)
    return jnp.where(column == target, 1.0, 0.0).astype(BF16)


def split3(x):
    hi = x.astype(BF16)
    rest = x - hi.astype(F32)
    mid = rest.astype(BF16)
    low = (rest - mid.astype(F32)).astype(BF16)
    return hi, mid, low


def by_head(array, group):
    heads = array.shape[1] // HD * group
    return jnp.concatenate([array[:, (h // group) * HD :][:, :HD] for h in range(heads)], axis=0)


def spread(x, lane):
    hi, mid, low = split3(jnp.broadcast_to(x, x.shape[:-1] + (HD,)))
    return jnp.where(
        lane < 32, hi.astype(F32), jnp.where(lane < 64, mid.astype(F32), low.astype(F32))
    ).astype(BF16)


def gathered(stats):
    return stats[..., 0:1] + stats[..., 32:33] + stats[..., 64:65]


def select_kernel(facts, new_ref, query_ref, own_ref):
    ids, _, _ = plan(facts)
    width = query_ref.shape[1]
    kv_width = (new_ref.shape[1] - width) // 2
    new = dot(pick_rows(ids, 8, new_ref.shape[0]), new_ref[...])[:SLOTS_R]
    query_ref[...] = new[:, :width].astype(BF16)
    keys = by_head(new[:, width : width + kv_width], Q_PER_KV)
    values = by_head(new[:, width + kv_width :], Q_PER_KV)
    score = jnp.sum(by_head(new[:, :width], 1) * keys, axis=1, keepdims=True)
    own_ref[:, :HD] = values
    own_ref[:, HD:] = jnp.broadcast_to(score * (1.0 / math.sqrt(HD)), values.shape)


def pack_kernel(key_ref, value_ref, out_ref):
    tokens, width = key_ref.shape
    for at in range(0, width, HD):
        keys = key_ref[:, at : at + HD].astype(F32)
        out_ref[at : at + HD, :] = jnp.transpose(keys).astype(BF16)
    for at in range(0, width, tokens):
        out_ref[width + at : width + at + tokens, :] = value_ref[:, at : at + tokens]


def value_place(kv, tokens):
    side = tokens // HD
    row = pl.multiple_of(kv // side * tokens, tokens)
    return row, pl.multiple_of(lax.rem(kv, side) * HD, HD)


def partial_kernel(n, facts, *refs):
    queries, cache_ref, outs = refs[:n], refs[n], refs[n + 1 : 2 * n + 1]
    query_ref, out_ref = refs[2 * n + 1 :]
    _, first, end = plan(facts)
    kv_width, tokens = cache_ref.shape[0] // 2, cache_ref.shape[1]
    kv_per = queries[0].shape[1] // (HD * Q_PER_KV)
    rows = Q_PER_KV * SLOTS_R
    slot = facts[1] * tokens + lax.broadcasted_iota(jnp.int32, (rows, tokens), 1)
    rank = lax.broadcasted_iota(jnp.int32, (rows, tokens), 0) & (SLOTS_R - 1)
    low = jnp.zeros((rows, tokens), jnp.int32)
    high = jnp.zeros((rows, tokens), jnp.int32)
    for k in range(MAX_IN_GROUP):
        low = jnp.where(rank == k, first[k], low)
        high = jnp.where(rank == k, end[k], high)
    allowed = (slot >= low) & (slot < high)
    lane = lax.broadcasted_iota(jnp.int32, (rows, HD), 1)
    scale = 1.0 / math.sqrt(HD)
    for t in range(n):
        query_ref[t] = queries[t][...].astype(F32)

    def head(j, carry):
        t = j // kv_per
        i = j - t * kv_per
        shard = lax.rem(facts[1] - t + n, n)
        kv = shard * kv_per + i
        keys = cache_ref[pl.ds(pl.multiple_of(kv * HD, HD), HD), :]
        row, lanes = value_place(kv, tokens)
        values = cache_ref[pl.ds(kv_width + row, tokens), pl.ds(lanes, HD)]
        width = Q_PER_KV * HD
        query = query_ref[t, :, pl.ds(pl.multiple_of(i * width, width), width)]
        scores = dot(by_head(query, 1).astype(BF16), keys) * scale
        scores = jnp.where(allowed, scores, NEGATIVE)
        top = jnp.max(scores, axis=1, keepdims=True)
        weights = jnp.where(allowed, jnp.exp(scores - top), 0.0)
        total = jnp.sum(weights, axis=1, keepdims=True)
        some = total > 0.0
        mixed = dot(weights.astype(BF16), values) / jnp.where(some, total, 1.0)
        level = jnp.where(some, top + jnp.log(jnp.where(some, total, 1.0)), NEGATIVE)
        out_ref[t, pl.ds(pl.multiple_of(i * rows, rows), rows), :] = jnp.concatenate(
            [mixed.astype(BF16), spread(level, lane)], axis=1
        )
        return carry

    lax.fori_loop(0, n * kv_per, head, 0)
    for t in range(n):
        outs[t][...] = out_ref[t]


def combine_kernel(n, count, *refs):
    parts, own_ref, out_ref = refs[:n], refs[n], refs[n + 1]
    own_value = own_ref[:, :HD]
    own_score = own_ref[:, HD : HD + 1]
    mixes = []
    levels = []
    top = own_score
    for t in range(n):
        part = parts[t][...].astype(F32)
        stats = part[:, HD:]
        level = stats[:, 0:1] + stats[:, 32:33] + stats[:, 64:65]
        mixes.append(part[:, :HD])
        levels.append(level)
        top = jnp.maximum(top, level)
    own_weight = jnp.exp(own_score - top)
    total = own_weight
    mixed = own_weight.astype(BF16).astype(F32) * own_value
    for t in range(n):
        weight = jnp.exp(levels[t] - top)
        total = total + weight
        mixed = mixed + weight * mixes[t]
    result = mixed / total
    for h in range(out_ref.shape[2] // HD):
        head = result[h * SLOTS_R : (h + 1) * SLOTS_R].astype(BF16)
        for g in range(count):
            out_ref[g, :, h * HD : (h + 1) * HD] = head


def start_all(pairs, sems):
    copies = [
        pltpu.make_async_copy(source, target, sems.at[i]) for i, (source, target) in enumerate(pairs)
    ]
    for copy in copies:
        copy.start()
    return copies


def project_kernel(count, pick_ref, parts_ref, weight_ref, out_ref, buffer_ref, att_ref, sems):
    steps, _, depth = att_ref.shape

    def copy(j):
        rows = pl.ds(pl.multiple_of(j * depth, depth), depth)
        return pltpu.make_async_copy(weight_ref.at[rows], buffer_ref.at[j], sems.at[j])

    for j in range(steps):
        copy(j).start()
    stacked = jnp.concatenate([parts_ref[g].astype(F32) for g in range(count)], axis=0)
    att = dot(pick_ref[...], stacked.astype(BF16)).astype(BF16)
    for j in range(steps):
        att_ref[j] = att[:, j * depth : (j + 1) * depth]

    def block(j, total):
        copy(j).wait()
        return total + dot(att_ref[j], buffer_ref[j])

    total = lax.fori_loop(0, steps, block, jnp.zeros(out_ref.shape, F32))
    out_ref[...] = total.astype(out_ref.dtype)


def gate_up_kernel(n, count, *refs):
    parts = refs[:n]
    hidden_ref, gain_ref, gate_ref, up_ref, resid_ref, send_ref, gates_ref, ups_ref, sems = refs[n:]
    width = gate_ref.shape[1] // count
    blocks = [pl.ds(g * width, width) for g in range(count)]
    pairs = []
    for b in blocks:
        pairs.append((gate_ref.at[:, b], gates_ref.at[:, b]))
        pairs.append((up_ref.at[:, b], ups_ref.at[:, b]))
    copies = start_all(pairs, sems)
    resid = parts[0][...].astype(F32)
    for part in parts[1:]:
        resid = resid + part[...].astype(F32)
    resid = resid + hidden_ref[...].astype(F32)
    resid_ref[...] = resid
    scaled = (resid * gain_ref[...].astype(F32)).astype(BF16)
    squares = jnp.sum(resid * resid, axis=1, keepdims=True)
    rows = resid.shape[0]
    hi, mid, low = split3(jnp.broadcast_to(squares, (rows, HD)))
    lane = lax.broadcasted_iota(jnp.int32, (rows, HD), 1)
    stats = jnp.where(
        lane < 32, hi.astype(F32), jnp.where(lane < 64, mid.astype(F32), low.astype(F32))
    ).astype(BF16)
    for g in range(count):
        send_ref[g, :, 2 * width :] = stats
    for g in range(count):
        copies[2 * g].wait()
        send_ref[g, :, :width] = dot(scaled, gates_ref[:, blocks[g]]).astype(BF16)
        copies[2 * g + 1].wait()
        send_ref[g, :, width : 2 * width] = dot(scaled, ups_ref[:, blocks[g]]).astype(BF16)


def hidden_kernel(count, features, parts_ref, out_ref):
    width = out_ref.shape[2]
    total = parts_ref[0].astype(F32)
    for g in range(1, count):
        total = total + parts_ref[g].astype(F32)
    stats = total[:, 2 * width :]
    squares = stats[:, 0:1] + stats[:, 32:33] + stats[:, 64:65]
    inverse = lax.rsqrt(squares / features + 1e-05)
    gate = total[:, :width] * inverse
    upper = total[:, width : 2 * width] * inverse
    hidden = (gate / (1.0 + jnp.exp(-gate)) * upper).astype(BF16)
    for g in range(count):
        out_ref[g] = hidden


def down_kernel(count, n, facts, parts_ref, weight_ref, *refs):
    sends, buffer_ref, sems = refs[:n], refs[n], refs[n + 1]
    depth = buffer_ref.shape[1]
    width = sends[0].shape[1]

    def copy(g):
        rows = pl.ds(pl.multiple_of(g * depth, depth), depth)
        return pltpu.make_async_copy(weight_ref.at[rows], buffer_ref.at[g], sems.at[g])

    for g in range(count):
        copy(g).start()

    def block(g, total):
        copy(g).wait()
        return total + dot(parts_ref[g], buffer_ref[g])

    shape = (sends[0].shape[0], weight_ref.shape[1])
    total = lax.fori_loop(0, count, block, jnp.zeros(shape, F32))
    for own in range(n):

        @pl.when(facts[1] == own)
        def _():
            for t in range(n):
                target = (own + t) % n
                sends[t][...] = total[:, target * width : (target + 1) * width]


def row_facts(facts, tokens):
    _, first, end = plan(facts)
    return facts[1] * tokens, facts[facts.shape[0] - 1], first, end


def live_rows(row_first, first, end, tokens):
    row = row_first + lax.broadcasted_iota(jnp.int32, (tokens, HD), 0)
    live = row < 0
    for k in range(MAX_IN_GROUP):
        live = live | ((row >= first[k]) & (row < end[k]))
    return live


def store_bias(bias_ref, row_first, first, end, pieces):
    tokens = bias_ref.shape[0]
    row = row_first + lax.broadcasted_iota(jnp.int32, (tokens, tokens), 0)
    column = lax.broadcasted_iota(jnp.int32, (tokens, tokens), 1)
    low = jnp.full((tokens, tokens), 1 << 30, jnp.int32)
    for k in range(MAX_IN_GROUP):
        low = jnp.where((row >= first[k]) & (row < end[k]), first[k], low)
    for place, t in enumerate(pieces):
        slot = row_first - t * tokens + column
        bias_ref[:, place * tokens : (place + 1) * tokens] = jnp.where(
            (slot >= low) & (slot <= row), 0.0, NEGATIVE
        )


SCALE = 1.0 / math.sqrt(HD)


def inverse_of(x):
    guess = pl.reciprocal(x, approx=True)
    return guess * (2.0 - x * guess)


def interleave(*tasks):
    order = sorted(
        ((k + 0.5) / len(task), which, step)
        for which, task in enumerate(tasks)
        for k, step in enumerate(range(len(task)))
    )
    for _, which, step in order:
        tasks[which][step]()


def prefill_kernel(n, facts, *refs):
    query_hbm, pieces, out_hbm = refs[0], refs[1 : 1 + n], refs[1 + n]
    query_ref, key_ref, value_ref, wide_ref, bias_ref, out_ref = refs[2 + n : 8 + n]
    scores, weights, (query_sems, piece_sems, out_sems) = (
        refs[8 + n : 10 + n],
        refs[10 + n : 12 + n],
        refs[12 + n :],
    )
    tokens = query_ref.shape[1]
    kv_heads = query_ref.shape[0]
    kv_width = key_ref.shape[1]
    row_first, needed, first, end = row_facts(facts, tokens)

    def columns(kv):
        width = Q_PER_KV * HD
        return pl.ds(pl.multiple_of(kv * width, width), width)

    def query_copy(kv):
        return pltpu.make_async_copy(
            query_hbm.at[:, columns(kv)], query_ref.at[kv], query_sems.at[kv]
        )

    def out_copy(kv):
        return pltpu.make_async_copy(out_ref.at[kv], out_hbm.at[:, columns(kv)], out_sems.at[kv])

    @pl.when(needed == 0)
    def _():
        out_ref[...] = jnp.zeros_like(out_ref)
        for kv in range(kv_heads):
            out_copy(kv).start()
        for kv in range(kv_heads):
            out_copy(kv).wait()

    def run(count, lone):
        slots = count * tokens
        chunk = 64
        copies = []
        for t in range(count):
            for part, target in enumerate((key_ref, value_ref)):
                source = pieces[t].at[pl.ds(part * kv_width, kv_width)]
                copies.append(
                    pltpu.make_async_copy(source, target.at[t], piece_sems.at[part, t])
                )
        for copy in copies:
            copy.start()
        for kv in range(kv_heads):
            query_copy(kv).start()
        store_bias(bias_ref, row_first, first, end, range(count))
        live = None if lone else live_rows(row_first, first, end, tokens)
        for copy in copies:
            copy.wait()

        def widen(kv, carry):
            row, lanes = value_place(kv, tokens)
            for t in range(count):
                rows = slice(t * tokens, (t + 1) * tokens)
                wide_ref[kv, rows, :HD] = value_ref[t, pl.ds(row, tokens), pl.ds(lanes, HD)]
                wide_ref[kv, rows, HD:] = jnp.ones((tokens, HD), BF16)
            return carry

        lax.fori_loop(0, kv_heads, widen, 0)

        def place(h):
            kv = h // Q_PER_KV
            return kv, pl.ds(pl.multiple_of((h - kv * Q_PER_KV) * HD, HD), HD)

        def score_steps(h, slot):
            kv, lanes = place(h)
            features = pl.ds(pl.multiple_of(kv * HD, HD), HD)

            def step(t):
                scores[slot][:, t * tokens : (t + 1) * tokens] = dot(
                    query_ref[kv, :, lanes], key_ref[t, features, :]
                )

            return [functools.partial(step, t) for t in range(count)]

        def weight_steps(slot):
            tops = {}

            half = tokens // 2

            def blocks(at):
                for t in range(count):
                    for side in range(2):
                        if t > 0 or side == 0 or at + chunk > half:
                            yield t, side

            def part(at, t, side):
                rows = slice(at, at + chunk)
                lanes = slice(t * tokens + side * half, t * tokens + (side + 1) * half)
                score = scores[slot][rows, lanes]
                return score if lone and t > 0 else score + bias_ref[rows, lanes]

            def top_step(at):
                most = None
                for t, side in blocks(at):
                    block = part(at, t, side)
                    most = block if most is None else jnp.maximum(most, block)
                tops[at] = jnp.max(most, axis=1, keepdims=True)

            def weight_step(at):
                top = tops.pop(at)
                for t, side in blocks(at):
                    weight = jnp.exp((part(at, t, side) - top) * SCALE)
                    lanes = slice(t * tokens + side * half, t * tokens + (side + 1) * half)
                    weights[slot][at : at + chunk, lanes] = weight.astype(BF16)

            starts = list(range(0, tokens, chunk))
            steps = [functools.partial(top_step, at) for at in starts[:2]]
            for i, at in enumerate(starts):
                steps.append(functools.partial(weight_step, at))
                if i + 2 < len(starts):
                    steps.append(functools.partial(top_step, starts[i + 2]))
            return steps

        def value_steps(h, slot):
            kv, lanes = place(h)

            def step(at):
                rows = slice(at, at + tokens // 2)
                mixed = dot(weights[slot][rows, :slots], wide_ref[kv, :slots])
                result = mixed[:, :HD] * inverse_of(mixed[:, HD:])
                if not lone:
                    result = jnp.where(live[rows], result, 0.0)
                out_ref[kv, rows, lanes] = result.astype(BF16)

            return [functools.partial(step, at) for at in range(0, tokens, tokens // 2)]

        for slot in range(2):
            weights[slot][: tokens // 2, tokens // 2 : tokens] = jnp.zeros(
                (tokens // 2, tokens // 2), BF16
            )
        last = kv_heads * Q_PER_KV - 1
        query_copy(0).wait()
        interleave(score_steps(jnp.int32(0), 0))
        interleave(score_steps(jnp.int32(1), 1), weight_steps(0))

        def kv_step(kv, carry):
            @pl.when(kv + 1 < kv_heads)
            def _():
                query_copy(kv + 1).wait()

            def two_heads(j, inner):
                for slot in range(2):
                    h = kv * Q_PER_KV + 2 * j + slot
                    interleave(
                        score_steps(jnp.minimum(h + 2, last), slot),
                        weight_steps(1 - slot),
                        value_steps(h, slot),
                    )
                return inner

            lax.fori_loop(0, Q_PER_KV // 2, two_heads, 0)
            out_copy(kv).start()
            return carry

        lax.fori_loop(0, kv_heads, kv_step, 0)
        for kv in range(kv_heads):
            out_copy(kv).wait()

    lone = needed < 0
    for k in range(MAX_IN_GROUP):
        lone = lone | (
            (first[k] <= row_first - (needed - 1) * tokens) & (end[k] >= row_first + tokens)
        )
    before = 0
    for count in sorted({c for c in (1, 2, 3, n) if c <= n}):
        here = (needed > before) & (needed <= count)
        exact = (needed == count) & lone
        before = count

        @pl.when(exact)
        def _():
            run(count, True)

        @pl.when(here & jnp.logical_not(exact))
        def _():
            run(count, False)


def call(body, scalars, args, outs, *, grid=None, in_specs=None, out_specs=None, scratch=(), cost, vmem=6, aliases=None):
    whole = pl.BlockSpec(memory_space=pltpu.VMEM)
    if grid is None:
        grid = (1,)
    flops, exps = cost
    moved = sum(a.size * a.dtype.itemsize for a in args) + sum(
        o.size * o.dtype.itemsize for o in outs
    )
    return pl.pallas_call(
        body,
        out_shape=list(outs),
        grid_spec=pltpu.PrefetchScalarGridSpec(
            num_scalar_prefetch=len(scalars),
            grid=grid,
            in_specs=in_specs or [whole] * len(args),
            out_specs=out_specs or [whole] * len(outs),
            scratch_shapes=list(scratch),
        ),
        compiler_params=pltpu.CompilerParams(
            dimension_semantics=("arbitrary",) * len(grid), vmem_limit_bytes=int(vmem * MIB)
        ),
        input_output_aliases=aliases or {},
        cost_estimate=pl.CostEstimate(flops=flops, bytes_accessed=moved, transcendentals=exps),
    )(*scalars, *args)


def shift(x, axis, count, t):
    return lax.ppermute(x, axis, [(i, (i + t) % count) for i in range(count)])


def shards(
    lengths,
    group_of,
    query_pre,
    key_pre,
    value_pre,
    query_new,
    key_new,
    value_new,
    hidden_new,
    out_weight,
    norm_gain,
    gate_weight,
    up_weight,
    down_weight,
):
    n = lax.axis_size("seq")
    count = lax.axis_size("grp")
    seq = lax.axis_index("seq").astype(jnp.int32)
    group = lax.axis_index("grp").astype(jnp.int32)
    tokens = query_pre.shape[0]
    reqs = query_new.shape[0]
    kv_heads = key_pre.shape[1] // HD
    shard_width = query_new.shape[1]
    shard_heads = shard_width // HD
    columns = out_weight.shape[1]
    shape = jax.ShapeDtypeStruct
    vmem = pl.BlockSpec(memory_space=pltpu.VMEM)
    anywhere = pl.BlockSpec(memory_space=pl.ANY)
    dma = pltpu.SemaphoreType.DMA
    facts = jnp.concatenate([jnp.stack([group, seq]), group_of, lengths])
    scalars = (facts,)

    def to_seq(x):
        return [x] + [shift(x, "seq", n, t) for t in range(1, n)]

    def to_grp(x):
        return lax.all_to_all(x, "grp", split_axis=0, concat_axis=0, tiled=True)

    def tie(x, after):
        return lax.optimization_barrier((x, after))[0]

    def up(x, step, after):
        return lax.ppermute(tie(x, after), "seq", [(i, i + 1) for i in range(step - 1, n - 1)])

    pieces = call(
        pack_kernel,
        (),
        (key_pre, value_pre),
        (shape((2 * kv_heads * HD, tokens), BF16),),
        cost=(key_pre.size, 0),
    )
    pieces = list(pieces)

    query, own = call(
        select_kernel,
        scalars,
        (jnp.concatenate([query_new, key_new, value_new], axis=1),),
        (shape((SLOTS_R, shard_width), BF16), shape((shard_heads * SLOTS_R, 2 * HD), F32)),
        cost=(2 * 8 * reqs * shard_width, 0),
    )
    queries = to_seq(query)
    rows = shard_heads * SLOTS_R
    partials = call(
        functools.partial(partial_kernel, n),
        scalars,
        (*queries, pieces[0]),
        [shape((rows, 2 * HD), BF16)] * n,
        scratch=(
            pltpu.VMEM((n, SLOTS_R, shard_width), F32),
            pltpu.VMEM((n, rows, 2 * HD), BF16),
        ),
        cost=(4 * n * rows * tokens * HD, n * rows * tokens),
    )
    partials = [partials[0]] + [shift(partials[t], "seq", n, n - t) for t in range(1, n)]
    pieces.append(up(pieces[-1], 1, partials[1:]))
    (att,) = call(
        functools.partial(combine_kernel, n, count),
        (),
        (*partials, own),
        (shape((count, SLOTS_R, shard_width), BF16),),
        cost=(8 * n * rows * HD, n * rows),
    )
    atts = to_grp(att)

    index = jnp.arange(reqs, dtype=jnp.int32)
    groups = tie(group_of, att)
    same = groups[None, :] == groups[:, None]
    rank = jnp.sum(jnp.where(same & (index[None, :] < index[:, None]), 1, 0), axis=1)
    place = groups * SLOTS_R + rank
    pick = (place[:, None] == jnp.arange(count * SLOTS_R, dtype=jnp.int32)[None, :]).astype(BF16)
    steps = 8
    depth = shard_width // steps
    (proj,) = call(
        functools.partial(project_kernel, count),
        (),
        (pick, atts, out_weight),
        (shape((reqs, columns), BF16),),
        in_specs=[vmem, vmem, anywhere],
        scratch=(
            pltpu.VMEM((steps, depth, columns), BF16),
            pltpu.VMEM((steps, reqs, depth), BF16),
            dma((steps,)),
        ),
        cost=(2 * reqs * shard_width * columns, 0),
        vmem=STREAM + 3,
    )
    projs = to_seq(proj)
    if n > 2:
        pieces.append(up(pieces[-1], 2, projs[1:]))

    hidden_shard = gate_weight.shape[1]
    width = hidden_shard // count
    resid, terms = call(
        functools.partial(gate_up_kernel, n, count),
        (),
        (*projs, hidden_new, norm_gain.reshape(1, -1), gate_weight, up_weight),
        [shape((reqs, columns), F32), shape((count, reqs, 2 * width + HD), BF16)],
        in_specs=[vmem] * (n + 2) + [anywhere] * 2,
        scratch=(
            pltpu.VMEM(gate_weight.shape, BF16),
            pltpu.VMEM(up_weight.shape, BF16),
            dma((2 * count,)),
        ),
        cost=(4 * reqs * columns * hidden_shard, 0),
        vmem=STREAM,
    )
    terms = to_grp(terms)
    (hidden,) = call(
        functools.partial(hidden_kernel, count, columns * count),
        (),
        (terms,),
        (shape((count, reqs, width), BF16),),
        cost=(8 * count * reqs * width, reqs * width),
    )
    if n > 3:
        pieces.append(up(pieces[-1], 3, hidden))
    hiddens = to_grp(hidden)
    share = columns // n
    downs = call(
        functools.partial(down_kernel, count, n),
        scalars,
        (hiddens, down_weight),
        [shape((reqs, share), F32)] * n,
        in_specs=[vmem, anywhere],
        scratch=(pltpu.VMEM((count, width, columns), BF16), dma((count,))),
        cost=(2 * reqs * columns * hidden_shard, 0),
        vmem=STREAM,
    )
    total = lax.dynamic_slice_in_dim(resid, seq * share, share, 1) + downs[0]
    arrived = [shift(downs[t], "seq", n, t) for t in range(1, n)]
    for part in arrived:
        total = total + part
    decode_hidden = total.astype(BF16)
    for step in range(len(pieces), n):
        pieces.append(up(pieces[-1], step, pieces[-1]))

    first = jnp.sum(jnp.where(same & (index[None, :] < index[:, None]), lengths[None, :], 0), axis=1)
    row_first = seq * tokens
    meets = (group_of == group) & (first + lengths > row_first) & (first < row_first + tokens)
    lowest = jnp.min(jnp.where(meets, first, row_first + tokens))
    scalars = (jnp.concatenate([facts, (seq - lax.div(lowest, tokens) + 1)[None]]),)
    wide = Q_PER_KV * HD
    (prefill,) = call(
        functools.partial(prefill_kernel, n),
        scalars,
        (query_pre, *pieces),
        (shape(query_pre.shape, BF16),),
        in_specs=[anywhere] * (1 + n),
        out_specs=[anywhere],
        scratch=[
            pltpu.VMEM((kv_heads, tokens, wide), BF16),
            pltpu.VMEM((n, kv_heads * HD, tokens), BF16),
            pltpu.VMEM((n, kv_heads * HD, tokens), BF16),
            pltpu.VMEM((kv_heads, n * tokens, 2 * HD), BF16),
            pltpu.VMEM((tokens, n * tokens), F32),
            pltpu.VMEM((kv_heads, tokens, wide), BF16),
        ]
        + [pltpu.VMEM((tokens, n * tokens), F32)] * 2
        + [pltpu.VMEM((tokens, n * tokens), BF16)] * 2
        + [dma((kv_heads,)), dma((2, n)), dma((kv_heads,))],
        cost=(8 * n * tokens * query_pre.size, n * tokens * query_pre.size // HD),
        vmem=STREAM + 3,
    )
    return (prefill, decode_hidden)


def solution(mesh):
    return jax.shard_map(
        shards,
        mesh=mesh,
        in_specs=(
            P(),
            P(),
            P(("grp", "seq"), None),
            P(("grp", "seq"), None),
            P(("grp", "seq"), None),
            P(None, "seq"),
            P(None, "seq"),
            P(None, "seq"),
            P(None, "grp"),
            P("seq", "grp"),
            P("grp"),
            P("grp", "seq"),
            P("grp", "seq"),
            P("seq", "grp"),
        ),
        out_specs=(P(("grp", "seq"), None), P(None, ("grp", "seq"))),
        check_vma=False,
    )
```

```python
import functools
import math

import jax
import jax.numpy as jnp
from jax import lax
from jax.experimental import pallas as pl
from jax.experimental.pallas import tpu as pltpu
from jax.sharding import PartitionSpec as P

HD = 128
Q_PER_KV = 8
MAX_IN_GROUP = 3
SLOTS_R = 4
NEGATIVE = -1e30
LOG2E = 1.4426950408889634
MIB = 1 << 20
STREAM = 57

F32 = jnp.float32
BF16 = jnp.bfloat16


def dot(a, b):
    return jnp.dot(a, b, preferred_element_type=F32)


def dot_t(a, b):
    return lax.dot_general(a, b, (((1,), (1,)), ((), ())), preferred_element_type=F32)


def plan(facts):
    group = facts[0]
    reqs = (facts.shape[0] - 2) // 2
    ids = [jnp.int32(-1)] * MAX_IN_GROUP
    first = [jnp.int32(0)] * MAX_IN_GROUP
    end = [jnp.int32(0)] * MAX_IN_GROUP
    count = jnp.int32(0)
    used = jnp.int32(0)
    for r in range(reqs):
        mine = facts[2 + r] == group
        length = facts[2 + reqs + r]
        for k in range(MAX_IN_GROUP):
            here = mine & (count == k)
            ids[k] = jnp.where(here, r, ids[k])
            first[k] = jnp.where(here, used, first[k])
            end[k] = jnp.where(here, used + length, end[k])
        count = count + jnp.where(mine, 1, 0)
        used = used + jnp.where(mine, length, 0)
    return ids, first, end


def pick_rows(ids, rows, columns):
    row = lax.broadcasted_iota(jnp.int32, (rows, columns), 0)
    column = lax.broadcasted_iota(jnp.int32, (rows, columns), 1)
    target = jnp.full((rows, columns), -1, jnp.int32)
    for k in range(MAX_IN_GROUP):
        target = jnp.where(row == k, ids[k], target)
    return jnp.where(column == target, 1.0, 0.0).astype(BF16)


def split3(x):
    hi = x.astype(BF16)
    rest = x - hi.astype(F32)
    mid = rest.astype(BF16)
    low = (rest - mid.astype(F32)).astype(BF16)
    return hi, mid, low


def by_head(array, group):
    heads = array.shape[1] // HD * group
    return jnp.concatenate([array[:, (h // group) * HD :][:, :HD] for h in range(heads)], axis=0)


def spread(x, lane):
    hi, mid, low = split3(jnp.broadcast_to(x, x.shape[:-1] + (HD,)))
    return jnp.where(
        lane < 32, hi.astype(F32), jnp.where(lane < 64, mid.astype(F32), low.astype(F32))
    ).astype(BF16)


def gathered(stats):
    return stats[..., 0:1] + stats[..., 32:33] + stats[..., 64:65]


def select_kernel(facts, new_ref, query_ref, own_ref):
    ids, _, _ = plan(facts)
    width = query_ref.shape[1]
    kv_width = (new_ref.shape[1] - width) // 2
    new = dot(pick_rows(ids, 8, new_ref.shape[0]), new_ref[...])[:SLOTS_R]
    query_ref[...] = new[:, :width].astype(BF16)
    keys = by_head(new[:, width : width + kv_width], Q_PER_KV)
    values = by_head(new[:, width + kv_width :], Q_PER_KV)
    score = jnp.sum(by_head(new[:, :width], 1) * keys, axis=1, keepdims=True)
    own_ref[:, :HD] = values
    own_ref[:, HD:] = jnp.broadcast_to(score * (1.0 / math.sqrt(HD)), values.shape)


def partial_kernel(n, facts, *refs):
    queries, cache_ref, outs = refs[:n], refs[n], refs[n + 1 : 2 * n + 1]
    query_ref, out_ref = refs[2 * n + 1 :]
    _, first, end = plan(facts)
    tokens = cache_ref.shape[0] // 2
    kv_per = queries[0].shape[1] // (HD * Q_PER_KV)
    rows = Q_PER_KV * SLOTS_R
    slot = facts[1] * tokens + lax.broadcasted_iota(jnp.int32, (rows, tokens), 1)
    rank = lax.broadcasted_iota(jnp.int32, (rows, tokens), 0) & (SLOTS_R - 1)
    low = jnp.zeros((rows, tokens), jnp.int32)
    high = jnp.zeros((rows, tokens), jnp.int32)
    for k in range(MAX_IN_GROUP):
        low = jnp.where(rank == k, first[k], low)
        high = jnp.where(rank == k, end[k], high)
    allowed = (slot >= low) & (slot < high)
    lane = lax.broadcasted_iota(jnp.int32, (rows, HD), 1)
    scale = 1.0 / math.sqrt(HD)
    for t in range(n):
        query_ref[t] = queries[t][...].astype(F32)

    def head(j, carry):
        t = j // kv_per
        i = j - t * kv_per
        shard = lax.rem(facts[1] - t + n, n)
        columns = pl.ds(pl.multiple_of((shard * kv_per + i) * HD, HD), HD)
        width = Q_PER_KV * HD
        query = query_ref[t, :, pl.ds(pl.multiple_of(i * width, width), width)]
        scores = dot_t(by_head(query, 1).astype(BF16), cache_ref[:tokens, columns]) * scale
        scores = jnp.where(allowed, scores, NEGATIVE)
        top = jnp.max(scores, axis=1, keepdims=True)
        weights = jnp.where(allowed, jnp.exp(scores - top), 0.0)
        total = jnp.sum(weights, axis=1, keepdims=True)
        some = total > 0.0
        mixed = dot(weights.astype(BF16), cache_ref[tokens:, columns]) / jnp.where(some, total, 1.0)
        level = jnp.where(some, top + jnp.log(jnp.where(some, total, 1.0)), NEGATIVE)
        out_ref[t, pl.ds(pl.multiple_of(i * rows, rows), rows), :] = jnp.concatenate(
            [mixed.astype(BF16), spread(level, lane)], axis=1
        )
        return carry

    lax.fori_loop(0, n * kv_per, head, 0)
    for t in range(n):
        outs[t][...] = out_ref[t]


def combine_kernel(n, count, *refs):
    parts, own_ref, out_ref = refs[:n], refs[n], refs[n + 1]
    own_value = own_ref[:, :HD]
    own_score = own_ref[:, HD : HD + 1]
    mixes = []
    levels = []
    top = own_score
    for t in range(n):
        part = parts[t][...].astype(F32)
        stats = part[:, HD:]
        level = stats[:, 0:1] + stats[:, 32:33] + stats[:, 64:65]
        mixes.append(part[:, :HD])
        levels.append(level)
        top = jnp.maximum(top, level)
    own_weight = jnp.exp(own_score - top)
    total = own_weight
    mixed = own_weight.astype(BF16).astype(F32) * own_value
    for t in range(n):
        weight = jnp.exp(levels[t] - top)
        total = total + weight
        mixed = mixed + weight * mixes[t]
    result = mixed / total
    for h in range(out_ref.shape[2] // HD):
        head = result[h * SLOTS_R : (h + 1) * SLOTS_R].astype(BF16)
        for g in range(count):
            out_ref[g, :, h * HD : (h + 1) * HD] = head


def start_all(pairs, sems):
    copies = [
        pltpu.make_async_copy(source, target, sems.at[i]) for i, (source, target) in enumerate(pairs)
    ]
    for copy in copies:
        copy.start()
    return copies


def project_kernel(count, pick_ref, parts_ref, weight_ref, out_ref, buffer_ref, att_ref, sems):
    steps, _, depth = att_ref.shape

    def copy(j):
        rows = pl.ds(pl.multiple_of(j * depth, depth), depth)
        return pltpu.make_async_copy(weight_ref.at[rows], buffer_ref.at[j], sems.at[j])

    for j in range(steps):
        copy(j).start()
    stacked = jnp.concatenate([parts_ref[g].astype(F32) for g in range(count)], axis=0)
    att = dot(pick_ref[...], stacked.astype(BF16)).astype(BF16)
    for j in range(steps):
        att_ref[j] = att[:, j * depth : (j + 1) * depth]

    def block(j, total):
        copy(j).wait()
        return total + dot(att_ref[j], buffer_ref[j])

    total = lax.fori_loop(0, steps, block, jnp.zeros(out_ref.shape, F32))
    out_ref[...] = total.astype(out_ref.dtype)


def gate_up_kernel(n, count, *refs):
    parts = refs[:n]
    hidden_ref, gain_ref, gate_ref, up_ref, resid_ref, send_ref, gates_ref, ups_ref, sems = refs[n:]
    width = gate_ref.shape[1] // count
    blocks = [pl.ds(g * width, width) for g in range(count)]
    pairs = []
    for b in blocks:
        pairs.append((gate_ref.at[:, b], gates_ref.at[:, b]))
        pairs.append((up_ref.at[:, b], ups_ref.at[:, b]))
    copies = start_all(pairs, sems)
    resid = parts[0][...].astype(F32)
    for part in parts[1:]:
        resid = resid + part[...].astype(F32)
    resid = resid + hidden_ref[...].astype(F32)
    resid_ref[...] = resid
    scaled = (resid * gain_ref[...].astype(F32)).astype(BF16)
    squares = jnp.sum(resid * resid, axis=1, keepdims=True)
    rows = resid.shape[0]
    hi, mid, low = split3(jnp.broadcast_to(squares, (rows, HD)))
    lane = lax.broadcasted_iota(jnp.int32, (rows, HD), 1)
    stats = jnp.where(
        lane < 32, hi.astype(F32), jnp.where(lane < 64, mid.astype(F32), low.astype(F32))
    ).astype(BF16)
    for g in range(count):
        send_ref[g, :, 2 * width :] = stats
    for g in range(count):
        copies[2 * g].wait()
        send_ref[g, :, :width] = dot(scaled, gates_ref[:, blocks[g]]).astype(BF16)
        copies[2 * g + 1].wait()
        send_ref[g, :, width : 2 * width] = dot(scaled, ups_ref[:, blocks[g]]).astype(BF16)


def hidden_kernel(count, features, parts_ref, out_ref):
    width = out_ref.shape[2]
    total = parts_ref[0].astype(F32)
    for g in range(1, count):
        total = total + parts_ref[g].astype(F32)
    stats = total[:, 2 * width :]
    squares = stats[:, 0:1] + stats[:, 32:33] + stats[:, 64:65]
    inverse = lax.rsqrt(squares / features + 1e-05)
    gate = total[:, :width] * inverse
    upper = total[:, width : 2 * width] * inverse
    hidden = (gate / (1.0 + jnp.exp(-gate)) * upper).astype(BF16)
    for g in range(count):
        out_ref[g] = hidden


def down_kernel(count, n, facts, parts_ref, weight_ref, *refs):
    sends, buffer_ref, sems = refs[:n], refs[n], refs[n + 1]
    depth = buffer_ref.shape[1]
    width = sends[0].shape[1]

    def copy(g):
        rows = pl.ds(pl.multiple_of(g * depth, depth), depth)
        return pltpu.make_async_copy(weight_ref.at[rows], buffer_ref.at[g], sems.at[g])

    for g in range(count):
        copy(g).start()

    def block(g, total):
        copy(g).wait()
        return total + dot(parts_ref[g], buffer_ref[g])

    shape = (sends[0].shape[0], weight_ref.shape[1])
    total = lax.fori_loop(0, count, block, jnp.zeros(shape, F32))
    for own in range(n):

        @pl.when(facts[1] == own)
        def _():
            for t in range(n):
                target = (own + t) % n
                sends[t][...] = total[:, target * width : (target + 1) * width]


def row_facts(facts, tokens):
    _, first, end = plan(facts)
    return facts[1] * tokens, facts[facts.shape[0] - 1], first, end


def live_rows(row_first, first, end, tokens):
    row = row_first + lax.broadcasted_iota(jnp.int32, (tokens, HD), 0)
    live = row < 0
    for k in range(MAX_IN_GROUP):
        live = live | ((row >= first[k]) & (row < end[k]))
    return live


def store_bias(bias_ref, row_first, first, end, pieces):
    tokens = bias_ref.shape[0]
    row = row_first + lax.broadcasted_iota(jnp.int32, (tokens, tokens), 0)
    column = lax.broadcasted_iota(jnp.int32, (tokens, tokens), 1)
    low = jnp.full((tokens, tokens), 1 << 30, jnp.int32)
    for k in range(MAX_IN_GROUP):
        low = jnp.where((row >= first[k]) & (row < end[k]), first[k], low)
    for place, t in enumerate(pieces):
        slot = row_first - t * tokens + column
        bias_ref[:, place * tokens : (place + 1) * tokens] = jnp.where(
            (slot >= low) & (slot <= row), 0.0, NEGATIVE
        )


EXP2 = LOG2E / math.sqrt(HD)


def inverse_of(x):
    guess = pl.reciprocal(x, approx=True)
    return guess * (2.0 - x * guess)


def interleave(*tasks):
    order = sorted(
        ((k + 0.5) / len(task), which, step)
        for which, task in enumerate(tasks)
        for k, step in enumerate(range(len(task)))
    )
    for _, which, step in order:
        tasks[which][step]()


def prefill_kernel(n, facts, *refs):
    query_hbm, own, pieces, out_hbm = refs[0], refs[1:3], refs[3 : 2 + n], refs[2 + n]
    query_ref, key_ref, value_ref, wide_ref, bias_ref, out_ref = refs[3 + n : 9 + n]
    scores, weights, (query_sems, piece_sems, out_sems) = (
        refs[9 + n : 11 + n],
        refs[11 + n : 13 + n],
        refs[13 + n :],
    )
    tokens = query_ref.shape[1]
    kv_heads = query_ref.shape[0]
    row_first, needed, first, end = row_facts(facts, tokens)

    def columns(kv):
        width = Q_PER_KV * HD
        return pl.ds(pl.multiple_of(kv * width, width), width)

    def query_copy(kv):
        return pltpu.make_async_copy(
            query_hbm.at[:, columns(kv)], query_ref.at[kv], query_sems.at[kv]
        )

    def out_copy(kv):
        return pltpu.make_async_copy(out_ref.at[kv], out_hbm.at[:, columns(kv)], out_sems.at[kv])

    @pl.when(needed == 0)
    def _():
        out_ref[...] = jnp.zeros_like(out_ref)
        for kv in range(kv_heads):
            out_copy(kv).start()
        for kv in range(kv_heads):
            out_copy(kv).wait()

    def run(count, lone):
        slots = count * tokens
        chunk = 64
        copies = []
        for t in range(count):
            for part, target in enumerate((key_ref, value_ref)):
                source = own[part] if t == 0 else pieces[t - 1].at[pl.ds(part * tokens, tokens)]
                copies.append(
                    pltpu.make_async_copy(source, target.at[t], piece_sems.at[part, t])
                )
        for copy in copies:
            copy.start()
        query_copy(0).start()
        store_bias(bias_ref, row_first, first, end, range(count))
        live = None if lone else live_rows(row_first, first, end, tokens)
        for copy in copies:
            copy.wait()
        for kv in range(1, kv_heads):
            query_copy(kv).start()

        def widen(kv, carry):
            lanes = pl.ds(pl.multiple_of(kv * HD, HD), HD)
            for t in range(count):
                rows = slice(t * tokens, (t + 1) * tokens)
                wide_ref[kv, rows, :HD] = value_ref[t, :, lanes]
                wide_ref[kv, rows, HD:] = jnp.ones((tokens, HD), BF16)
            return carry

        lax.fori_loop(0, kv_heads, widen, 0)

        def place(h):
            kv = h // Q_PER_KV
            return kv, pl.ds(pl.multiple_of((h - kv * Q_PER_KV) * HD, HD), HD)

        def score_steps(h, slot):
            kv, lanes = place(h)
            features = pl.ds(pl.multiple_of(kv * HD, HD), HD)

            def step(t):
                scores[slot][:, t * tokens : (t + 1) * tokens] = dot_t(
                    query_ref[kv, :, lanes], key_ref[t, :, features]
                )

            return [functools.partial(step, t) for t in range(count)]

        def weight_steps(slot):
            tops = {}

            def part(at, t):
                piece = slice(t * tokens, (t + 1) * tokens)
                score = scores[slot][at : at + chunk, piece]
                if lone and t > 0:
                    return score
                return score + bias_ref[at : at + chunk, piece]

            def top_step(at):
                most = part(at, 0)
                for t in range(1, count):
                    most = jnp.maximum(most, part(at, t))
                tops[at] = jnp.max(most, axis=1, keepdims=True)

            def weight_step(at):
                top = tops.pop(at)
                for t in range(count):
                    weights[slot][at : at + chunk, t * tokens : (t + 1) * tokens] = jnp.exp2(
                        (part(at, t) - top) * EXP2
                    ).astype(BF16)

            starts = list(range(0, tokens, chunk))
            steps = [functools.partial(top_step, at) for at in starts[:2]]
            for i, at in enumerate(starts):
                steps.append(functools.partial(weight_step, at))
                if i + 2 < len(starts):
                    steps.append(functools.partial(top_step, starts[i + 2]))
            return steps

        def value_steps(h, slot):
            kv, lanes = place(h)

            def step(at):
                rows = slice(at, at + tokens // 2)
                mixed = dot(weights[slot][rows, :slots], wide_ref[kv, :slots])
                result = mixed[:, :HD] * inverse_of(mixed[:, HD:])
                if not lone:
                    result = jnp.where(live[rows], result, 0.0)
                out_ref[kv, rows, lanes] = result.astype(BF16)

            return [functools.partial(step, at) for at in range(0, tokens, tokens // 2)]

        last = kv_heads * Q_PER_KV - 1
        query_copy(0).wait()
        interleave(score_steps(jnp.int32(0), 0))
        interleave(score_steps(jnp.int32(1), 1), weight_steps(0))

        def kv_step(kv, carry):
            @pl.when(kv + 1 < kv_heads)
            def _():
                query_copy(kv + 1).wait()

            def two_heads(j, inner):
                for slot in range(2):
                    h = kv * Q_PER_KV + 2 * j + slot
                    interleave(
                        score_steps(jnp.minimum(h + 2, last), slot),
                        weight_steps(1 - slot),
                        value_steps(h, slot),
                    )
                return inner

            lax.fori_loop(0, Q_PER_KV // 2, two_heads, 0)
            out_copy(kv).start()
            return carry

        lax.fori_loop(0, kv_heads, kv_step, 0)
        for kv in range(kv_heads):
            out_copy(kv).wait()

    lone = needed < 0
    for k in range(MAX_IN_GROUP):
        lone = lone | (
            (first[k] <= row_first - (needed - 1) * tokens) & (end[k] >= row_first + tokens)
        )
    before = 0
    for count in sorted({c for c in (1, 2, 3, n) if c <= n}):
        here = (needed > before) & (needed <= count)
        exact = (needed == count) & lone
        before = count

        @pl.when(exact)
        def _():
            run(count, True)

        @pl.when(here & jnp.logical_not(exact))
        def _():
            run(count, False)


def call(body, scalars, args, outs, *, grid=None, in_specs=None, out_specs=None, scratch=(), cost, vmem=6, aliases=None):
    whole = pl.BlockSpec(memory_space=pltpu.VMEM)
    if grid is None:
        grid = (1,)
    flops, exps = cost
    moved = sum(a.size * a.dtype.itemsize for a in args) + sum(
        o.size * o.dtype.itemsize for o in outs
    )
    return pl.pallas_call(
        body,
        out_shape=list(outs),
        grid_spec=pltpu.PrefetchScalarGridSpec(
            num_scalar_prefetch=len(scalars),
            grid=grid,
            in_specs=in_specs or [whole] * len(args),
            out_specs=out_specs or [whole] * len(outs),
            scratch_shapes=list(scratch),
        ),
        compiler_params=pltpu.CompilerParams(
            dimension_semantics=("arbitrary",) * len(grid), vmem_limit_bytes=int(vmem * MIB)
        ),
        input_output_aliases=aliases or {},
        cost_estimate=pl.CostEstimate(flops=flops, bytes_accessed=moved, transcendentals=exps),
    )(*scalars, *args)


def shift(x, axis, count, t):
    return lax.ppermute(x, axis, [(i, (i + t) % count) for i in range(count)])


def shards(
    lengths,
    group_of,
    query_pre,
    key_pre,
    value_pre,
    query_new,
    key_new,
    value_new,
    hidden_new,
    out_weight,
    norm_gain,
    gate_weight,
    up_weight,
    down_weight,
):
    n = lax.axis_size("seq")
    count = lax.axis_size("grp")
    seq = lax.axis_index("seq").astype(jnp.int32)
    group = lax.axis_index("grp").astype(jnp.int32)
    tokens = query_pre.shape[0]
    reqs = query_new.shape[0]
    kv_heads = key_pre.shape[1] // HD
    shard_width = query_new.shape[1]
    shard_heads = shard_width // HD
    columns = out_weight.shape[1]
    shape = jax.ShapeDtypeStruct
    vmem = pl.BlockSpec(memory_space=pltpu.VMEM)
    anywhere = pl.BlockSpec(memory_space=pl.ANY)
    dma = pltpu.SemaphoreType.DMA
    facts = jnp.concatenate([jnp.stack([group, seq]), group_of, lengths])
    scalars = (facts,)

    def to_seq(x):
        return [x] + [shift(x, "seq", n, t) for t in range(1, n)]

    def to_grp(x):
        return lax.all_to_all(x, "grp", split_axis=0, concat_axis=0, tiled=True)

    def tie(x, after):
        return lax.optimization_barrier((x, after))[0]

    def up(x, step, after):
        return lax.ppermute(tie(x, after), "seq", [(i, i + 1) for i in range(step - 1, n - 1)])

    pieces = [jnp.concatenate([key_pre, value_pre], axis=0)]

    query, own = call(
        select_kernel,
        scalars,
        (jnp.concatenate([query_new, key_new, value_new], axis=1),),
        (shape((SLOTS_R, shard_width), BF16), shape((shard_heads * SLOTS_R, 2 * HD), F32)),
        cost=(2 * 8 * reqs * shard_width, 0),
    )
    queries = to_seq(query)
    rows = shard_heads * SLOTS_R
    partials = call(
        functools.partial(partial_kernel, n),
        scalars,
        (*queries, pieces[0]),
        [shape((rows, 2 * HD), BF16)] * n,
        scratch=(
            pltpu.VMEM((n, SLOTS_R, shard_width), F32),
            pltpu.VMEM((n, rows, 2 * HD), BF16),
        ),
        cost=(4 * n * rows * tokens * HD, n * rows * tokens),
    )
    partials = [partials[0]] + [shift(partials[t], "seq", n, n - t) for t in range(1, n)]
    pieces.append(up(pieces[-1], 1, partials[1:]))
    (att,) = call(
        functools.partial(combine_kernel, n, count),
        (),
        (*partials, own),
        (shape((count, SLOTS_R, shard_width), BF16),),
        cost=(8 * n * rows * HD, n * rows),
    )
    atts = to_grp(att)

    index = jnp.arange(reqs, dtype=jnp.int32)
    groups = tie(group_of, att)
    same = groups[None, :] == groups[:, None]
    rank = jnp.sum(jnp.where(same & (index[None, :] < index[:, None]), 1, 0), axis=1)
    place = groups * SLOTS_R + rank
    pick = (place[:, None] == jnp.arange(count * SLOTS_R, dtype=jnp.int32)[None, :]).astype(BF16)
    steps = 8
    depth = shard_width // steps
    (proj,) = call(
        functools.partial(project_kernel, count),
        (),
        (pick, atts, out_weight),
        (shape((reqs, columns), BF16),),
        in_specs=[vmem, vmem, anywhere],
        scratch=(
            pltpu.VMEM((steps, depth, columns), BF16),
            pltpu.VMEM((steps, reqs, depth), BF16),
            dma((steps,)),
        ),
        cost=(2 * reqs * shard_width * columns, 0),
        vmem=STREAM + 3,
    )
    projs = to_seq(proj)
    if n > 2:
        pieces.append(up(pieces[-1], 2, projs[1:]))

    hidden_shard = gate_weight.shape[1]
    width = hidden_shard // count
    resid, terms = call(
        functools.partial(gate_up_kernel, n, count),
        (),
        (*projs, hidden_new, norm_gain.reshape(1, -1), gate_weight, up_weight),
        [shape((reqs, columns), F32), shape((count, reqs, 2 * width + HD), BF16)],
        in_specs=[vmem] * (n + 2) + [anywhere] * 2,
        scratch=(
            pltpu.VMEM(gate_weight.shape, BF16),
            pltpu.VMEM(up_weight.shape, BF16),
            dma((2 * count,)),
        ),
        cost=(4 * reqs * columns * hidden_shard, 0),
        vmem=STREAM,
    )
    terms = to_grp(terms)
    (hidden,) = call(
        functools.partial(hidden_kernel, count, columns * count),
        (),
        (terms,),
        (shape((count, reqs, width), BF16),),
        cost=(8 * count * reqs * width, reqs * width),
    )
    if n > 3:
        pieces.append(up(pieces[-1], 3, hidden))
    hiddens = to_grp(hidden)
    share = columns // n
    downs = call(
        functools.partial(down_kernel, count, n),
        scalars,
        (hiddens, down_weight),
        [shape((reqs, share), F32)] * n,
        in_specs=[vmem, anywhere],
        scratch=(pltpu.VMEM((count, width, columns), BF16), dma((count,))),
        cost=(2 * reqs * columns * hidden_shard, 0),
        vmem=STREAM,
    )
    total = lax.dynamic_slice_in_dim(resid, seq * share, share, 1) + downs[0]
    arrived = [shift(downs[t], "seq", n, t) for t in range(1, n)]
    for part in arrived:
        total = total + part
    decode_hidden = total.astype(BF16)
    for step in range(len(pieces), n):
        pieces.append(up(pieces[-1], step, pieces[-1]))

    first = jnp.sum(jnp.where(same & (index[None, :] < index[:, None]), lengths[None, :], 0), axis=1)
    row_first = seq * tokens
    meets = (group_of == group) & (first + lengths > row_first) & (first < row_first + tokens)
    lowest = jnp.min(jnp.where(meets, first, row_first + tokens))
    scalars = (jnp.concatenate([facts, (seq - lax.div(lowest, tokens) + 1)[None]]),)
    wide = Q_PER_KV * HD
    (prefill,) = call(
        functools.partial(prefill_kernel, n),
        scalars,
        (query_pre, key_pre, value_pre, *pieces[1:]),
        (shape(query_pre.shape, BF16),),
        in_specs=[anywhere] * (2 + n),
        out_specs=[anywhere],
        scratch=[
            pltpu.VMEM((kv_heads, tokens, wide), BF16),
            pltpu.VMEM((n, tokens, kv_heads * HD), BF16),
            pltpu.VMEM((n, tokens, kv_heads * HD), BF16),
            pltpu.VMEM((kv_heads, n * tokens, 2 * HD), BF16),
            pltpu.VMEM((tokens, n * tokens), F32),
            pltpu.VMEM((kv_heads, tokens, wide), BF16),
        ]
        + [pltpu.VMEM((tokens, n * tokens), F32)] * 2
        + [pltpu.VMEM((tokens, n * tokens), BF16)] * 2
        + [dma((kv_heads,)), dma((2, n)), dma((kv_heads,))],
        cost=(8 * n * tokens * query_pre.size, n * tokens * query_pre.size // HD),
        vmem=STREAM + 3,
    )
    return (prefill, decode_hidden)


def solution(mesh):
    return jax.shard_map(
        shards,
        mesh=mesh,
        in_specs=(
            P(),
            P(),
            P(("grp", "seq"), None),
            P(("grp", "seq"), None),
            P(("grp", "seq"), None),
            P(None, "seq"),
            P(None, "seq"),
            P(None, "seq"),
            P(None, "grp"),
            P("seq", "grp"),
            P("grp"),
            P("grp", "seq"),
            P("grp", "seq"),
            P("seq", "grp"),
        ),
        out_specs=(P(("grp", "seq"), None), P(None, ("grp", "seq"))),
        check_vma=False,
    )
```

```python
import functools
import math

import jax
import jax.numpy as jnp
from jax import lax
from jax.experimental import pallas as pl
from jax.experimental.pallas import tpu as pltpu
from jax.sharding import PartitionSpec as P

HD = 128
Q_PER_KV = 8
MAX_IN_GROUP = 3
SLOTS_R = 4
NEGATIVE = -1e30
LOG2E = 1.4426950408889634
MIB = 1 << 20
STREAM = 57

F32 = jnp.float32
BF16 = jnp.bfloat16


def dot(a, b):
    return jnp.dot(a, b, preferred_element_type=F32)


def dot_t(a, b):
    return lax.dot_general(a, b, (((1,), (1,)), ((), ())), preferred_element_type=F32)


def plan(facts):
    group = facts[0]
    reqs = (facts.shape[0] - 2) // 2
    ids = [jnp.int32(-1)] * MAX_IN_GROUP
    first = [jnp.int32(0)] * MAX_IN_GROUP
    end = [jnp.int32(0)] * MAX_IN_GROUP
    count = jnp.int32(0)
    used = jnp.int32(0)
    for r in range(reqs):
        mine = facts[2 + r] == group
        length = facts[2 + reqs + r]
        for k in range(MAX_IN_GROUP):
            here = mine & (count == k)
            ids[k] = jnp.where(here, r, ids[k])
            first[k] = jnp.where(here, used, first[k])
            end[k] = jnp.where(here, used + length, end[k])
        count = count + jnp.where(mine, 1, 0)
        used = used + jnp.where(mine, length, 0)
    return ids, first, end


def pick_rows(ids, rows, columns):
    row = lax.broadcasted_iota(jnp.int32, (rows, columns), 0)
    column = lax.broadcasted_iota(jnp.int32, (rows, columns), 1)
    target = jnp.full((rows, columns), -1, jnp.int32)
    for k in range(MAX_IN_GROUP):
        target = jnp.where(row == k, ids[k], target)
    return jnp.where(column == target, 1.0, 0.0).astype(BF16)


def split3(x):
    hi = x.astype(BF16)
    rest = x - hi.astype(F32)
    mid = rest.astype(BF16)
    low = (rest - mid.astype(F32)).astype(BF16)
    return hi, mid, low


def by_head(array, group):
    heads = array.shape[1] // HD * group
    return jnp.concatenate([array[:, (h // group) * HD :][:, :HD] for h in range(heads)], axis=0)


def spread(x, lane):
    hi, mid, low = split3(jnp.broadcast_to(x, x.shape[:-1] + (HD,)))
    return jnp.where(
        lane < 32, hi.astype(F32), jnp.where(lane < 64, mid.astype(F32), low.astype(F32))
    ).astype(BF16)


def gathered(stats):
    return stats[..., 0:1] + stats[..., 32:33] + stats[..., 64:65]


def select_kernel(facts, new_ref, query_ref, own_ref):
    ids, _, _ = plan(facts)
    width = query_ref.shape[1]
    kv_width = (new_ref.shape[1] - width) // 2
    new = dot(pick_rows(ids, 8, new_ref.shape[0]), new_ref[...])[:SLOTS_R]
    query_ref[...] = new[:, :width].astype(BF16)
    keys = by_head(new[:, width : width + kv_width], Q_PER_KV)
    values = by_head(new[:, width + kv_width :], Q_PER_KV)
    score = jnp.sum(by_head(new[:, :width], 1) * keys, axis=1, keepdims=True)
    own_ref[:, :HD] = values
    own_ref[:, HD:] = jnp.broadcast_to(score * (1.0 / math.sqrt(HD)), values.shape)


def pack_kernel(key_ref, value_ref, out_ref):
    tokens, width = key_ref.shape
    for at in range(0, width, HD):
        keys = key_ref[:, at : at + HD].astype(F32)
        out_ref[at : at + HD, :] = jnp.transpose(keys).astype(BF16)
    for at in range(0, width, tokens):
        out_ref[width + at : width + at + tokens, :] = value_ref[:, at : at + tokens]


def value_place(kv, tokens):
    side = tokens // HD
    row = pl.multiple_of(kv // side * tokens, tokens)
    return row, pl.multiple_of(lax.rem(kv, side) * HD, HD)


def partial_kernel(n, facts, *refs):
    queries, cache_ref, outs = refs[:n], refs[n], refs[n + 1 : 2 * n + 1]
    query_ref, out_ref = refs[2 * n + 1 :]
    _, first, end = plan(facts)
    kv_width, tokens = cache_ref.shape[0] // 2, cache_ref.shape[1]
    kv_per = queries[0].shape[1] // (HD * Q_PER_KV)
    rows = Q_PER_KV * SLOTS_R
    slot = facts[1] * tokens + lax.broadcasted_iota(jnp.int32, (rows, tokens), 1)
    rank = lax.broadcasted_iota(jnp.int32, (rows, tokens), 0) & (SLOTS_R - 1)
    low = jnp.zeros((rows, tokens), jnp.int32)
    high = jnp.zeros((rows, tokens), jnp.int32)
    for k in range(MAX_IN_GROUP):
        low = jnp.where(rank == k, first[k], low)
        high = jnp.where(rank == k, end[k], high)
    allowed = (slot >= low) & (slot < high)
    lane = lax.broadcasted_iota(jnp.int32, (rows, HD), 1)
    scale = 1.0 / math.sqrt(HD)
    for t in range(n):
        query_ref[t] = queries[t][...].astype(F32)

    def head(j, carry):
        t = j // kv_per
        i = j - t * kv_per
        shard = lax.rem(facts[1] - t + n, n)
        kv = shard * kv_per + i
        keys = cache_ref[pl.ds(pl.multiple_of(kv * HD, HD), HD), :]
        row, lanes = value_place(kv, tokens)
        values = cache_ref[pl.ds(kv_width + row, tokens), pl.ds(lanes, HD)]
        width = Q_PER_KV * HD
        query = query_ref[t, :, pl.ds(pl.multiple_of(i * width, width), width)]
        scores = dot(by_head(query, 1).astype(BF16), keys) * scale
        scores = jnp.where(allowed, scores, NEGATIVE)
        top = jnp.max(scores, axis=1, keepdims=True)
        weights = jnp.where(allowed, jnp.exp(scores - top), 0.0)
        total = jnp.sum(weights, axis=1, keepdims=True)
        some = total > 0.0
        mixed = dot(weights.astype(BF16), values) / jnp.where(some, total, 1.0)
        level = jnp.where(some, top + jnp.log(jnp.where(some, total, 1.0)), NEGATIVE)
        out_ref[t, pl.ds(pl.multiple_of(i * rows, rows), rows), :] = jnp.concatenate(
            [mixed.astype(BF16), spread(level, lane)], axis=1
        )
        return carry

    lax.fori_loop(0, n * kv_per, head, 0)
    for t in range(n):
        outs[t][...] = out_ref[t]


def combine_kernel(n, count, *refs):
    parts, own_ref, out_ref = refs[:n], refs[n], refs[n + 1]
    own_value = own_ref[:, :HD]
    own_score = own_ref[:, HD : HD + 1]
    mixes = []
    levels = []
    top = own_score
    for t in range(n):
        part = parts[t][...].astype(F32)
        stats = part[:, HD:]
        level = stats[:, 0:1] + stats[:, 32:33] + stats[:, 64:65]
        mixes.append(part[:, :HD])
        levels.append(level)
        top = jnp.maximum(top, level)
    own_weight = jnp.exp(own_score - top)
    total = own_weight
    mixed = own_weight.astype(BF16).astype(F32) * own_value
    for t in range(n):
        weight = jnp.exp(levels[t] - top)
        total = total + weight
        mixed = mixed + weight * mixes[t]
    result = mixed / total
    for h in range(out_ref.shape[2] // HD):
        head = result[h * SLOTS_R : (h + 1) * SLOTS_R].astype(BF16)
        for g in range(count):
            out_ref[g, :, h * HD : (h + 1) * HD] = head


def start_all(pairs, sems):
    copies = [
        pltpu.make_async_copy(source, target, sems.at[i]) for i, (source, target) in enumerate(pairs)
    ]
    for copy in copies:
        copy.start()
    return copies


def project_kernel(count, pick_ref, parts_ref, weight_ref, out_ref, buffer_ref, att_ref, sems):
    steps, _, depth = att_ref.shape

    def copy(j):
        rows = pl.ds(pl.multiple_of(j * depth, depth), depth)
        return pltpu.make_async_copy(weight_ref.at[rows], buffer_ref.at[j], sems.at[j])

    for j in range(steps):
        copy(j).start()
    stacked = jnp.concatenate([parts_ref[g].astype(F32) for g in range(count)], axis=0)
    att = dot(pick_ref[...], stacked.astype(BF16)).astype(BF16)
    for j in range(steps):
        att_ref[j] = att[:, j * depth : (j + 1) * depth]

    def block(j, total):
        copy(j).wait()
        return total + dot(att_ref[j], buffer_ref[j])

    total = lax.fori_loop(0, steps, block, jnp.zeros(out_ref.shape, F32))
    out_ref[...] = total.astype(out_ref.dtype)


def gate_up_kernel(n, count, *refs):
    parts = refs[:n]
    hidden_ref, gain_ref, gate_ref, up_ref, resid_ref, send_ref, gates_ref, ups_ref, sems = refs[n:]
    width = gate_ref.shape[1] // count
    blocks = [pl.ds(g * width, width) for g in range(count)]
    pairs = []
    for b in blocks:
        pairs.append((gate_ref.at[:, b], gates_ref.at[:, b]))
        pairs.append((up_ref.at[:, b], ups_ref.at[:, b]))
    copies = start_all(pairs, sems)
    resid = parts[0][...].astype(F32)
    for part in parts[1:]:
        resid = resid + part[...].astype(F32)
    resid = resid + hidden_ref[...].astype(F32)
    resid_ref[...] = resid
    scaled = (resid * gain_ref[...].astype(F32)).astype(BF16)
    squares = jnp.sum(resid * resid, axis=1, keepdims=True)
    rows = resid.shape[0]
    hi, mid, low = split3(jnp.broadcast_to(squares, (rows, HD)))
    lane = lax.broadcasted_iota(jnp.int32, (rows, HD), 1)
    stats = jnp.where(
        lane < 32, hi.astype(F32), jnp.where(lane < 64, mid.astype(F32), low.astype(F32))
    ).astype(BF16)
    for g in range(count):
        send_ref[g, :, 2 * width :] = stats
    for g in range(count):
        copies[2 * g].wait()
        send_ref[g, :, :width] = dot(scaled, gates_ref[:, blocks[g]]).astype(BF16)
        copies[2 * g + 1].wait()
        send_ref[g, :, width : 2 * width] = dot(scaled, ups_ref[:, blocks[g]]).astype(BF16)


def hidden_kernel(count, features, parts_ref, out_ref):
    width = out_ref.shape[2]
    total = parts_ref[0].astype(F32)
    for g in range(1, count):
        total = total + parts_ref[g].astype(F32)
    stats = total[:, 2 * width :]
    squares = stats[:, 0:1] + stats[:, 32:33] + stats[:, 64:65]
    inverse = lax.rsqrt(squares / features + 1e-05)
    gate = total[:, :width] * inverse
    upper = total[:, width : 2 * width] * inverse
    hidden = (gate / (1.0 + jnp.exp(-gate)) * upper).astype(BF16)
    for g in range(count):
        out_ref[g] = hidden


def down_kernel(count, n, facts, parts_ref, resid_ref, weight_ref, *refs):
    sends, buffer_ref, sems = refs[:n], refs[n], refs[n + 1]
    depth = buffer_ref.shape[1]
    width = sends[0].shape[1]

    def copy(g):
        rows = pl.ds(pl.multiple_of(g * depth, depth), depth)
        return pltpu.make_async_copy(weight_ref.at[rows], buffer_ref.at[g], sems.at[g])

    for g in range(count):
        copy(g).start()

    def block(g, total):
        copy(g).wait()
        return total + dot(parts_ref[g], buffer_ref[g])

    shape = (sends[0].shape[0], weight_ref.shape[1])
    total = lax.fori_loop(0, count, block, jnp.zeros(shape, F32))
    for own in range(n):

        @pl.when(facts[1] == own)
        def _():
            for t in range(n):
                columns = slice((own + t) % n * width, ((own + t) % n + 1) * width)
                share = total[:, columns]
                sends[t][...] = share + resid_ref[:, columns] if t == 0 else share


def sum_kernel(*refs):
    total = refs[0][...]
    for ref in refs[1:-1]:
        total = total + ref[...]
    refs[-1][...] = total.astype(refs[-1].dtype)


def row_facts(facts, tokens):
    _, first, end = plan(facts)
    return facts[1] * tokens, facts[facts.shape[0] - 1], first, end


def live_rows(row_first, first, end, tokens):
    row = row_first + lax.broadcasted_iota(jnp.int32, (tokens, HD), 0)
    live = row < 0
    for k in range(MAX_IN_GROUP):
        live = live | ((row >= first[k]) & (row < end[k]))
    return live


def store_bias(bias_ref, row_first, first, end, pieces):
    tokens = bias_ref.shape[0]
    row = row_first + lax.broadcasted_iota(jnp.int32, (tokens, tokens), 0)
    column = lax.broadcasted_iota(jnp.int32, (tokens, tokens), 1)
    low = jnp.full((tokens, tokens), 1 << 30, jnp.int32)
    for k in range(MAX_IN_GROUP):
        low = jnp.where((row >= first[k]) & (row < end[k]), first[k], low)
    for place, t in enumerate(pieces):
        slot = row_first - t * tokens + column
        bias_ref[:, place * tokens : (place + 1) * tokens] = jnp.where(
            (slot >= low) & (slot <= row), 0.0, NEGATIVE
        )


EXP2 = LOG2E / math.sqrt(HD)


def inverse_of(x):
    guess = pl.reciprocal(x, approx=True)
    return guess * (2.0 - x * guess)


def interleave(*tasks):
    order = sorted(
        ((k + 0.5) / len(task), which, step)
        for which, task in enumerate(tasks)
        for k, step in enumerate(range(len(task)))
    )
    for _, which, step in order:
        tasks[which][step]()


def prefill_kernel(n, facts, *refs):
    query_hbm, pieces, out_hbm = refs[0], refs[1 : 1 + n], refs[1 + n]
    query_ref, key_ref, value_ref, wide_ref, bias_ref, out_ref = refs[2 + n : 8 + n]
    scores, weights, (query_sems, piece_sems, out_sems) = (
        refs[8 + n : 10 + n],
        refs[10 + n : 12 + n],
        refs[12 + n :],
    )
    tokens = query_ref.shape[1]
    kv_heads = query_ref.shape[0]
    kv_width = key_ref.shape[1]
    row_first, needed, first, end = row_facts(facts, tokens)

    def columns(kv):
        width = Q_PER_KV * HD
        return pl.ds(pl.multiple_of(kv * width, width), width)

    def query_copy(kv):
        return pltpu.make_async_copy(
            query_hbm.at[:, columns(kv)], query_ref.at[kv], query_sems.at[kv]
        )

    def out_copy(kv):
        return pltpu.make_async_copy(out_ref.at[kv], out_hbm.at[:, columns(kv)], out_sems.at[kv])

    @pl.when(needed == 0)
    def _():
        out_ref[...] = jnp.zeros_like(out_ref)
        for kv in range(kv_heads):
            out_copy(kv).start()
        for kv in range(kv_heads):
            out_copy(kv).wait()

    def run(count, lone):
        slots = count * tokens
        chunk = 64
        copies = []
        for t in range(count):
            for part, target in enumerate((key_ref, value_ref)):
                source = pieces[t].at[pl.ds(part * kv_width, kv_width)]
                copies.append(
                    pltpu.make_async_copy(source, target.at[t], piece_sems.at[part, t])
                )
        for copy in copies:
            copy.start()
        for kv in range(kv_heads):
            query_copy(kv).start()
        store_bias(bias_ref, row_first, first, end, range(count))
        live = None if lone else live_rows(row_first, first, end, tokens)
        for copy in copies:
            copy.wait()

        def widen(kv, carry):
            row, lanes = value_place(kv, tokens)
            for t in range(count):
                rows = slice(t * tokens, (t + 1) * tokens)
                wide_ref[kv, rows, :HD] = value_ref[t, pl.ds(row, tokens), pl.ds(lanes, HD)]
                wide_ref[kv, rows, HD:] = jnp.ones((tokens, HD), BF16)
            return carry

        lax.fori_loop(0, kv_heads, widen, 0)

        def place(h):
            kv = h // Q_PER_KV
            return kv, pl.ds(pl.multiple_of((h - kv * Q_PER_KV) * HD, HD), HD)

        def score_steps(h, slot):
            kv, lanes = place(h)
            features = pl.ds(pl.multiple_of(kv * HD, HD), HD)

            def step(t):
                scores[slot][:, t * tokens : (t + 1) * tokens] = dot(
                    query_ref[kv, :, lanes], key_ref[t, features, :]
                )

            return [functools.partial(step, t) for t in range(count)]

        def weight_steps(slot):
            tops = {}

            def part(at, t):
                piece = slice(t * tokens, (t + 1) * tokens)
                score = scores[slot][at : at + chunk, piece]
                if lone and t > 0:
                    return score
                return score + bias_ref[at : at + chunk, piece]

            def top_step(at):
                most = part(at, 0)
                for t in range(1, count):
                    most = jnp.maximum(most, part(at, t))
                tops[at] = jnp.max(most, axis=1, keepdims=True)

            def weight_step(at):
                top = tops.pop(at)
                for t in range(count):
                    weights[slot][at : at + chunk, t * tokens : (t + 1) * tokens] = jnp.exp2(
                        (part(at, t) - top) * EXP2
                    ).astype(BF16)

            starts = list(range(0, tokens, chunk))
            steps = [functools.partial(top_step, at) for at in starts[:2]]
            for i, at in enumerate(starts):
                steps.append(functools.partial(weight_step, at))
                if i + 2 < len(starts):
                    steps.append(functools.partial(top_step, starts[i + 2]))
            return steps

        def value_steps(h, slot):
            kv, lanes = place(h)

            def step(at):
                rows = slice(at, at + tokens // 2)
                mixed = dot(weights[slot][rows, :slots], wide_ref[kv, :slots])
                result = mixed[:, :HD] * inverse_of(mixed[:, HD:])
                if not lone:
                    result = jnp.where(live[rows], result, 0.0)
                out_ref[kv, rows, lanes] = result.astype(BF16)

            return [functools.partial(step, at) for at in range(0, tokens, tokens // 2)]

        last = kv_heads * Q_PER_KV - 1
        query_copy(0).wait()
        interleave(score_steps(jnp.int32(0), 0))
        interleave(score_steps(jnp.int32(1), 1), weight_steps(0))

        def kv_step(kv, carry):
            @pl.when(kv + 1 < kv_heads)
            def _():
                query_copy(kv + 1).wait()

            def two_heads(j, inner):
                for slot in range(2):
                    h = kv * Q_PER_KV + 2 * j + slot
                    interleave(
                        score_steps(jnp.minimum(h + 2, last), slot),
                        weight_steps(1 - slot),
                        value_steps(h, slot),
                    )
                return inner

            lax.fori_loop(0, Q_PER_KV // 2, two_heads, 0)
            out_copy(kv).start()
            return carry

        lax.fori_loop(0, kv_heads, kv_step, 0)
        for kv in range(kv_heads):
            out_copy(kv).wait()

    lone = needed < 0
    for k in range(MAX_IN_GROUP):
        lone = lone | (
            (first[k] <= row_first - (needed - 1) * tokens) & (end[k] >= row_first + tokens)
        )
    before = 0
    for count in sorted({c for c in (1, 2, 3, n) if c <= n}):
        here = (needed > before) & (needed <= count)
        exact = (needed == count) & lone
        before = count

        @pl.when(exact)
        def _():
            run(count, True)

        @pl.when(here & jnp.logical_not(exact))
        def _():
            run(count, False)


def call(body, scalars, args, outs, *, grid=None, in_specs=None, out_specs=None, scratch=(), cost, vmem=6, aliases=None):
    whole = pl.BlockSpec(memory_space=pltpu.VMEM)
    if grid is None:
        grid = (1,)
    flops, exps = cost
    moved = sum(a.size * a.dtype.itemsize for a in args) + sum(
        o.size * o.dtype.itemsize for o in outs
    )
    return pl.pallas_call(
        body,
        out_shape=list(outs),
        grid_spec=pltpu.PrefetchScalarGridSpec(
            num_scalar_prefetch=len(scalars),
            grid=grid,
            in_specs=in_specs or [whole] * len(args),
            out_specs=out_specs or [whole] * len(outs),
            scratch_shapes=list(scratch),
        ),
        compiler_params=pltpu.CompilerParams(
            dimension_semantics=("arbitrary",) * len(grid), vmem_limit_bytes=int(vmem * MIB)
        ),
        input_output_aliases=aliases or {},
        cost_estimate=pl.CostEstimate(flops=flops, bytes_accessed=moved, transcendentals=exps),
    )(*scalars, *args)


def shift(x, axis, count, t):
    return lax.ppermute(x, axis, [(i, (i + t) % count) for i in range(count)])


def shards(
    lengths,
    group_of,
    query_pre,
    key_pre,
    value_pre,
    query_new,
    key_new,
    value_new,
    hidden_new,
    out_weight,
    norm_gain,
    gate_weight,
    up_weight,
    down_weight,
):
    n = lax.axis_size("seq")
    count = lax.axis_size("grp")
    seq = lax.axis_index("seq").astype(jnp.int32)
    group = lax.axis_index("grp").astype(jnp.int32)
    tokens = query_pre.shape[0]
    reqs = query_new.shape[0]
    kv_heads = key_pre.shape[1] // HD
    shard_width = query_new.shape[1]
    shard_heads = shard_width // HD
    columns = out_weight.shape[1]
    shape = jax.ShapeDtypeStruct
    vmem = pl.BlockSpec(memory_space=pltpu.VMEM)
    anywhere = pl.BlockSpec(memory_space=pl.ANY)
    dma = pltpu.SemaphoreType.DMA
    facts = jnp.concatenate([jnp.stack([group, seq]), group_of, lengths])
    scalars = (facts,)

    def to_seq(x):
        return [x] + [shift(x, "seq", n, t) for t in range(1, n)]

    def to_grp(x):
        return lax.all_to_all(x, "grp", split_axis=0, concat_axis=0, tiled=True)

    def tie(x, after):
        return lax.optimization_barrier((x, after))[0]

    def up(x, step, after):
        return lax.ppermute(tie(x, after), "seq", [(i, i + 1) for i in range(step - 1, n - 1)])

    pieces = call(
        pack_kernel,
        (),
        (key_pre, value_pre),
        (shape((2 * kv_heads * HD, tokens), BF16),),
        cost=(key_pre.size, 0),
    )
    pieces = list(pieces)

    query, own = call(
        select_kernel,
        scalars,
        (jnp.concatenate([query_new, key_new, value_new], axis=1),),
        (shape((SLOTS_R, shard_width), BF16), shape((shard_heads * SLOTS_R, 2 * HD), F32)),
        cost=(2 * 8 * reqs * shard_width, 0),
    )
    queries = to_seq(query)
    rows = shard_heads * SLOTS_R
    partials = call(
        functools.partial(partial_kernel, n),
        scalars,
        (*queries, pieces[0]),
        [shape((rows, 2 * HD), BF16)] * n,
        scratch=(
            pltpu.VMEM((n, SLOTS_R, shard_width), F32),
            pltpu.VMEM((n, rows, 2 * HD), BF16),
        ),
        cost=(4 * n * rows * tokens * HD, n * rows * tokens),
    )
    partials = [partials[0]] + [shift(partials[t], "seq", n, n - t) for t in range(1, n)]
    pieces.append(up(pieces[-1], 1, partials[1:]))
    (att,) = call(
        functools.partial(combine_kernel, n, count),
        (),
        (*partials, own),
        (shape((count, SLOTS_R, shard_width), BF16),),
        cost=(8 * n * rows * HD, n * rows),
    )
    atts = to_grp(att)

    index = jnp.arange(reqs, dtype=jnp.int32)
    groups = tie(group_of, att)
    same = groups[None, :] == groups[:, None]
    rank = jnp.sum(jnp.where(same & (index[None, :] < index[:, None]), 1, 0), axis=1)
    place = groups * SLOTS_R + rank
    pick = (place[:, None] == jnp.arange(count * SLOTS_R, dtype=jnp.int32)[None, :]).astype(BF16)
    steps = 8
    depth = shard_width // steps
    (proj,) = call(
        functools.partial(project_kernel, count),
        (),
        (pick, atts, out_weight),
        (shape((reqs, columns), BF16),),
        in_specs=[vmem, vmem, anywhere],
        scratch=(
            pltpu.VMEM((steps, depth, columns), BF16),
            pltpu.VMEM((steps, reqs, depth), BF16),
            dma((steps,)),
        ),
        cost=(2 * reqs * shard_width * columns, 0),
        vmem=STREAM + 3,
    )
    projs = to_seq(proj)
    if n > 2:
        pieces.append(up(pieces[-1], 2, projs[1:]))

    hidden_shard = gate_weight.shape[1]
    width = hidden_shard // count
    resid, terms = call(
        functools.partial(gate_up_kernel, n, count),
        (),
        (*projs, hidden_new, norm_gain.reshape(1, -1), gate_weight, up_weight),
        [shape((reqs, columns), F32), shape((count, reqs, 2 * width + HD), BF16)],
        in_specs=[vmem] * (n + 2) + [anywhere] * 2,
        scratch=(
            pltpu.VMEM(gate_weight.shape, BF16),
            pltpu.VMEM(up_weight.shape, BF16),
            dma((2 * count,)),
        ),
        cost=(4 * reqs * columns * hidden_shard, 0),
        vmem=STREAM,
    )
    terms = to_grp(terms)
    (hidden,) = call(
        functools.partial(hidden_kernel, count, columns * count),
        (),
        (terms,),
        (shape((count, reqs, width), BF16),),
        cost=(8 * count * reqs * width, reqs * width),
    )
    if n > 3:
        pieces.append(up(pieces[-1], 3, hidden))
    hiddens = to_grp(hidden)
    share = columns // n
    downs = call(
        functools.partial(down_kernel, count, n),
        scalars,
        (hiddens, resid, down_weight),
        [shape((reqs, share), F32)] * n,
        in_specs=[vmem, vmem, anywhere],
        scratch=(pltpu.VMEM((count, width, columns), BF16), dma((count,))),
        cost=(2 * reqs * columns * hidden_shard, 0),
        vmem=STREAM,
    )
    arrived = [shift(downs[t], "seq", n, t) for t in range(1, n)]
    (decode_hidden,) = call(
        sum_kernel,
        (),
        (downs[0], *arrived),
        (shape((reqs, share), BF16),),
        cost=(n * reqs * share, 0),
    )
    for step in range(len(pieces), n):
        pieces.append(up(pieces[-1], step, pieces[-1]))

    first = jnp.sum(jnp.where(same & (index[None, :] < index[:, None]), lengths[None, :], 0), axis=1)
    row_first = seq * tokens
    meets = (group_of == group) & (first + lengths > row_first) & (first < row_first + tokens)
    lowest = jnp.min(jnp.where(meets, first, row_first + tokens))
    scalars = (jnp.concatenate([facts, (seq - lax.div(lowest, tokens) + 1)[None]]),)
    wide = Q_PER_KV * HD
    (prefill,) = call(
        functools.partial(prefill_kernel, n),
        scalars,
        (query_pre, *pieces),
        (shape(query_pre.shape, BF16),),
        in_specs=[anywhere] * (1 + n),
        out_specs=[anywhere],
        scratch=[
            pltpu.VMEM((kv_heads, tokens, wide), BF16),
            pltpu.VMEM((n, kv_heads * HD, tokens), BF16),
            pltpu.VMEM((n, kv_heads * HD, tokens), BF16),
            pltpu.VMEM((kv_heads, n * tokens, 2 * HD), BF16),
            pltpu.VMEM((tokens, n * tokens), F32),
            pltpu.VMEM((kv_heads, tokens, wide), BF16),
        ]
        + [pltpu.VMEM((tokens, n * tokens), F32)] * 2
        + [pltpu.VMEM((tokens, n * tokens), BF16)] * 2
        + [dma((kv_heads,)), dma((2, n)), dma((kv_heads,))],
        cost=(8 * n * tokens * query_pre.size, n * tokens * query_pre.size // HD),
        vmem=48,
    )
    return (prefill, decode_hidden)


def solution(mesh):
    return jax.shard_map(
        shards,
        mesh=mesh,
        in_specs=(
            P(),
            P(),
            P(("grp", "seq"), None),
            P(("grp", "seq"), None),
            P(("grp", "seq"), None),
            P(None, "seq"),
            P(None, "seq"),
            P(None, "seq"),
            P(None, "grp"),
            P("seq", "grp"),
            P("grp"),
            P("grp", "seq"),
            P("grp", "seq"),
            P("seq", "grp"),
        ),
        out_specs=(P(("grp", "seq"), None), P(None, ("grp", "seq"))),
        check_vma=False,
    )
```
